32 devices in a mesh: dp: 4 (over y, x), tensor: 8 (over z, core).
Axes of the slice: x: 2, y: 2, z: 4, core: 2. Of those that a mesh axis runs over, the one named last changes fastest.
Arguments:
- tokens: bfloat16 [4096, 1280], P(('dp', 'tensor'))
- cotangent: bfloat16 [4096, 1280], P(('dp', 'tensor')), may hold values from -6 to 6
- gate_weights: float32 [4096, 2], P(('dp', 'tensor')), may hold values from 0.2 to 1
- routes: int32 [4096, 2], P(('dp', 'tensor')), may hold values from 0 to 7, as said below
- slot_index: int32 [4096, 2], P(('dp', 'tensor')), may hold values from -1 to 1, as said below
- qkv_weight: bfloat16 [1280, 16, 240], P(None, 'tensor'), may hold values from -0.15625 to 0.15625
- proj_weight: bfloat16 [16, 80, 1280], P('tensor'), may hold values from -1.25 to 1.25
- up_weight: bfloat16 [8, 1280, 5120], P('dp', None, 'tensor'), may hold values from -0.15625 to 0.15625
- down_weight: bfloat16 [8, 5120, 1280], P('dp', 'tensor'), may hold values from -0.078125 to 0.078125
Outputs:
- layer_out: bfloat16 [4096, 1280], P(('dp', 'tensor'))
- gate_grad: float32 [4096, 2], P(('dp', 'tensor'))
- grad_qkv: float32 [1280, 16, 240], P('dp', 'tensor')
- grad_proj: float32 [16, 80, 1280], P('tensor', None, 'dp')
- grad_up: bfloat16 [8, 1280, 5120], P('dp', None, 'tensor')
- grad_down: bfloat16 [8, 5120, 1280], P('dp', 'tensor')
The draws below stay inside these ranges and needn't reach their ends.
Inputs may be any that keep to these rules, and one draw needn't show every extreme that they name: `routes`: the two experts of a row differ. `slot_index`: -1 marks a dropped pair; within the rows of one device (aligned blocks of 128 rows) and one expert, the kept pairs hold the slots 0, 1, 2, ... without gaps, each at most once.
All inputs are finite; a program needn't handle non-finite values.
Results may differ from the reference program's by a relative error of at most 0.035.
Values may be sent and summed in bfloat16 or wider, within the bound.
No kernel may reach another device: no remote copies, remote signals or barrier semaphores. Data moves between devices by JAX's collectives and lax.ppermute only.
A program may use at most 128 MiB of HBM per device.

```python
import math
import jax
import jax.numpy as jnp
from jax import lax

D = 1280
HEADS = 16
HD = 80
FF = 5120
CAP = 2
ROWS_DEV = 128
EXPERTS = 8
SEQ = 1024
TOKENS = 4096
HEADS_DEV = 2
FF_DEV = 640
N_DP = 4
N_TENSOR = 8


def route_table(key):
    base_key = jax.random.fold_in(key, 71)
    key_relabel, key_pick, key_offset, key_order = jax.random.split(base_key, 4)
    relabel = jax.random.permutation(key_relabel, EXPERTS).astype(jnp.int32)
    first_pick = jax.random.randint(key_pick, (TOKENS,), 0, 2 * EXPERTS, dtype=jnp.int32)
    hot_count = max(EXPERTS // 4, 1)
    first_expert = jnp.where(first_pick < EXPERTS, first_pick, first_pick % hot_count)
    offset = jax.random.randint(key_offset, (TOKENS,), 1, EXPERTS, dtype=jnp.int32)
    second_expert = (first_expert + offset) % EXPERTS
    routes = jnp.take(relabel, jnp.stack([first_expert, second_expert], axis=1))
    block_total = TOKENS // ROWS_DEV

    def order_rows(block_key):
        return jax.random.permutation(block_key, ROWS_DEV).astype(jnp.int32)
    orders = jax.vmap(order_rows)(jax.random.split(key_order, block_total))
    priority = jnp.stack([orders, orders + ROWS_DEV], axis=2).reshape(block_total, ROWS_DEV * 2)
    block_routes = routes.reshape(block_total, ROWS_DEV * 2)

    def rank_block(pieces):
        chosen, order_rank = pieces
        same_expert = chosen[:, None] == chosen[None, :]
        earlier = order_rank[None, :] < order_rank[:, None]
        return jnp.sum((same_expert & earlier).astype(jnp.int32), axis=1)
    rank_counts = lax.map(rank_block, (block_routes, priority))
    slot_values = jnp.where(rank_counts < CAP, rank_counts, -1).reshape(TOKENS, 2)
    return (routes.astype(jnp.int32), slot_values.astype(jnp.int32))


def draw_routes(key, part):
    return route_table(key)[0]


def draw_slot_index(key, part):
    return route_table(key)[1]


def draw_tokens(key, part):
    base_key = jax.random.fold_in(key, 29)
    key_rows, key_cols, key_main = jax.random.split(base_key, 3)
    low_end = math.log(0.3)
    high_end = math.log(3.0)
    row_scale = jnp.exp(jax.random.uniform(key_rows, (TOKENS, 1), jnp.float32, low_end, high_end))
    col_scale = jnp.exp(jax.random.uniform(key_cols, (1, D), jnp.float32, low_end, high_end))
    main_part = jax.random.normal(key_main, (TOKENS, D), jnp.float32)
    return (main_part * row_scale * col_scale).astype(jnp.bfloat16)


def block_levels(own_key, extent, shards, smallest, largest):
    factor_of = 1.0
    for axis_at, blocks in shards:
        steps = jax.random.uniform(jax.random.fold_in(jax.random.fold_in(own_key, 6), axis_at), (blocks,), jnp.float32, smallest / len(shards), largest / len(shards))
        factor_of = factor_of * jnp.repeat(jnp.exp(steps), extent[axis_at] // blocks).reshape((-1,) + (1,) * (len(extent) - 1 - axis_at))
    return factor_of


def scatter_about(stream_key, shape, spread, limit, shards=(), kind=jnp.bfloat16):
    result = spread * jax.random.normal(stream_key, shape, jnp.float32)
    if shards:
        result = result * block_levels(stream_key, shape, shards, -0.22, 0.18)
    return jnp.clip(result, -limit, limit).astype(kind)


def setup_inputs(seed: int = 0) -> dict:
    keys = jax.random.split(jax.random.key(seed), 10)
    return {
        "tokens": draw_tokens(jax.random.fold_in(keys[9], 71), 0),
        "cotangent": scatter_about(keys[1], (TOKENS, D), 1.0, 6.0, ((0, 32),)),
        "gate_weights": jnp.clip(jnp.exp(math.log(1.0) - 1.609438 * jax.random.uniform(keys[2], (TOKENS, 2), jnp.float32) ** block_levels(keys[2], (TOKENS, 2), ((0, 32),), -0.2, 0.2)), 0.2, 1.0),
        "routes": draw_routes(jax.random.fold_in(keys[9], 71), 0),
        "slot_index": draw_slot_index(jax.random.fold_in(keys[9], 71), 0),
        "qkv_weight": scatter_about(keys[5], (D, HEADS, 3 * HD), D ** -0.5, 0.15625, ((1, 8),)),
        "proj_weight": scatter_about(keys[6], (HEADS, HD, D), (HEADS * HD // 64) ** -0.5, 1.25, ((0, 8),)),
        "up_weight": scatter_about(keys[7], (EXPERTS, D, FF), D ** -0.5, 0.15625, ((0, 4), (2, 8))),
        "down_weight": scatter_about(keys[8], (EXPERTS, FF, D), FF ** -0.5, 0.078125, ((0, 4), (1, 8))),
    }


epsilon = 1e-06
half_root = 1.0 / math.sqrt(2.0)
bell_scale = 1.0 / math.sqrt(2.0 * math.pi)

def norm_parts(row_block):
    widened = row_block.astype(jnp.float32)
    center = widened - lax.optimization_barrier(jnp.mean(widened, axis=-1, keepdims=True))
    factor = lax.rsqrt(lax.optimization_barrier(jnp.mean(center * center, axis=-1, keepdims=True)) + epsilon)
    return (center * factor, factor)

def norm_back(normal_rows, factor, upstream):
    mean_up = lax.optimization_barrier(jnp.mean(upstream, axis=-1, keepdims=True))
    mean_mix = lax.optimization_barrier(jnp.mean(upstream * normal_rows, axis=-1, keepdims=True))
    return factor * (upstream - mean_up - normal_rows * mean_mix)

def gelu_value(pre_act):
    return 0.5 * pre_act * (1.0 + lax.erf(pre_act * half_root))

def gelu_slope(pre_act):
    return 0.5 * (1.0 + lax.erf(pre_act * half_root)) + pre_act * jnp.exp(-0.5 * pre_act * pre_act) * bell_scale

def round_low(values):
    return lax.optimization_barrier(values.astype(jnp.bfloat16)).astype(jnp.float32)

def split_parts(widened):
    shaped = widened.reshape(SEQ, HEADS, 3 * HD)
    return (shaped[:, :, :HD], shaped[:, :, HD:2 * HD], shaped[:, :, 2 * HD:])

def chart_shares(queries, key_rows):
    scores = jnp.einsum('shk,thk->hst', queries, key_rows) * HD ** (-0.5)
    raised = jnp.exp(scores)
    return raised / lax.optimization_barrier(jnp.sum(raised, axis=-1, keepdims=True))

def reference(tokens, cotangent, gate_weights, routes, slot_index, qkv_weight, proj_weight, up_weight, down_weight):
    score_scale = HD ** (-0.5)
    block_total = N_DP * N_TENSOR
    places = EXPERTS * CAP
    slot_rows = block_total * CAP
    normal_in, factor_in = norm_parts(tokens)
    normed = normal_in.astype(jnp.bfloat16)
    flat_qkv = qkv_weight.reshape(D, HEADS * 3 * HD)
    proj_groups = proj_weight.reshape(N_TENSOR, HEADS_DEV, HD, D).astype(jnp.float32)

    def chart_forward(chart_norm):
        raw_qkv = jnp.dot(chart_norm, flat_qkv, preferred_element_type=jnp.float32)
        queries, key_rows, value_rows = split_parts(round_low(raw_qkv))
        shares = chart_shares(queries, key_rows)
        context = jnp.einsum('hst,thk->hsk', round_low(shares), value_rows)
        partial_value = jnp.einsum('ghsk,ghkd->gsd', round_low(context).reshape(N_TENSOR, HEADS_DEV, SEQ, HD), proj_groups)
        attention = lax.optimization_barrier(jnp.sum(round_low(partial_value), axis=0))
        return (raw_qkv.astype(jnp.bfloat16), context.astype(jnp.bfloat16), attention)
    qkv_all, context_all, attention_all = lax.map(chart_forward, normed.reshape(N_DP, SEQ, D))
    mid = (tokens.astype(jnp.float32) + attention_all.reshape(TOKENS, D)).astype(jnp.bfloat16)
    normal_mid, factor_mid = norm_parts(mid)
    mid_normed = normal_mid.astype(jnp.bfloat16)
    row_owner = (jnp.arange(TOKENS, dtype=jnp.int32) // ROWS_DEV)[:, None]
    target = jnp.where(slot_index >= 0, row_owner * places + routes * CAP + slot_index, block_total * places)
    target = target.reshape(TOKENS * 2).astype(jnp.int32)

    def scatter_slots(pair_rows):
        filled = jnp.zeros((block_total * places + 1, D), pair_rows.dtype).at[target].set(pair_rows.reshape(TOKENS * 2, D))
        shaped = filled[:-1].reshape(block_total, EXPERTS, CAP, D)
        return shaped.transpose(1, 0, 2, 3).reshape(EXPERTS, slot_rows, D)

    def gather_slots(per_expert):
        flat = per_expert.reshape(EXPERTS, block_total, CAP, D).transpose(1, 0, 2, 3).reshape(block_total * places, D)
        flat = jnp.concatenate([flat, jnp.zeros((1, D), flat.dtype)], axis=0)
        return flat[target].reshape(TOKENS, 2, D)
    slot_in = scatter_slots(jnp.broadcast_to(mid_normed[:, None, :], (TOKENS, 2, D)))

    def expert_forward(pieces):
        inputs, up_mat, down_mat = pieces
        pre_act = jnp.dot(inputs, up_mat, preferred_element_type=jnp.float32)
        hidden = round_low(gelu_value(pre_act))
        partial_value = jnp.einsum('mgf,gfd->mgd', hidden.reshape(slot_rows, N_TENSOR, FF_DEV), down_mat.astype(jnp.float32).reshape(N_TENSOR, FF_DEV, D))
        return lax.optimization_barrier(jnp.sum(round_low(partial_value), axis=1)).astype(jnp.bfloat16)
    expert_out = lax.map(expert_forward, (slot_in, up_weight, down_weight))
    picked = gather_slots(expert_out).astype(jnp.float32)
    mixed_rows = gate_weights[:, 0:1] * picked[:, 0] + gate_weights[:, 1:2] * picked[:, 1]
    layer_out = (mid.astype(jnp.float32) + mixed_rows).astype(jnp.bfloat16)
    upstream = cotangent.astype(jnp.float32)
    gate_grad = lax.optimization_barrier(jnp.sum(upstream[:, None, :] * picked, axis=-1))
    grad_pairs = (gate_weights[:, :, None] * upstream[:, None, :]).astype(jnp.bfloat16)
    grad_slot = scatter_slots(grad_pairs)

    def expert_backward(pieces):
        inputs, grads, up_mat, down_mat = pieces
        pre_act = jnp.dot(inputs, up_mat, preferred_element_type=jnp.float32)
        hidden = gelu_value(pre_act).astype(jnp.bfloat16)
        grad_hidden = jnp.dot(grads, down_mat.T, preferred_element_type=jnp.float32)
        grad_pre_wide = grad_hidden * gelu_slope(pre_act)
        grad_pre = grad_pre_wide.astype(jnp.bfloat16)
        grad_down = jnp.dot(hidden.T, grads, preferred_element_type=jnp.float32).astype(jnp.bfloat16)
        grad_up = jnp.dot(inputs.T, grad_pre, preferred_element_type=jnp.float32).astype(jnp.bfloat16)
        partial_value = jnp.einsum('mgf,dgf->mgd', round_low(grad_pre_wide).reshape(slot_rows, N_TENSOR, FF_DEV), up_mat.astype(jnp.float32).reshape(D, N_TENSOR, FF_DEV))
        grad_in = lax.optimization_barrier(jnp.sum(round_low(partial_value), axis=1)).astype(jnp.bfloat16)
        return (grad_in, grad_up, grad_down)
    grad_in, grad_up, grad_down = lax.map(expert_backward, (slot_in, grad_slot, up_weight, down_weight))
    back_pairs = gather_slots(grad_in).astype(jnp.float32)
    grad_norm = back_pairs[:, 0] + back_pairs[:, 1]
    grad_mid = (upstream + norm_back(normal_mid, factor_mid, grad_norm)).astype(jnp.bfloat16)

    def chart_backward(pieces):
        chart_norm, chart_qkv, context, chart_grad = pieces
        queries, key_rows, value_rows = split_parts(chart_qkv.astype(jnp.float32))
        shares = chart_shares(queries, key_rows)
        grad_wide = chart_grad.astype(jnp.float32)
        grad_context = round_low(jnp.einsum('sd,hkd->hsk', grad_wide, proj_weight.astype(jnp.float32)))
        grad_proj = jnp.einsum('hsk,sd->hkd', context.astype(jnp.float32), grad_wide)
        grad_shares = jnp.einsum('hsk,thk->hst', grad_context, value_rows)
        grad_scores = round_low(shares * (grad_shares - lax.optimization_barrier(jnp.sum(shares * grad_shares, axis=-1, keepdims=True))) * score_scale)
        grad_query = jnp.einsum('hst,thk->shk', grad_scores, key_rows).astype(jnp.bfloat16)
        grad_key = jnp.einsum('hst,shk->thk', grad_scores, queries).astype(jnp.bfloat16)
        grad_value = jnp.einsum('hst,hsk->thk', round_low(shares), grad_context).astype(jnp.bfloat16)
        grad_rows = jnp.concatenate([grad_query, grad_key, grad_value], axis=-1).reshape(SEQ, HEADS * 3 * HD)
        grad_qkv = jnp.dot(chart_norm.T, grad_rows, preferred_element_type=jnp.float32)
        return (grad_qkv, grad_proj)
    per_qkv, per_proj = lax.map(chart_backward, (normed.reshape(N_DP, SEQ, D), qkv_all, context_all, grad_mid.reshape(N_DP, SEQ, D)))
    grad_qkv = lax.optimization_barrier(jnp.sum(per_qkv, axis=0)).reshape(D, HEADS, 3 * HD)
    grad_proj = lax.optimization_barrier(jnp.sum(per_proj, axis=0))
    return (layer_out, gate_grad, grad_qkv, grad_proj, grad_up, grad_down)
```

```python
import math

import jax
import jax.numpy as jnp
from jax import lax
from jax.experimental import pallas as pl
from jax.experimental.pallas import tpu as pltpu
from jax.sharding import PartitionSpec as P

CAP = 2
LANES = 128
epsilon = 1e-06
half_root = 1.0 / math.sqrt(2.0)
bell_scale = 1.0 / math.sqrt(2.0 * math.pi)
f32 = jnp.float32
bf16 = jnp.bfloat16


def norm_parts(row_block):
    widened = row_block.astype(f32)
    center = widened - jnp.mean(widened, axis=-1, keepdims=True)
    factor = lax.rsqrt(jnp.mean(center * center, axis=-1, keepdims=True) + epsilon)
    return (center * factor, factor)


def norm_back(normal_rows, factor, upstream):
    mean_up = jnp.mean(upstream, axis=-1, keepdims=True)
    mean_mix = jnp.mean(upstream * normal_rows, axis=-1, keepdims=True)
    return factor * (upstream - mean_up - normal_rows * mean_mix)


def dot(a, b):
    return lax.dot_general(a, b, (((1,), (0,)), ((), ())), preferred_element_type=f32)


def dot_nt(a, b):
    return lax.dot_general(a, b, (((1,), (1,)), ((), ())), preferred_element_type=f32)


def dot_tn(a, b):
    return lax.dot_general(a, b, (((0,), (0,)), ((), ())), preferred_element_type=f32)


def run(body, outs, ins, name, flops=0, mib=48, smem=()):
    specs = [
        pl.BlockSpec(memory_space=pltpu.SMEM if i in smem else pltpu.VMEM) for i in range(len(ins))
    ]
    sizes = [math.prod(x.shape) * x.dtype.itemsize for x in list(ins) + list(outs)]
    return pl.pallas_call(
        body,
        out_shape=list(outs),
        in_specs=specs,
        out_specs=[pl.BlockSpec(memory_space=pltpu.VMEM)] * len(outs),
        compiler_params=pltpu.CompilerParams(vmem_limit_bytes=mib * 2**20),
        cost_estimate=pl.CostEstimate(
            flops=int(flops), bytes_accessed=int(sum(sizes)), transcendentals=0
        ),
        name=name,
    )(*ins)


def shape(dims, dtype=bf16):
    return jax.ShapeDtypeStruct(tuple(dims), dtype)


def block_of(rows, most=256):
    return max(b for b in range(16, most + 1, 16) if rows % b == 0)


def hop(x, axis, mask):
    size = lax.axis_size(axis)
    return lax.ppermute(x, axis, [(i, i ^ mask) for i in range(size)])


def gather_rel(x):
    size = lax.axis_size("tensor")
    even = [x] + [hop(x, "tensor", m) for m in range(2, size, 2)]
    odd = [hop(e, "tensor", 1) for e in even]
    return [y for pair in zip(even, odd) for y in pair]


def prologue_body(group, tok, cot, gate, routes, slots, *outs):
    normed_o, cot_o, tok_o, perm_o, pick0_o, pick1_o, link_o, gout_o = outs
    rows = tok.shape[0]
    places = pick0_o.shape[1]
    code = jnp.where(slots[...] >= 0, (routes[...] ^ group[0]) * CAP + slots[...], -1)
    lane = lax.broadcasted_iota(jnp.int32, (rows, LANES), 1)
    wide0 = (code[:, 0:1] == lane).astype(f32)
    wide1 = (code[:, 1:2] == lane).astype(f32)
    kept0 = (code[:, 0:1] >= 0).astype(f32)
    prim = wide0 + wide1 * (1.0 - kept0)
    plain = 1.0 - jnp.sum(prim, axis=1, keepdims=True)
    open_at = 1.0 - jnp.sum(prim, axis=0, keepdims=True)
    ri = lax.broadcasted_iota(jnp.int32, (rows, rows), 0)
    ci = lax.broadcasted_iota(jnp.int32, (rows, rows), 1)
    row_rank = dot(
        (ci < ri).astype(bf16), jnp.broadcast_to(plain, (rows, rows)).astype(bf16)
    )
    place_rank = dot(
        jnp.broadcast_to(open_at, (rows, rows)).astype(bf16), (ri < ci).astype(bf16)
    )
    filler = plain * open_at * (row_rank == place_rank).astype(f32)
    perm = (prim + filler).astype(bf16)
    perm_o[...] = perm
    normal, _ = norm_parts(tok[...])
    normed_o[...] = dot_tn(perm, normal.astype(bf16)).astype(bf16)
    cot_o[...] = dot_tn(perm, cot[...]).astype(bf16)
    tok_o[...] = dot_tn(perm, tok[...]).astype(bf16)
    pick0 = wide0.astype(bf16)
    pick1 = wide1.astype(bf16)
    pick0_o[...] = pick0[:, :places]
    pick1_o[...] = pick1[:, :places]
    link_o[...] = dot_tn((pick0 + pick1), prim.astype(bf16))[:places, :places].astype(bf16)
    upstream = cot[...].astype(f32)
    g0 = (gate[:, 0:1] * upstream).astype(bf16)
    g1 = (gate[:, 1:2] * upstream).astype(bf16)
    gout_o[...] = (dot_tn(pick0, g0) + dot_tn(pick1, g1))[:places].astype(bf16)


def probs_of(queries, keys, scale):
    raised = jnp.exp(dot_nt(queries, keys) * scale)
    return raised * (1.0 / jnp.sum(raised, axis=-1, keepdims=True))


def part_of(ref, rows, which, head):
    at = (3 * head + which) * LANES
    return ref[rows, at : at + LANES]


def make_front(count, places, heads, scale):
    def body(*refs):
        shards, (wqkv, proj) = refs[:count], refs[count : count + 2]
        fn, qkv, ctx, part = refs[count + 2 :]
        rows = shards[0].shape[0]
        cold = rows - places
        hot_all = count * places
        for k in range(count):
            fn[k * places : (k + 1) * places] = shards[k][:places]
            if cold:
                fn[hot_all + k * cold : hot_all + (k + 1) * cold] = shards[k][places:]
        total = fn.shape[0]
        step = block_of(total)

        def chunk(i, _):
            at = pl.ds(pl.multiple_of(i * step, 16), step)
            qkv[at, :] = dot(fn[at, :], wqkv[...]).astype(bf16)
            return 0

        lax.fori_loop(0, total // step, chunk, 0)
        every = slice(None)
        hot = slice(0, hot_all)
        for h in range(heads):
            shares = probs_of(part_of(qkv, hot, 0, h), part_of(qkv, every, 1, h), scale)
            ctx[:, h * LANES : (h + 1) * LANES] = dot(
                shares.astype(bf16), part_of(qkv, every, 2, h)
            ).astype(bf16)
        part[...] = dot(ctx[...], proj[...]).astype(bf16)

    return body


def make_cold(hot_all, heads, scale):
    def body(qkv, proj, ctx, part):
        total = ctx.shape[0]
        step = block_of(total)
        every = slice(None)

        def chunk(i, _):
            at = pl.ds(pl.multiple_of(i * step, 16), step)
            src = pl.ds(pl.multiple_of(hot_all + i * step, 16), step)
            for h in range(heads):
                shares = probs_of(part_of(qkv, src, 0, h), part_of(qkv, every, 1, h), scale)
                ctx[at, h * LANES : (h + 1) * LANES] = dot(
                    shares.astype(bf16), part_of(qkv, every, 2, h)
                ).astype(bf16)
            part[at, :] = dot(ctx[at, :], proj[...]).astype(bf16)
            return 0

        lax.fori_loop(0, total // step, chunk, 0)

    return body


def back_block(qkv, src, grad_ctx, head, scale):
    every = slice(None)
    queries = part_of(qkv, src, 0, head)
    keys = part_of(qkv, every, 1, head)
    shares = probs_of(queries, keys, scale)
    grad_shares = dot_nt(grad_ctx, part_of(qkv, every, 2, head))
    mix = jnp.sum(shares * grad_shares, axis=-1, keepdims=True)
    grad_scores = (shares * (grad_shares - mix) * scale).astype(bf16)
    return (
        dot(grad_scores, keys),
        dot_tn(queries, grad_scores),
        dot_tn(grad_ctx, shares.astype(bf16)),
    )


def make_cold_back(count, places, heads, scale):
    def body(*refs):
        shards, (qkv, proj, ctx) = refs[:count], refs[count : count + 3]
        gq, gk, gv, gp, cots = refs[count + 3 :]
        cold = shards[0].shape[0]
        hot_all = count * places
        for k in range(count):
            cots[k * cold : (k + 1) * cold] = shards[k][...]
        total = cots.shape[0]
        step = block_of(total)
        gk[...] = jnp.zeros_like(gk)
        gv[...] = jnp.zeros_like(gv)
        gp[...] = jnp.zeros_like(gp)

        def chunk(i, _):
            at = pl.ds(pl.multiple_of(i * step, 16), step)
            src = pl.ds(pl.multiple_of(hot_all + i * step, 16), step)
            grad_ctx = dot_nt(cots[at, :], proj[...]).astype(bf16)
            gp[...] += dot_tn(ctx[at, :], cots[at, :])
            for h in range(heads):
                cut = slice(h * LANES, (h + 1) * LANES)
                a, b, c = back_block(qkv, src, grad_ctx[:, cut], h, scale)
                gq[at, cut] = a.astype(bf16)
                gk[cut, :] += b
                gv[cut, :] += c
            return 0

        lax.fori_loop(0, total // step, chunk, 0)

    return body


def make_hot_back(count, heads, size, groups, scale):
    def body(*refs):
        shards = refs[:count]
        qkv, proj, ctx, gq, gk, gv, gp, fn, out, rows_t = refs[count:]
        grads = jnp.concatenate([s[...] for s in shards], axis=0)
        hot_all = grads.shape[0]
        grad_ctx = dot_nt(grads, proj[...]).astype(bf16)
        proj_grad = gp[...] + dot_tn(ctx[...], grads)
        width = fn.shape[1] // groups
        base = heads * 3 * size
        for h in range(heads):
            cut = slice(h * LANES, (h + 1) * LANES)
            a, b, c = back_block(qkv, slice(0, hot_all), grad_ctx[:, cut], h, scale)
            at = h * 3 * size
            rows_t[at : at + size, :hot_all] = a.T[:size].astype(bf16)
            rows_t[at : at + size, hot_all:] = gq[:, cut].T[:size]
            rows_t[at + size : at + 2 * size, :] = (gk[cut, :] + b)[:size].astype(bf16)
            rows_t[at + 2 * size : at + 3 * size, :] = (gv[cut, :] + c)[:size].astype(bf16)
            for g in range(groups):
                out[g, base + h * size : base + (h + 1) * size, :] = proj_grad[
                    h * LANES : h * LANES + size, g * width : (g + 1) * width
                ].astype(bf16)
        for h in range(heads):
            part = slice(h * 3 * size, (h + 1) * 3 * size)
            whole = dot(rows_t[part, :], fn[...])
            for g in range(groups):
                out[g, part, :] = whole[:, g * width : (g + 1) * width].astype(bf16)

    return body


def make_fold(count):
    def body(mine, theirs, *outs):
        rows = outs[0].shape[0]
        for i in range(count):
            at = slice(i * rows, (i + 1) * rows)
            outs[i][...] = (mine[at].astype(f32) + theirs[at].astype(f32)).astype(bf16)

    return body


def total_of(refs):
    total = refs[0][...].astype(f32)
    for r in refs[1:]:
        total = total + r[...].astype(f32)
    return total


def make_mid(count, groups):
    def body(*refs):
        parts, (tok, link) = refs[:count], refs[count : count + 2]
        mid_o, normal_o, factor_o = refs[count + 2 : count + 5]
        outs = refs[count + 5 :]
        mid = (tok[...].astype(f32) + total_of(parts)).astype(bf16)
        normal, factor = norm_parts(mid)
        mid_o[...] = mid
        normal_o[...] = normal
        factor_o[...] = factor
        slot_in = dot(link[...], normal.astype(bf16))
        each = slot_in.shape[0] // groups
        for g in range(groups):
            outs[g][...] = slot_in[g * each : (g + 1) * each].astype(bf16)

    return body


def slot_mask(rows, experts, e):
    row = lax.broadcasted_iota(jnp.int32, (rows, 1), 0)
    return (row // CAP) % experts == e


def make_expert_grad(count, experts):
    def body(*refs):
        shards, down, grads, out = refs[:count], refs[count], refs[count + 1], refs[count + 2]
        grads[...] = jnp.concatenate([s[...] for s in shards], axis=0)
        for e in range(experts):
            out[e] = dot_nt(grads[...], down[e])

    return body


def make_expert(count, experts):
    def body(*refs):
        shards = refs[:count]
        up, down, grad_hidden, arrived, hid_o, pre_o, even, odd = refs[count:]
        arrived[...] = jnp.concatenate([s[...] for s in shards], axis=0)
        rows = arrived.shape[0]
        forth = None
        back = None
        for e in range(experts):
            keep = slot_mask(rows, experts, e)
            pre = dot(arrived[...], up[e])
            cdf = 0.5 * (1.0 + lax.erf(pre * half_root))
            hidden = jnp.where(keep, pre * cdf, 0.0).astype(bf16)
            slope = cdf + pre * jnp.exp(-0.5 * pre * pre) * bell_scale
            grad_pre = jnp.where(keep, grad_hidden[e] * slope, 0.0).astype(bf16)
            hid_o[e] = hidden
            pre_o[e] = grad_pre
            a = dot(hidden, down[e])
            b = dot_nt(grad_pre, up[e])
            forth = a if forth is None else forth + a
            back = b if back is None else back + b
        both = jnp.concatenate([back, forth], axis=1).astype(bf16)
        each = rows // count
        for k in range(count):
            to = even if k % 2 == 0 else odd
            to[(k // 2) * each : (k // 2 + 1) * each] = both[k * each : (k + 1) * each]

    return body


def make_weight_grads(experts):
    def body(arrived, grads, hidden, grad_pre, up_o, down_o):
        for e in range(experts):
            up_o[e] = dot_tn(arrived[...], grad_pre[e]).astype(bf16)
            down_o[e] = dot_tn(hidden[e], grads[...]).astype(bf16)

    return body


def make_split(count, groups):
    def body(*refs):
        parts, outs = refs[:count], refs[count:]
        total = total_of(parts)
        each = total.shape[0] // groups
        for g in range(groups):
            outs[g][...] = total[g * each : (g + 1) * each].astype(bf16)

    return body


def make_mid_back(groups):
    def body(*refs):
        parts = refs[:groups]
        link, cot, normal, factor, grad_o, expert_o = refs[groups:]
        both = jnp.concatenate([p[...].astype(f32) for p in parts], axis=0).astype(bf16)
        width = cot.shape[1]
        expert_o[...] = both[:, width:]
        grad_norm = dot_tn(link[...], both[:, :width])
        grad_o[...] = (
            cot[...].astype(f32) + norm_back(normal[...], factor[...], grad_norm)
        ).astype(bf16)

    return body


def make_epilogue(count):
    def body(*refs):
        parts = refs[:count]
        tok, mid_hot, perm, pick0, pick1, experts, gate, cot, out, gate_o = refs[count:]
        cold = (tok[...].astype(f32) + total_of(parts)).astype(bf16)
        ordered = jnp.concatenate([mid_hot[...], cold], axis=0)
        mid = dot(perm[...], ordered)
        first = dot(pick0[...], experts[...])
        second = dot(pick1[...], experts[...])
        out[...] = (mid + gate[:, 0:1] * first + gate[:, 1:2] * second).astype(bf16)
        upstream = cot[...].astype(f32)
        gate_o[:, 0:1] = jnp.sum(upstream * first, axis=-1, keepdims=True)
        gate_o[:, 1:2] = jnp.sum(upstream * second, axis=-1, keepdims=True)

    return body


def fold_scatter(even, odd, rows, name):
    count = lax.axis_size("tensor") // 2
    theirs = hop(odd, "tensor", 1)
    sums = run(
        make_fold(count), [shape((rows, even.shape[1]))] * count, [even, theirs], name, mib=24
    )
    return [sums[0]] + [hop(sums[i], "tensor", 2 * i) for i in range(1, count)]


def shards(
    tokens,
    cotangent,
    gate_weights,
    routes,
    slot_index,
    qkv_weight,
    proj_weight,
    up_weight,
    down_weight,
):
    rows, width = tokens.shape
    heads, size = qkv_weight.shape[1], qkv_weight.shape[2] // 3
    scale = size ** (-0.5)
    groups = lax.axis_size("dp")
    count = lax.axis_size("tensor")
    experts, _, hidden_dev = up_weight.shape
    each = experts * CAP
    places = groups * each
    cold = rows - places
    hot_all = count * places
    total = count * rows
    slots = count * places

    wqkv = jnp.pad(
        qkv_weight.reshape(width, heads, 3, size), ((0, 0), (0, 0), (0, 0), (0, LANES - size))
    ).reshape(width, heads * 3 * LANES)
    proj = jnp.pad(proj_weight, ((0, 0), (0, LANES - size), (0, 0))).reshape(heads * LANES, width)

    group = (lax.axis_index("dp") * experts).astype(jnp.int32).reshape(1)
    normed, cot, tok, perm, pick0, pick1, link, grad_out = run(
        prologue_body,
        [
            shape((rows, width)),
            shape((rows, width)),
            shape((rows, width)),
            shape((rows, rows)),
            shape((rows, places)),
            shape((rows, places)),
            shape((places, places)),
            shape((places, width)),
        ],
        [group, tokens, cotangent, gate_weights, routes, slot_index],
        "prologue",
        smem=(0,),
        mib=24,
    )
    normed_all = gather_rel(normed)
    fn, qkv, ctx_hot, part_hot = run(
        make_front(count, places, heads, scale),
        [
            shape((total, width)),
            shape((total, heads * 3 * LANES)),
            shape((hot_all, heads * LANES)),
            shape((hot_all, width)),
        ],
        normed_all + [wqkv, proj],
        "front",
        flops=2 * total * width * heads * 3 * LANES,
    )

    def parity(x, n):
        blocks = x.reshape(count // 2, 2, n, x.shape[1])
        return (
            blocks[:, 0].reshape(count // 2 * n, x.shape[1]),
            blocks[:, 1].reshape(count // 2 * n, x.shape[1]),
        )

    even, odd = parity(part_hot, places)
    hot_sums = fold_scatter(even, odd, places, "fold_hot")

    pieces = [grad_out[g * each : (g + 1) * each] for g in range(groups)]
    landed = jnp.concatenate(
        [pieces[0]] + [hop(pieces[g], "dp", g) for g in range(1, groups)], axis=0
    )
    grads_all = gather_rel(landed)
    slot_grads, grad_hidden = run(
        make_expert_grad(count, experts),
        [shape((slots, width)), shape((experts, slots, hidden_dev), f32)],
        grads_all + [down_weight],
        "slot_grads",
        flops=2 * slots * width * hidden_dev * experts,
        mib=24,
    )

    outs = run(
        make_mid(count // 2, groups),
        [shape((places, width)), shape((places, width), f32), shape((places, 1), f32)]
        + [shape((each, width))] * groups,
        hot_sums + [tok[:places], link],
        "mid_hot",
        mib=16,
    )
    mid_hot, normal_hot, factor_hot = outs[:3]
    pieces = outs[3:]
    landed = jnp.concatenate(
        [pieces[0]] + [hop(pieces[g], "dp", g) for g in range(1, groups)], axis=0
    )
    arrived_all = gather_rel(landed)
    arrived, hidden, grad_pre, even, odd = run(
        make_expert(count, experts),
        [
            shape((slots, width)),
            shape((experts, slots, hidden_dev)),
            shape((experts, slots, hidden_dev)),
            shape((slots // 2, 2 * width)),
            shape((slots // 2, 2 * width)),
        ],
        arrived_all + [up_weight, down_weight, grad_hidden],
        "experts",
        flops=6 * slots * width * hidden_dev * experts,
        mib=32,
    )
    sums = fold_scatter(even, odd, places, "fold_slots")
    pieces = run(
        make_split(count // 2, groups),
        [shape((each, 2 * width))] * groups,
        sums,
        "split_slots",
        mib=16,
    )
    back = [pieces[0]] + [hop(pieces[g], "dp", g) for g in range(1, groups)]
    grad_hot, expert_out = run(
        make_mid_back(groups),
        [shape((places, width)), shape((places, width))],
        back + [link, cot[:places], normal_hot, factor_hot],
        "mid_back",
        mib=16,
    )
    grad_hot_all = gather_rel(grad_hot)

    ctx_cold, part_cold = run(
        make_cold(hot_all, heads, scale),
        [shape((count * cold, heads * LANES)), shape((count * cold, width))],
        [qkv, proj],
        "cold",
        flops=4 * total * total * heads * LANES,
    )
    even, odd = parity(part_cold, cold)
    cold_sums = fold_scatter(even, odd, cold, "fold_cold")
    cot_all = gather_rel(cot[places:])
    gq, gk, gv, gp = run(
        lambda *refs: make_cold_back(count, places, heads, scale)(*refs),
        [
            shape((count * cold, heads * LANES)),
            shape((heads * LANES, total), f32),
            shape((heads * LANES, total), f32),
            shape((heads * LANES, width), f32),
            shape((count * cold, width)),
        ],
        cot_all + [qkv, proj, ctx_cold],
        "cold_back",
        flops=10 * total * total * heads * LANES,
    )[:4]
    grad_up, grad_down = run(
        make_weight_grads(experts),
        [shape(up_weight.shape), shape(down_weight.shape)],
        [arrived, slot_grads, hidden, grad_pre],
        "weight_grads",
        flops=4 * slots * width * hidden_dev * experts,
        mib=32,
    )

    sums, _ = run(
        make_hot_back(count, heads, size, groups, scale),
        [
            shape((groups, heads * 4 * size, width // groups)),
            shape((heads * 3 * size, total)),
        ],
        grad_hot_all + [qkv, proj, ctx_hot, gq, gk, gv, gp, fn],
        "hot_back",
        flops=2 * total * width * heads * 3 * LANES,
    )
    me = lax.axis_index("dp")
    mine = lax.dynamic_index_in_dim(sums, me, 0, False).astype(f32)
    for g in range(1, groups):
        piece = lax.dynamic_index_in_dim(sums, me ^ g, 0, False)
        mine = mine + hop(piece, "dp", g).astype(f32)
    base = heads * 3 * size
    grad_qkv = mine[:base].T.reshape(width // groups, heads, 3 * size)
    grad_proj = mine[base:].reshape(heads, size, width // groups)

    layer_out, gate_grad = run(
        make_epilogue(count // 2),
        [shape((rows, width)), shape((rows, 2), f32)],
        cold_sums
        + [tok[places:], mid_hot, perm, pick0, pick1, expert_out, gate_weights, cotangent],
        "epilogue",
        mib=24,
    )
    return (layer_out, gate_grad, grad_qkv, grad_proj, grad_up, grad_down)


def solution(mesh):
    return jax.shard_map(
        shards,
        mesh=mesh,
        in_specs=(
            P(("dp", "tensor"), None),
            P(("dp", "tensor"), None),
            P(("dp", "tensor"), None),
            P(("dp", "tensor"), None),
            P(("dp", "tensor"), None),
            P(None, "tensor", None),
            P("tensor", None, None),
            P("dp", None, "tensor"),
            P("dp", "tensor", None),
        ),
        out_specs=(
            P(("dp", "tensor"), None),
            P(("dp", "tensor"), None),
            P("dp", "tensor", None),
            P("tensor", None, "dp"),
            P("dp", None, "tensor"),
            P("dp", "tensor", None),
        ),
        check_vma=False,
    )
```

```python
import math

import jax
import jax.numpy as jnp
from jax import lax
from jax.experimental import pallas as pl
from jax.experimental.pallas import tpu as pltpu
from jax.sharding import PartitionSpec as P

CAP = 2
LANES = 128
epsilon = 1e-06
half_root = 1.0 / math.sqrt(2.0)
bell_scale = 1.0 / math.sqrt(2.0 * math.pi)
LOG2E = math.log2(math.e)
f32 = jnp.float32
bf16 = jnp.bfloat16


def norm_parts(row_block):
    widened = row_block.astype(f32)
    center = widened - jnp.mean(widened, axis=-1, keepdims=True)
    factor = lax.rsqrt(jnp.mean(center * center, axis=-1, keepdims=True) + epsilon)
    return (center * factor, factor)


def norm_back(normal_rows, factor, upstream):
    mean_up = jnp.mean(upstream, axis=-1, keepdims=True)
    mean_mix = jnp.mean(upstream * normal_rows, axis=-1, keepdims=True)
    return factor * (upstream - mean_up - normal_rows * mean_mix)


def dot(a, b):
    return lax.dot_general(a, b, (((1,), (0,)), ((), ())), preferred_element_type=f32)


def dot_nt(a, b):
    return lax.dot_general(a, b, (((1,), (1,)), ((), ())), preferred_element_type=f32)


def dot_tn(a, b):
    return lax.dot_general(a, b, (((0,), (0,)), ((), ())), preferred_element_type=f32)


def run(body, outs, ins, name, flops=0, mib=48, smem=(), loose=0, scratch=()):
    specs = [
        pl.BlockSpec(
            memory_space=pl.ANY if i < loose else pltpu.SMEM if i in smem else pltpu.VMEM
        )
        for i in range(len(ins))
    ]
    sizes = [math.prod(x.shape) * x.dtype.itemsize for x in list(ins) + list(outs)]
    return pl.pallas_call(
        body,
        out_shape=list(outs),
        in_specs=specs,
        out_specs=[pl.BlockSpec(memory_space=pltpu.VMEM)] * len(outs),
        scratch_shapes=list(scratch),
        compiler_params=pltpu.CompilerParams(vmem_limit_bytes=mib * 2**20),
        cost_estimate=pl.CostEstimate(
            flops=int(flops), bytes_accessed=int(sum(sizes)), transcendentals=0
        ),
        name=name,
    )(*ins)


def after(x, *others):
    return lax.optimization_barrier((x, others))[0]


def pull(pairs, sems):
    copies = [pltpu.make_async_copy(a, b, sems.at[i]) for i, (a, b) in enumerate(pairs)]
    for c in copies:
        c.start()
    for c in copies:
        c.wait()


def shape(dims, dtype=bf16):
    return jax.ShapeDtypeStruct(tuple(dims), dtype)


def block_of(rows, most=256):
    return max(b for b in range(16, most + 1, 16) if rows % b == 0)


def hop(x, axis, mask):
    size = lax.axis_size(axis)
    return lax.ppermute(x, axis, [(i, i ^ mask) for i in range(size)])


def gather_rel(x, hold=None, firm=()):
    size = lax.axis_size("tensor")
    have = {0: x}
    odd = {}
    mask = size // 2
    while mask > 1:
        have.update({k ^ mask: hop(y, "tensor", mask) for k, y in list(have.items())})
        mask //= 2
    if hold is not None:
        held = hold(have)
        last = size - 2
        have[last] = after(have[last], held)
    return [hop(have[k - 1], "tensor", 1) if k % 2 else have[k] for k in range(size)]


def fold_order(count):
    keys = range(0, count, 2)
    return sorted(keys, key=lambda k: tuple((k >> b) & 1 for b in range(1, 8)))


def prologue_body(tok_in, cot_in, group, gate_t, routes_t, slots_t, *outs):
    normed_o, cot_o, tok_o, perm_o, pick0_o, pick1_o, link_o, gout_o, tok, cot, sems = outs
    half = tok.shape[0] // 2
    pairs = [(tok_in, tok), (cot_in, cot)]
    copies = [
        pltpu.make_async_copy(
            a.at[i * half : (i + 1) * half], b.at[i * half : (i + 1) * half], sems.at[2 * n + i]
        )
        for n, (a, b) in enumerate(pairs)
        for i in range(2)
    ]
    for c in copies:
        c.start()
    rows = tok.shape[0]
    places = pick0_o.shape[1]
    code_t = jnp.where(slots_t[...] >= 0, (routes_t[...] ^ group[0]) * CAP + slots_t[...], -1)
    packed = jnp.concatenate(
        [code_t.astype(f32), gate_t[...], jnp.zeros((4, rows), f32)], axis=0
    ).T
    code = packed[:, 0:2].astype(jnp.int32)
    gate = packed[:, 2:4]
    lane = lax.broadcasted_iota(jnp.int32, (rows, LANES), 1)
    wide0 = (code[:, 0:1] == lane).astype(f32)
    wide1 = (code[:, 1:2] == lane).astype(f32)
    kept0 = (code[:, 0:1] >= 0).astype(f32)
    prim = wide0 + wide1 * (1.0 - kept0)
    plain = 1.0 - jnp.sum(prim, axis=1, keepdims=True)
    open_at = 1.0 - jnp.sum(prim, axis=0, keepdims=True)
    ri = lax.broadcasted_iota(jnp.int32, (rows, rows), 0)
    ci = lax.broadcasted_iota(jnp.int32, (rows, rows), 1)
    row_rank = dot(
        (ci < ri).astype(bf16), jnp.broadcast_to(plain, (rows, rows)).astype(bf16)
    )
    place_rank = dot(
        jnp.broadcast_to(open_at, (rows, rows)).astype(bf16), (ri < ci).astype(bf16)
    )
    filler = plain * open_at * (row_rank == place_rank).astype(f32)
    perm = (prim + filler).astype(bf16)
    perm_o[...] = perm
    for c in copies:
        c.wait()
    normal, _ = norm_parts(tok[...])
    normed_o[...] = dot_tn(perm, normal.astype(bf16)).astype(bf16)
    cot_o[...] = dot_tn(perm, cot[...]).astype(bf16)
    tok_o[...] = dot_tn(perm, tok[...]).astype(bf16)
    pick0 = wide0.astype(bf16)
    pick1 = wide1.astype(bf16)
    pick0_o[...] = pick0[:, :places]
    pick1_o[...] = pick1[:, :places]
    link_o[...] = dot_tn((pick0 + pick1), prim.astype(bf16))[:places, :places].astype(bf16)
    upstream = cot[...].astype(f32)
    g0 = (gate[:, 0:1] * upstream).astype(bf16)
    g1 = (gate[:, 1:2] * upstream).astype(bf16)
    gout_o[...] = (dot_tn(pick0, g0) + dot_tn(pick1, g1))[:places].astype(bf16)


def make_prep(heads, size):
    def body(w, p, wo, po):
        wo[...] = jnp.zeros_like(wo)
        po[...] = jnp.zeros_like(po)
        for h in range(heads):
            for i in range(3):
                at = (3 * h + i) * LANES
                wo[at : at + size] = w[h, i * size : (i + 1) * size]
            po[h * LANES : h * LANES + size] = p[h]

    return body


def spare_lanes(dims, size):
    lane = lax.broadcasted_iota(jnp.int32, dims, 1) % LANES
    return (lane >= size) & (lane < size + 3)


def with_term(rows, term, size):
    lane = lax.broadcasted_iota(jnp.int32, rows.shape, 1)
    first = term.astype(bf16).astype(f32)
    second = (term - first).astype(bf16).astype(f32)
    third = term - first - second
    term = jnp.where(lane == size, first, jnp.where(lane == size + 1, second, third))
    return jnp.where(spare_lanes(rows.shape, size), term, rows.astype(f32)).astype(bf16)


def project(rows, weights, heads, size, scale):
    raw = dot_nt(rows, weights)
    part = lax.broadcasted_iota(jnp.int32, raw.shape, 1) // LANES % 3
    factor = jnp.where(part == 0, scale * LOG2E, 1.0)
    ones = ((part != 0) & spare_lanes(raw.shape, size)).astype(f32)
    return (raw * factor + ones).astype(bf16)


def attend(queries, keys, values, size):
    raised = jnp.exp2(dot_nt(queries, keys))
    total = jnp.sum(raised, axis=-1, keepdims=True)
    shares = raised * (1.0 / total)
    return dot(shares.astype(bf16), values).astype(bf16), with_term(queries, -jnp.log2(total), size)


def part_of(ref, rows, which, head):
    at = (3 * head + which) * LANES
    return ref[rows, at : at + LANES]


def pieces_of(ref, first, count, every, lo, hi, at):
    return jnp.concatenate(
        [ref[(first + k) * every + lo : (first + k) * every + hi, at] for k in range(count)], axis=0
    )


def make_half(count, heads, size, scale):
    def body(*refs):
        shards, (weights, qkv, fn_t, fn, sems) = refs[:count], refs[count:]
        rows = shards[0].shape[0]
        pull([(shards[k], fn.at[k * rows : (k + 1) * rows]) for k in range(count)], sems)
        for k in range(count):
            at = slice(k * rows, (k + 1) * rows)
            fn_t[:, at] = fn[at, :].T
        step = block_of(fn.shape[0])

        def chunk(i, _):
            at = pl.ds(pl.multiple_of(i * step, 16), step)
            qkv[at, :] = project(fn[at, :], weights[...], heads, size, scale)
            return 0

        lax.fori_loop(0, fn.shape[0] // step, chunk, 0)

    return body


def make_turn(count):
    def body(*refs):
        shards, fn_t = refs[:count], refs[count]
        rows = shards[0].shape[0]
        for k in range(count):
            fn_t[:, k * rows : (k + 1) * rows] = shards[k][...].T

    return body


def make_front(count, places, heads, size, scale):
    def body(*refs):
        half = count // 2
        shards, (first, weights, proj) = refs[:half], refs[half : half + 3]
        qkv, ctx, ask, even, odd, fn, sems = refs[half + 3 :]
        rows = shards[0].shape[0]
        pull([(shards[k], fn.at[k * rows : (k + 1) * rows]) for k in range(half)], sems)
        done = first.shape[0]
        qkv[:done] = first[...]
        step = block_of(fn.shape[0])

        def chunk(i, _):
            at = pl.ds(pl.multiple_of(i * step, 16), step)
            to = pl.ds(pl.multiple_of(done + i * step, 16), step)
            qkv[to, :] = project(fn[at, :], weights[...], heads, size, scale)
            return 0

        lax.fori_loop(0, fn.shape[0] // step, chunk, 0)
        every = slice(None)
        for h in range(heads):
            cut = slice(h * LANES, (h + 1) * LANES)
            queries = pieces_of(
                qkv, 0, count, rows, 0, places, slice(3 * h * LANES, (3 * h + 1) * LANES)
            )
            ctx[:, cut], ask[:, cut] = attend(
                queries, part_of(qkv, every, 1, h), part_of(qkv, every, 2, h), size
            )
        part = dot(ctx[...], proj[...]).astype(bf16)
        for i, k in enumerate(range(0, count, 2)):
            even[i * places : (i + 1) * places] = part[k * places : (k + 1) * places]
            odd[i * places : (i + 1) * places] = part[(k + 1) * places : (k + 2) * places]

    return body


def make_cold(count, places, heads, size):
    def body(qkv, proj, ctx, ask, even, odd):
        rows = qkv.shape[0] // count
        cold = rows - places
        every = slice(None)
        group = min(4, count)
        order = fold_order(count)
        for first in range(0, count, group):
            at = slice(first * cold, (first + group) * cold)
            for h in range(heads):
                cut = slice(h * LANES, (h + 1) * LANES)
                queries = pieces_of(
                    qkv, first, group, rows, places, rows, slice(3 * h * LANES, (3 * h + 1) * LANES)
                )
                ctx[at, cut], ask[at, cut] = attend(
                    queries, part_of(qkv, every, 1, h), part_of(qkv, every, 2, h), size
                )
            part = dot(ctx[at, :], proj[...]).astype(bf16)
            for k in range(first, first + group):
                to = odd if k % 2 else even
                i = order.index(k // 2 * 2)
                to[i * cold : (i + 1) * cold] = part[(k - first) * cold : (k - first + 1) * cold]

    return body


def back_block(ask, keys, values, ctx, grad_ctx, size):
    shares = jnp.exp2(dot_nt(ask, keys))
    mix = jnp.sum(grad_ctx.astype(f32) * ctx.astype(f32), axis=-1, keepdims=True)
    grad_ctx = with_term(grad_ctx, -mix, size)
    grad_scores = (shares * dot_nt(grad_ctx, values)).astype(bf16)
    return (
        dot(grad_scores, keys),
        dot_tn(ask, grad_scores),
        dot_tn(grad_ctx, shares.astype(bf16)),
    )


def make_cold_back(count, places, heads, size, scale):
    def body(*refs):
        shards, (qkv, proj, ctx, ask) = refs[:count], refs[count : count + 4]
        gq, gk, gv, gp, cots, sems = refs[count + 4 :]
        cold = shards[0].shape[0]
        pull([(shards[k], cots.at[k * cold : (k + 1) * cold]) for k in range(count)], sems)
        every = slice(None)
        group = min(4, count)
        for first in range(0, count, group):
            at = slice(first * cold, (first + group) * cold)
            grad_ctx = dot_nt(cots[at, :], proj[...]).astype(bf16)
            proj_grad = dot_tn(ctx[at, :], cots[at, :])
            for h in range(heads):
                cut = slice(h * LANES, (h + 1) * LANES)
                a, b, c = back_block(
                    ask[at, cut],
                    part_of(qkv, every, 1, h),
                    part_of(qkv, every, 2, h),
                    ctx[at, cut],
                    grad_ctx[:, cut],
                    size,
                )
                gq[at, cut] = (a * scale).astype(bf16)
                if first:
                    gk[cut, :] += b
                    gv[cut, :] += c
                else:
                    gk[cut, :] = b
                    gv[cut, :] = c
            if first:
                gp[...] += proj_grad
            else:
                gp[...] = proj_grad

    return body


def make_hot_back(count, heads, size, groups, scale):
    def body(*refs):
        shards = refs[:count]
        place, qkv, proj, ctx, ask, gq, gk, gv, gp, fn_a, fn_b = refs[count : count + 11]
        outs = refs[count + 11 : count + 11 + groups]
        rows_t, grad_q, whole = refs[count + 11 + groups :]
        grads = jnp.concatenate([s[...] for s in shards], axis=0)
        places = shards[0].shape[0]
        rows = qkv.shape[0] // count
        cold = rows - places
        grad_ctx = dot_nt(grads, proj[...]).astype(bf16)
        proj_grad = gp[...] + dot_tn(ctx[...], grads)
        base = heads * 3 * size
        every = slice(None)
        proj_rows = []
        for h in range(heads):
            cut = slice(h * LANES, (h + 1) * LANES)
            a, b, c = back_block(
                ask[:, cut],
                part_of(qkv, every, 1, h),
                part_of(qkv, every, 2, h),
                ctx[:, cut],
                grad_ctx[:, cut],
                size,
            )
            a = (a * scale).astype(bf16)
            for k in range(count):
                grad_q[k * rows : k * rows + places] = a[k * places : (k + 1) * places]
                grad_q[k * rows + places : (k + 1) * rows] = gq[k * cold : (k + 1) * cold, cut]
            at = h * 3 * size
            rows_t[at : at + size, :] = grad_q[...].T[:size]
            rows_t[at + size : at + 2 * size, :] = ((gk[cut, :] + b) * (1.0 / LOG2E))[
                :size
            ].astype(bf16)
            rows_t[at + 2 * size : at + 3 * size, :] = (gv[cut, :] + c)[:size].astype(bf16)
            proj_rows.append(proj_grad[h * LANES : h * LANES + size].astype(bf16))
        done = fn_a.shape[1]
        turned = rows_t[...].T
        whole[:, :base] = (dot(fn_a[...], turned[:done]) + dot(fn_b[...], turned[done:])).astype(
            bf16
        )
        whole[:, base:] = jnp.concatenate(proj_rows, axis=0).T
        each = whole.shape[0] // groups
        for g in range(groups):
            at = pl.multiple_of((place[0] ^ g) * each, 16)
            outs[g][...] = whole[pl.ds(at, each), :]

    return body


def make_last(heads, size, groups):
    def body(*refs):
        parts, (qkv_o, proj_o) = refs[:groups], refs[groups:]
        total = total_of(parts)
        base = heads * 3 * size
        turned = total[:, base:].T
        for h in range(heads):
            qkv_o[:, h, :] = total[:, h * 3 * size : (h + 1) * 3 * size]
            proj_o[h] = turned[h * size : (h + 1) * size]

    return body


def make_fold(count):
    def body(mine, theirs, *outs):
        rows = outs[0].shape[0]
        for i in range(count):
            at = slice(i * rows, (i + 1) * rows)
            outs[i][...] = (mine[at].astype(f32) + theirs[at].astype(f32)).astype(bf16)

    return body


def total_of(refs):
    total = refs[0][...].astype(f32)
    for r in refs[1:]:
        total = total + r[...].astype(f32)
    return total


def make_mid(count, groups):
    def body(*refs):
        parts, (tok, link) = refs[:count], refs[count : count + 2]
        mid_o, normal_o, factor_o = refs[count + 2 : count + 5]
        outs = refs[count + 5 :]
        mid = (tok[...].astype(f32) + total_of(parts)).astype(bf16)
        normal, factor = norm_parts(mid)
        mid_o[...] = mid
        normal_o[...] = normal
        factor_o[...] = factor
        slot_in = dot(link[...], normal.astype(bf16))
        each = slot_in.shape[0] // groups
        for g in range(groups):
            outs[g][...] = slot_in[g * each : (g + 1) * each].astype(bf16)

    return body


def slot_mask(rows, experts, e):
    row = lax.broadcasted_iota(jnp.int32, (rows, 1), 0)
    return (row // CAP) % experts == e


def make_expert_grad(count, experts):
    def body(*refs):
        shards, down, grads, out = refs[:count], refs[count], refs[count + 1], refs[count + 2]
        grads[...] = jnp.concatenate([s[...] for s in shards], axis=0)
        for e in range(experts):
            out[e] = dot_nt(grads[...], down[e])

    return body


def make_expert(count, experts):
    def body(*refs):
        shards = refs[:count]
        up, down, grad_hidden, arrived, hid_o, pre_o, even, odd = refs[count:]
        arrived[...] = jnp.concatenate([s[...] for s in shards], axis=0)
        rows = arrived.shape[0]
        forth = None
        back = None
        for e in range(experts):
            keep = slot_mask(rows, experts, e)
            pre = dot(arrived[...], up[e])
            cdf = 0.5 * (1.0 + lax.erf(pre * half_root))
            hidden = jnp.where(keep, pre * cdf, 0.0).astype(bf16)
            slope = cdf + pre * jnp.exp(-0.5 * pre * pre) * bell_scale
            grad_pre = jnp.where(keep, grad_hidden[e] * slope, 0.0).astype(bf16)
            hid_o[e] = hidden
            pre_o[e] = grad_pre
            a = dot(hidden, down[e])
            b = dot_nt(grad_pre, up[e])
            forth = a if forth is None else forth + a
            back = b if back is None else back + b
        both = jnp.concatenate([back, forth], axis=1).astype(bf16)
        each = rows // count
        for k in range(count):
            to = odd if k % 2 else even
            to[(k // 2) * each : (k // 2 + 1) * each] = both[k * each : (k + 1) * each]

    return body


def make_weight_grads(experts):
    def body(arrived, grads, hidden, grad_pre, up_o, down_o):
        for e in range(experts):
            up_o[e] = dot_tn(arrived[...], grad_pre[e]).astype(bf16)
            down_o[e] = dot_tn(hidden[e], grads[...]).astype(bf16)

    return body


def make_split(count, groups):
    def body(*refs):
        parts, outs = refs[:count], refs[count:]
        total = total_of(parts)
        each = total.shape[0] // groups
        for g in range(groups):
            outs[g][...] = total[g * each : (g + 1) * each].astype(bf16)

    return body


def make_mid_back(groups):
    def body(*refs):
        parts = refs[:groups]
        link, cot, normal, factor, grad_o, expert_o = refs[groups:]
        both = jnp.concatenate([p[...].astype(f32) for p in parts], axis=0).astype(bf16)
        width = cot.shape[1]
        expert_o[...] = both[:, width:]
        grad_norm = dot_tn(link[...], both[:, :width])
        grad_o[...] = (
            cot[...].astype(f32) + norm_back(normal[...], factor[...], grad_norm)
        ).astype(bf16)

    return body


def make_epilogue(count):
    def body(*refs):
        parts = refs[:count]
        tok, mid_hot, perm, pick0, pick1, experts, gate_t, cot, out, gate_o = refs[count:]
        cold = (tok[...].astype(f32) + total_of(parts)).astype(bf16)
        ordered = jnp.concatenate([mid_hot[...], cold], axis=0)
        mid = dot(perm[...], ordered)
        gate = jnp.concatenate([gate_t[...], jnp.zeros((6, gate_t.shape[1]), f32)], axis=0).T
        first = dot(pick0[...], experts[...])
        second = dot(pick1[...], experts[...])
        out[...] = (mid + gate[:, 0:1] * first + gate[:, 1:2] * second).astype(bf16)
        upstream = cot[...].astype(f32)
        lane = lax.broadcasted_iota(jnp.int32, (upstream.shape[0], LANES), 1)
        one = jnp.sum(upstream * first, axis=-1, keepdims=True)
        two = jnp.sum(upstream * second, axis=-1, keepdims=True)
        gate_o[...] = jnp.where(lane == 0, one, two).T[:2]

    return body


def fold_scatter(even, odd, rows, name):
    count = lax.axis_size("tensor") // 2
    theirs = hop(odd, "tensor", 1)
    sums = run(
        make_fold(count), [shape((rows, even.shape[1]))] * count, [even, theirs], name, mib=24
    )
    return [sums[0]] + [hop(sums[i], "tensor", 2 * i) for i in range(1, count)]


def halving_scatter(even, odd, name):
    mine, mask, theirs = even, 1, odd
    while True:
        theirs = hop(theirs, "tensor", mask)
        if mine.shape[0] == even.shape[0] * 2 // lax.axis_size("tensor"):
            return [mine, theirs]
        half = (mine.shape[0] // 2, mine.shape[1])
        mine, theirs = run(
            make_fold(2), [shape(half), shape(half)], [mine, theirs], f"{name}_{mask}", mib=24
        )
        mask *= 2


def shards(
    tokens,
    cotangent,
    gate_weights,
    routes,
    slot_index,
    qkv_weight,
    proj_weight,
    up_weight,
    down_weight,
):
    rows, width = tokens.shape
    heads, size = qkv_weight.shape[1], qkv_weight.shape[2] // 3
    scale = size ** (-0.5)
    groups = lax.axis_size("dp")
    count = lax.axis_size("tensor")
    experts, _, hidden_dev = up_weight.shape
    each = experts * CAP
    places = groups * each
    cold = rows - places
    hot_all = count * places
    total = count * rows
    slots = count * places

    wqkv, proj = run(
        make_prep(heads, size),
        [shape((heads * 3 * LANES, width)), shape((heads * LANES, width))],
        [qkv_weight.transpose(1, 2, 0), proj_weight],
        "prep",
        mib=24,
    )
    group = (lax.axis_index("dp") * experts).astype(jnp.int32).reshape(1)
    normed, cot, tok, perm, pick0, pick1, link, grad_out = run(
        prologue_body,
        [
            shape((rows, width)),
            shape((rows, width)),
            shape((rows, width)),
            shape((rows, rows)),
            shape((rows, places)),
            shape((rows, places)),
            shape((places, places)),
            shape((places, width)),
        ],
        [tokens, cotangent, group, gate_weights.T, routes.T, slot_index.T],
        "prologue",
        smem=(2,),
        loose=2,
        mib=24,
        scratch=[
            pltpu.VMEM((rows, width), bf16),
            pltpu.VMEM((rows, width), bf16),
            pltpu.SemaphoreType.DMA((4,)),
        ],
    )
    half = count // 2
    cot_cold = cot[places:]

    def first_half(have):
        near = [
            hop(have[k - 1], "tensor", 1) if k % 2 else have[k] for k in range(half)
        ]
        return run(
            make_half(half, heads, size, scale),
            [shape((half * rows, heads * 3 * LANES)), shape((width, half * rows))],
            near + [wqkv],
            "half",
            flops=2 * half * rows * width * heads * 3 * LANES,
            loose=half,
            mib=40,
            scratch=[
                pltpu.VMEM((half * rows, width), bf16),
                pltpu.SemaphoreType.DMA((half,)),
            ],
        )

    box = []

    def hold(have):
        box.append((have, first_half(have)))
        return box[0][1]

    normed_all = gather_rel(normed, hold)
    have, (qkv_a, fn_a) = box[0]

    pieces = [grad_out[g * each : (g + 1) * each] for g in range(groups)]
    landed = jnp.concatenate(
        [pieces[0]] + [hop(pieces[g], "dp", g) for g in range(1, groups)], axis=0
    )
    grads_all = gather_rel(landed)
    slot_grads, grad_hidden = run(
        make_expert_grad(count, experts),
        [shape((slots, width)), shape((experts, slots, hidden_dev), f32)],
        grads_all + [down_weight],
        "slot_grads",
        flops=2 * slots * width * hidden_dev * experts,
        mib=24,
    )
    far = count // 2
    cots = {0: cot_cold}
    mask = 2
    while mask < far:
        cots.update({k ^ mask: hop(y, "tensor", mask) for k, y in list(cots.items())})
        mask *= 2
    near_cots = list(cots.values())

    qkv, ctx_hot, ask_hot, even, odd = run(
        make_front(count, places, heads, size, scale),
        [
            shape((total, heads * 3 * LANES)),
            shape((hot_all, heads * LANES)),
            shape((hot_all, heads * LANES)),
            shape((hot_all // 2, width)),
            shape((hot_all // 2, width)),
        ],
        after(normed_all[half:], grad_hidden, near_cots) + [qkv_a, wqkv, proj],
        "front",
        flops=2 * total * width * heads * 3 * LANES,
        loose=half,
        scratch=[
            pltpu.VMEM((half * rows, width), bf16),
            pltpu.SemaphoreType.DMA((half,)),
        ],
    )
    cots[far] = hop(after(cot_cold, have[far]), "tensor", far)
    odd = after(odd, cots[far])
    hot_sums = fold_scatter(even, odd, places, "fold_hot")

    outs = run(
        make_mid(count // 2, groups),
        [shape((places, width)), shape((places, width), f32), shape((places, 1), f32)]
        + [shape((each, width))] * groups,
        hot_sums + [tok[:places], link],
        "mid_hot",
        mib=16,
    )
    mid_hot, normal_hot, factor_hot = outs[:3]
    pieces = outs[3:]

    ctx_cold, ask_cold, even_cold, odd_cold = run(
        make_cold(count, places, heads, size),
        [
            shape((count * cold, heads * LANES)),
            shape((count * cold, heads * LANES)),
            shape((count * cold // 2, width)),
            shape((count * cold // 2, width)),
        ],
        [after(qkv, mid_hot), proj],
        "cold",
        flops=4 * total * total * heads * LANES,
    )
    start = after(cots[far], mid_hot)
    rest = {far: start}
    mask = 2
    while mask < far:
        rest.update({k ^ mask: hop(y, "tensor", mask) for k, y in list(rest.items())})
        mask *= 2
    cots.update(rest)
    landed = jnp.concatenate(
        [pieces[0]] + [hop(pieces[g], "dp", g) for g in range(1, groups)], axis=0
    )
    landed = after(landed, ctx_cold, list(cots.values()))
    arrived_all = gather_rel(landed)
    arrived, hidden, grad_pre, even, odd = run(
        make_expert(count, experts),
        [
            shape((slots, width)),
            shape((experts, slots, hidden_dev)),
            shape((experts, slots, hidden_dev)),
            shape((slots // 2, 2 * width)),
            shape((slots // 2, 2 * width)),
        ],
        arrived_all + [up_weight, down_weight, grad_hidden],
        "experts",
        flops=6 * slots * width * hidden_dev * experts,
        mib=32,
    )
    sums = fold_scatter(even, odd, places, "fold_slots")

    pieces = run(
        make_split(count // 2, groups),
        [shape((each, 2 * width))] * groups,
        sums,
        "split_slots",
        mib=16,
    )
    back = [pieces[0]] + [hop(pieces[g], "dp", g) for g in range(1, groups)]
    cot_all = [hop(cots[k - 1], "tensor", 1) if k % 2 else cots[k] for k in range(count)]
    gq, gk, gv, gp = run(
        make_cold_back(count, places, heads, size, scale),
        [
            shape((count * cold, heads * LANES)),
            shape((heads * LANES, total), f32),
            shape((heads * LANES, total), f32),
            shape((heads * LANES, width), f32),
        ],
        cot_all + [after(qkv, pieces[0]), proj, ctx_cold, ask_cold],
        "cold_back",
        flops=10 * total * total * heads * LANES,
        loose=count,
        scratch=[
            pltpu.VMEM((count * cold, width), bf16),
            pltpu.SemaphoreType.DMA((count,)),
        ],
    )
    back = after(back, gp)
    grad_hot, expert_out = run(
        make_mid_back(groups),
        [shape((places, width)), shape((places, width))],
        back + [link, cot[:places], normal_hot, factor_hot],
        "mid_back",
        mib=16,
    )
    box.clear()

    def turn(_):
        box.append(
            run(
                make_turn(half),
                [shape((width, half * rows))],
                after(normed_all[half:], grad_hot),
                "turn",
                mib=24,
            )[0]
        )
        return box[0]

    grad_hot_all = gather_rel(grad_hot, turn)
    fn_b = box[0]
    cold_sums = halving_scatter(even_cold, after(odd_cold, grad_hot_all), "fold_cold")

    me = lax.axis_index("dp").astype(jnp.int32).reshape(1)
    pieces = run(
        make_hot_back(count, heads, size, groups, scale),
        [shape((width // groups, heads * 4 * size))] * groups,
        grad_hot_all + [me, qkv, proj, ctx_hot, ask_hot, gq, gk, gv, gp, fn_a, fn_b],
        "hot_back",
        flops=2 * total * width * heads * 3 * LANES,
        smem=(count,),
        scratch=[
            pltpu.VMEM((heads * 3 * size, total), bf16),
            pltpu.VMEM((total, LANES), bf16),
            pltpu.VMEM((width, heads * 4 * size), bf16),
        ],
    )
    grad_up, grad_down = run(
        make_weight_grads(experts),
        [shape(up_weight.shape), shape(down_weight.shape)],
        [after(arrived, pieces[0]), slot_grads, hidden, grad_pre],
        "weight_grads",
        flops=4 * slots * width * hidden_dev * experts,
        mib=32,
    )
    parts = [pieces[0]] + [hop(pieces[g], "dp", g) for g in range(1, groups)]
    layer_out, gate_grad = run(
        make_epilogue(2),
        [shape((rows, width)), shape((2, rows), f32)],
        cold_sums
        + [tok[places:], mid_hot, perm, pick0, pick1, expert_out, gate_weights.T, cotangent],
        "epilogue",
        mib=24,
    )
    grad_qkv, grad_proj = run(
        make_last(heads, size, groups),
        [shape((width // groups, heads, 3 * size), f32), shape((heads, size, width // groups), f32)],
        after(parts, layer_out, grad_up),
        "last",
        mib=24,
    )
    return (layer_out, gate_grad.T, grad_qkv, grad_proj, grad_up, grad_down)


def solution(mesh):
    return jax.shard_map(
        shards,
        mesh=mesh,
        in_specs=(
            P(("dp", "tensor"), None),
            P(("dp", "tensor"), None),
            P(("dp", "tensor"), None),
            P(("dp", "tensor"), None),
            P(("dp", "tensor"), None),
            P(None, "tensor", None),
            P("tensor", None, None),
            P("dp", None, "tensor"),
            P("dp", "tensor", None),
        ),
        out_specs=(
            P(("dp", "tensor"), None),
            P(("dp", "tensor"), None),
            P("dp", "tensor", None),
            P("tensor", None, "dp"),
            P("dp", None, "tensor"),
            P("dp", "tensor", None),
        ),
        check_vma=False,
    )
```

```python
import math

import jax
import jax.numpy as jnp
from jax import lax
from jax.experimental import pallas as pl
from jax.experimental.pallas import tpu as pltpu
from jax.sharding import PartitionSpec as P

CAP = 2
LANES = 128
epsilon = 1e-06
half_root = 1.0 / math.sqrt(2.0)
bell_scale = 1.0 / math.sqrt(2.0 * math.pi)
LOG2E = math.log2(math.e)
f32 = jnp.float32
bf16 = jnp.bfloat16


def norm_parts(row_block):
    widened = row_block.astype(f32)
    center = widened - jnp.mean(widened, axis=-1, keepdims=True)
    factor = lax.rsqrt(jnp.mean(center * center, axis=-1, keepdims=True) + epsilon)
    return (center * factor, factor)


def norm_back(normal_rows, factor, upstream):
    mean_up = jnp.mean(upstream, axis=-1, keepdims=True)
    mean_mix = jnp.mean(upstream * normal_rows, axis=-1, keepdims=True)
    return factor * (upstream - mean_up - normal_rows * mean_mix)


def dot(a, b):
    return lax.dot_general(a, b, (((1,), (0,)), ((), ())), preferred_element_type=f32)


def dot_nt(a, b):
    return lax.dot_general(a, b, (((1,), (1,)), ((), ())), preferred_element_type=f32)


def dot_tn(a, b):
    return lax.dot_general(a, b, (((0,), (0,)), ((), ())), preferred_element_type=f32)


def run(body, outs, ins, name, flops=0, extra=1, smem=(), loose=0, scratch=()):
    specs = [
        pl.BlockSpec(
            memory_space=pl.ANY if i < loose else pltpu.SMEM if i in smem else pltpu.VMEM
        )
        for i in range(len(ins))
    ]
    sizes = [math.prod(x.shape) * x.dtype.itemsize for x in list(ins)[loose:] + list(outs)]
    sizes += [math.prod(x.shape) * x.dtype.itemsize for x in scratch if x.dtype in (f32, bf16)]
    limit = int(sum(sizes) * 1.2) + extra * 2**20
    return pl.pallas_call(
        body,
        out_shape=list(outs),
        in_specs=specs,
        out_specs=[pl.BlockSpec(memory_space=pltpu.VMEM)] * len(outs),
        scratch_shapes=list(scratch),
        compiler_params=pltpu.CompilerParams(vmem_limit_bytes=limit),
        cost_estimate=pl.CostEstimate(
            flops=int(flops), bytes_accessed=int(sum(sizes)), transcendentals=0
        ),
        name=name,
    )(*ins)


def after(x, *others):
    return lax.optimization_barrier((x, others))[0]


def pull(pairs, sems):
    copies = [pltpu.make_async_copy(a, b, sems.at[i]) for i, (a, b) in enumerate(pairs)]
    for c in copies:
        c.start()
    for c in copies:
        c.wait()


def shape(dims, dtype=bf16):
    return jax.ShapeDtypeStruct(tuple(dims), dtype)


def block_of(rows, most=256):
    return max(b for b in range(16, most + 1, 16) if rows % b == 0)


def hop(x, axis, mask):
    size = lax.axis_size(axis)
    return lax.ppermute(x, axis, [(i, i ^ mask) for i in range(size)])


def gather_rel(x, hold=None, firm=()):
    size = lax.axis_size("tensor")
    have = {0: x}
    odd = {}
    mask = size // 2
    while mask > 1:
        have.update({k ^ mask: hop(y, "tensor", mask) for k, y in list(have.items())})
        mask //= 2
    if hold is not None:
        held = hold(have)
        last = size - 2
        have[last] = after(have[last], held)
    return [hop(have[k - 1], "tensor", 1) if k % 2 else have[k] for k in range(size)]


def fold_order(keys, flip=False):
    bits = range(7, -1, -1) if flip else range(8)
    return sorted(keys, key=lambda k: tuple((k >> b) & 1 for b in bits))


def prologue_body(tok_in, cot_in, group, gate_t, routes_t, slots_t, *outs):
    normed_o, cot_o, tok_o, perm_o, pick0_o, pick1_o, link_o, gout_o, tok, cot, sems = outs
    half = tok.shape[0] // 2
    pairs = [(tok_in, tok), (cot_in, cot)]
    copies = [
        pltpu.make_async_copy(
            a.at[i * half : (i + 1) * half], b.at[i * half : (i + 1) * half], sems.at[2 * n + i]
        )
        for n, (a, b) in enumerate(pairs)
        for i in range(2)
    ]
    for c in copies:
        c.start()
    rows = tok.shape[0]
    places = pick0_o.shape[1]
    code_t = jnp.where(slots_t[...] >= 0, (routes_t[...] ^ group[0]) * CAP + slots_t[...], -1)
    packed = jnp.concatenate(
        [code_t.astype(f32), gate_t[...], jnp.zeros((4, rows), f32)], axis=0
    ).T
    code = packed[:, 0:2].astype(jnp.int32)
    gate = packed[:, 2:4]
    lane = lax.broadcasted_iota(jnp.int32, (rows, LANES), 1)
    wide0 = (code[:, 0:1] == lane).astype(f32)
    wide1 = (code[:, 1:2] == lane).astype(f32)
    kept0 = (code[:, 0:1] >= 0).astype(f32)
    prim = wide0 + wide1 * (1.0 - kept0)
    plain = 1.0 - jnp.sum(prim, axis=1, keepdims=True)
    open_at = 1.0 - jnp.sum(prim, axis=0, keepdims=True)
    ri = lax.broadcasted_iota(jnp.int32, (rows, rows), 0)
    ci = lax.broadcasted_iota(jnp.int32, (rows, rows), 1)
    row_rank = dot(
        (ci < ri).astype(bf16), jnp.broadcast_to(plain, (rows, rows)).astype(bf16)
    )
    place_rank = dot(
        jnp.broadcast_to(open_at, (rows, rows)).astype(bf16), (ri < ci).astype(bf16)
    )
    filler = plain * open_at * (row_rank == place_rank).astype(f32)
    perm = (prim + filler).astype(bf16)
    perm_o[...] = perm
    for c in copies:
        c.wait()
    normal, _ = norm_parts(tok[...])
    normed_o[...] = dot_tn(perm, normal.astype(bf16)).astype(bf16)
    cot_o[...] = dot_tn(perm, cot[...]).astype(bf16)
    tok_o[...] = dot_tn(perm, tok[...]).astype(bf16)
    pick0 = wide0.astype(bf16)
    pick1 = wide1.astype(bf16)
    pick0_o[...] = pick0[:, :places]
    pick1_o[...] = pick1[:, :places]
    link_o[...] = dot_tn((pick0 + pick1), prim.astype(bf16))[:places, :places].astype(bf16)
    upstream = cot[...].astype(f32)
    g0 = (gate[:, 0:1] * upstream).astype(bf16)
    g1 = (gate[:, 1:2] * upstream).astype(bf16)
    gout_o[...] = (dot_tn(pick0, g0) + dot_tn(pick1, g1))[:places].astype(bf16)


def make_prep(heads, size):
    def body(w, p, wo, po):
        wo[...] = jnp.zeros_like(wo)
        po[...] = jnp.zeros_like(po)
        for h in range(heads):
            for i in range(3):
                at = (3 * h + i) * LANES
                wo[at : at + size] = w[h, i * size : (i + 1) * size]
            po[h * LANES : h * LANES + size] = p[h]

    return body


def spare_lanes(dims, size):
    lane = lax.broadcasted_iota(jnp.int32, dims, 1) % LANES
    return (lane >= size) & (lane < size + 3)


def with_term(rows, term, size):
    lane = lax.broadcasted_iota(jnp.int32, rows.shape, 1)
    first = term.astype(bf16).astype(f32)
    second = (term - first).astype(bf16).astype(f32)
    third = term - first - second
    term = jnp.where(lane == size, first, jnp.where(lane == size + 1, second, third))
    return jnp.where(spare_lanes(rows.shape, size), term, rows.astype(f32)).astype(bf16)


def project(rows, weights, heads, size, scale):
    raw = dot_nt(rows, weights)
    part = lax.broadcasted_iota(jnp.int32, raw.shape, 1) // LANES % 3
    factor = jnp.where(part == 0, scale * LOG2E, 1.0)
    ones = ((part != 0) & spare_lanes(raw.shape, size)).astype(f32)
    return (raw * factor + ones).astype(bf16)


def attend(queries, keys, values, size):
    raised = jnp.exp2(dot_nt(queries, keys))
    total = jnp.sum(raised, axis=-1, keepdims=True)
    shares = raised * (1.0 / total)
    return dot(shares.astype(bf16), values).astype(bf16), with_term(queries, -jnp.log2(total), size)


def part_of(ref, rows, which, head):
    at = (3 * head + which) * LANES
    return ref[rows, at : at + LANES]


def pieces_of(ref, first, count, every, lo, hi, at):
    return jnp.concatenate(
        [ref[(first + k) * every + lo : (first + k) * every + hi, at] for k in range(count)], axis=0
    )


def make_half(count, heads, size, scale):
    def body(*refs):
        shards, (weights, qkv, fn_t, fn, sems) = refs[:count], refs[count:]
        rows = shards[0].shape[0]
        pull([(shards[k], fn.at[k * rows : (k + 1) * rows]) for k in range(count)], sems)
        for k in range(count):
            at = slice(k * rows, (k + 1) * rows)
            fn_t[:, at] = fn[at, :].T
        step = block_of(fn.shape[0])

        def chunk(i, _):
            at = pl.ds(pl.multiple_of(i * step, 16), step)
            qkv[at, :] = project(fn[at, :], weights[...], heads, size, scale)
            return 0

        lax.fori_loop(0, fn.shape[0] // step, chunk, 0)

    return body


def make_turn(count):
    def body(*refs):
        shards, fn_t = refs[:count], refs[count]
        rows = shards[0].shape[0]
        for k in range(count):
            fn_t[:, k * rows : (k + 1) * rows] = shards[k][...].T

    return body


def make_front(count, places, heads, size, scale):
    def body(*refs):
        half = count // 2
        shards, (first, weights, proj) = refs[:half], refs[half : half + 3]
        qkv, ctx, ask, even, odd, fn, sems = refs[half + 3 :]
        rows = shards[0].shape[0]
        pull([(shards[k], fn.at[k * rows : (k + 1) * rows]) for k in range(half)], sems)
        done = first.shape[0]
        qkv[:done] = first[...]
        step = block_of(fn.shape[0])

        def chunk(i, _):
            at = pl.ds(pl.multiple_of(i * step, 16), step)
            to = pl.ds(pl.multiple_of(done + i * step, 16), step)
            qkv[to, :] = project(fn[at, :], weights[...], heads, size, scale)
            return 0

        lax.fori_loop(0, fn.shape[0] // step, chunk, 0)
        every = slice(None)
        for h in range(heads):
            cut = slice(h * LANES, (h + 1) * LANES)
            queries = pieces_of(
                qkv, 0, count, rows, 0, places, slice(3 * h * LANES, (3 * h + 1) * LANES)
            )
            ctx[:, cut], ask[:, cut] = attend(
                queries, part_of(qkv, every, 1, h), part_of(qkv, every, 2, h), size
            )
        part = dot(ctx[...], proj[...]).astype(bf16)
        for i, k in enumerate(range(0, count, 2)):
            even[i * places : (i + 1) * places] = part[k * places : (k + 1) * places]
            odd[i * places : (i + 1) * places] = part[(k + 1) * places : (k + 2) * places]

    return body


def make_cold(count, places, heads, size):
    def body(qkv, proj, ctx, ask, even, odd):
        rows = qkv.shape[0] // count
        cold = rows - places
        every = slice(None)
        group = min(4, count)
        order = fold_order(range(0, count, 2))
        for first in range(0, count, group):
            at = slice(first * cold, (first + group) * cold)
            for h in range(heads):
                cut = slice(h * LANES, (h + 1) * LANES)
                queries = pieces_of(
                    qkv, first, group, rows, places, rows, slice(3 * h * LANES, (3 * h + 1) * LANES)
                )
                ctx[at, cut], ask[at, cut] = attend(
                    queries, part_of(qkv, every, 1, h), part_of(qkv, every, 2, h), size
                )
            part = dot(ctx[at, :], proj[...]).astype(bf16)
            for k in range(first, first + group):
                to = odd if k % 2 else even
                i = order.index(k // 2 * 2)
                to[i * cold : (i + 1) * cold] = part[(k - first) * cold : (k - first + 1) * cold]

    return body


def back_block(ask, keys, values, ctx, grad_ctx, size):
    shares = jnp.exp2(dot_nt(ask, keys))
    mix = jnp.sum(grad_ctx.astype(f32) * ctx.astype(f32), axis=-1, keepdims=True)
    grad_ctx = with_term(grad_ctx, -mix, size)
    grad_scores = (shares * dot_nt(grad_ctx, values)).astype(bf16)
    return (
        dot(grad_scores, keys),
        dot_tn(ask, grad_scores),
        dot_tn(grad_ctx, shares.astype(bf16)),
    )


def make_cold_back(count, places, heads, size, scale):
    def body(*refs):
        shards, (qkv, proj, ctx, ask) = refs[:count], refs[count : count + 4]
        gq, gk, gv, gp, cots, sems = refs[count + 4 :]
        cold = shards[0].shape[0]
        pull([(shards[k], cots.at[k * cold : (k + 1) * cold]) for k in range(count)], sems)
        every = slice(None)
        group = min(4, count)
        for first in range(0, count, group):
            at = slice(first * cold, (first + group) * cold)
            grad_ctx = dot_nt(cots[at, :], proj[...]).astype(bf16)
            proj_grad = dot_tn(ctx[at, :], cots[at, :])
            for h in range(heads):
                cut = slice(h * LANES, (h + 1) * LANES)
                a, b, c = back_block(
                    ask[at, cut],
                    part_of(qkv, every, 1, h),
                    part_of(qkv, every, 2, h),
                    ctx[at, cut],
                    grad_ctx[:, cut],
                    size,
                )
                gq[at, cut] = (a * scale).astype(bf16)
                if first:
                    gk[cut, :] += b
                    gv[cut, :] += c
                else:
                    gk[cut, :] = b
                    gv[cut, :] = c
            if first:
                gp[...] += proj_grad
            else:
                gp[...] = proj_grad

    return body


def make_hot_back(count, heads, size, groups, scale):
    def body(*refs):
        shards = refs[:count]
        place, qkv, proj, ctx, ask, gq, gk, gv, gp, fn_a, fn_b = refs[count : count + 11]
        outs = refs[count + 11 : count + 15]
        rows_t, grad_q, whole = refs[count + 15 :]
        grads = jnp.concatenate([s[...] for s in shards], axis=0)
        places = shards[0].shape[0]
        rows = qkv.shape[0] // count
        cold = rows - places
        grad_ctx = dot_nt(grads, proj[...]).astype(bf16)
        proj_grad = gp[...] + dot_tn(ctx[...], grads)
        base = heads * 3 * size
        every = slice(None)
        proj_rows = []
        for h in range(heads):
            cut = slice(h * LANES, (h + 1) * LANES)
            a, b, c = back_block(
                ask[:, cut],
                part_of(qkv, every, 1, h),
                part_of(qkv, every, 2, h),
                ctx[:, cut],
                grad_ctx[:, cut],
                size,
            )
            a = (a * scale).astype(bf16)
            for k in range(count):
                grad_q[k * rows : k * rows + places] = a[k * places : (k + 1) * places]
                grad_q[k * rows + places : (k + 1) * rows] = gq[k * cold : (k + 1) * cold, cut]
            at = h * 3 * size
            rows_t[at : at + size, :] = grad_q[...].T[:size]
            rows_t[at + size : at + 2 * size, :] = ((gk[cut, :] + b) * (1.0 / LOG2E))[
                :size
            ].astype(bf16)
            rows_t[at + 2 * size : at + 3 * size, :] = (gv[cut, :] + c)[:size].astype(bf16)
            proj_rows.append(proj_grad[h * LANES : h * LANES + size].astype(bf16))
        done = fn_a.shape[1]
        turned = rows_t[...].T
        whole[:, :base] = (dot(fn_a[...], turned[:done]) + dot(fn_b[...], turned[done:])).astype(
            bf16
        )
        whole[:, base:] = jnp.concatenate(proj_rows, axis=0).T
        each = whole.shape[0] // groups
        cuts = (0, near_rows(each), each)
        for n in range(2):
            size_n = cuts[n + 1] - cuts[n]
            for i, g in enumerate(fold_order(range(groups), n == 1)):
                at = pl.multiple_of((place[0] ^ g) * each + cuts[n], 16)
                to = outs[2 * n + i // (groups // 2)]
                i = i % (groups // 2)
                to[i * size_n : (i + 1) * size_n] = whole[pl.ds(at, size_n), :]

    return body


def near_rows(rows):
    return (rows // 2 + 15) // 16 * 16


def make_last(heads, size):
    def body(a, b, c, d, qkv_o, proj_o):
        total = jnp.concatenate([total_of([a, b]), total_of([c, d])], axis=0)
        base = heads * 3 * size
        turned = total[:, base:].T
        for h in range(heads):
            qkv_o[:, h, :] = total[:, h * 3 * size : (h + 1) * 3 * size]
            proj_o[h] = turned[h * size : (h + 1) * size]

    return body


def make_fold(count):
    def body(mine, theirs, *outs):
        rows = outs[0].shape[0]
        for i in range(count):
            at = slice(i * rows, (i + 1) * rows)
            outs[i][...] = (mine[at].astype(f32) + theirs[at].astype(f32)).astype(bf16)

    return body


def total_of(refs):
    total = refs[0][...].astype(f32)
    for r in refs[1:]:
        total = total + r[...].astype(f32)
    return total


def make_mid(count, groups):
    def body(*refs):
        parts, (tok, link, grads) = refs[:count], refs[count : count + 3]
        mid_o, normal_o, factor_o = refs[count + 3 : count + 6]
        outs = refs[count + 6 :]
        mid = (tok[...].astype(f32) + total_of(parts)).astype(bf16)
        normal, factor = norm_parts(mid)
        mid_o[...] = mid
        normal_o[...] = normal
        factor_o[...] = factor
        slot_in = dot(link[...], normal.astype(bf16))
        each = slot_in.shape[0] // groups
        for g in range(groups):
            at = slice(g * each, (g + 1) * each)
            both = jnp.concatenate([slot_in[at], grads[at].astype(f32)], axis=1)
            outs[g][...] = both.astype(bf16)

    return body


def slot_mask(rows, experts, e):
    row = lax.broadcasted_iota(jnp.int32, (rows, 1), 0)
    return (row // CAP) % experts == e


def make_expert(count, experts):
    def body(*refs):
        shards = refs[:count]
        up, down, arrived, grads, hid_o, pre_o, even, odd = refs[count:]
        width = arrived.shape[1]
        arrived[...] = jnp.concatenate([s[:, :width] for s in shards], axis=0)
        grads[...] = jnp.concatenate([s[:, width:] for s in shards], axis=0)
        rows = arrived.shape[0]
        forth = None
        back = None
        for e in range(experts):
            keep = slot_mask(rows, experts, e)
            pre = dot(arrived[...], up[e])
            cdf = 0.5 * (1.0 + lax.erf(pre * half_root))
            hidden = jnp.where(keep, pre * cdf, 0.0).astype(bf16)
            slope = cdf + pre * jnp.exp(-0.5 * pre * pre) * bell_scale
            grad_pre = jnp.where(keep, dot_nt(grads[...], down[e]) * slope, 0.0).astype(bf16)
            hid_o[e] = hidden
            pre_o[e] = grad_pre
            a = dot(hidden, down[e])
            b = dot_nt(grad_pre, up[e])
            forth = a if forth is None else forth + a
            back = b if back is None else back + b
        both = jnp.concatenate([back, forth], axis=1).astype(bf16)
        each = rows // count
        for k in range(count):
            to = odd if k % 2 else even
            to[(k // 2) * each : (k // 2 + 1) * each] = both[k * each : (k + 1) * each]

    return body


def make_weight_grads(experts):
    def body(arrived, grads, hidden, grad_pre, up_o, down_o):
        for e in range(experts):
            up_o[e] = dot_tn(arrived[...], grad_pre[e]).astype(bf16)
            down_o[e] = dot_tn(hidden[e], grads[...]).astype(bf16)

    return body


def make_split(count, groups):
    def body(*refs):
        parts, outs = refs[:count], refs[count:]
        total = total_of(parts)
        each = total.shape[0] // groups
        for g in range(groups):
            outs[g][...] = total[g * each : (g + 1) * each].astype(bf16)

    return body


def make_mid_back(groups):
    def body(*refs):
        parts = refs[:groups]
        link, cot, normal, factor, grad_o, expert_o = refs[groups:]
        both = jnp.concatenate([p[...].astype(f32) for p in parts], axis=0).astype(bf16)
        width = cot.shape[1]
        expert_o[...] = both[:, width:]
        grad_norm = dot_tn(link[...], both[:, :width])
        grad_o[...] = (
            cot[...].astype(f32) + norm_back(normal[...], factor[...], grad_norm)
        ).astype(bf16)

    return body


def make_epilogue(count):
    def body(*refs):
        parts = refs[:count]
        tok, mid_hot, perm, pick0, pick1, experts, gate_t, cot, out, gate_o = refs[count:]
        cold = (tok[...].astype(f32) + total_of(parts)).astype(bf16)
        ordered = jnp.concatenate([mid_hot[...], cold], axis=0)
        mid = dot(perm[...], ordered)
        gate = jnp.concatenate([gate_t[...], jnp.zeros((6, gate_t.shape[1]), f32)], axis=0).T
        first = dot(pick0[...], experts[...])
        second = dot(pick1[...], experts[...])
        out[...] = (mid + gate[:, 0:1] * first + gate[:, 1:2] * second).astype(bf16)
        upstream = cot[...].astype(f32)
        lane = lax.broadcasted_iota(jnp.int32, (upstream.shape[0], LANES), 1)
        one = jnp.sum(upstream * first, axis=-1, keepdims=True)
        two = jnp.sum(upstream * second, axis=-1, keepdims=True)
        gate_o[...] = jnp.where(lane == 0, one, two).T[:2]

    return body


def fold_scatter(even, odd, rows, name):
    count = lax.axis_size("tensor") // 2
    theirs = hop(odd, "tensor", 1)
    sums = run(
        make_fold(count), [shape((rows, even.shape[1]))] * count, [even, theirs], name
    )
    return [sums[0]] + [hop(sums[i], "tensor", 2 * i) for i in range(1, count)]


def halve(mine, theirs, name):
    half = (mine.shape[0] // 2, mine.shape[1])
    return run(make_fold(2), [shape(half), shape(half)], [mine, theirs], name)


def shards(
    tokens,
    cotangent,
    gate_weights,
    routes,
    slot_index,
    qkv_weight,
    proj_weight,
    up_weight,
    down_weight,
):
    rows, width = tokens.shape
    heads, size = qkv_weight.shape[1], qkv_weight.shape[2] // 3
    scale = size ** (-0.5)
    groups = lax.axis_size("dp")
    count = lax.axis_size("tensor")
    experts, _, hidden_dev = up_weight.shape
    each = experts * CAP
    places = groups * each
    cold = rows - places
    hot_all = count * places
    total = count * rows
    slots = count * places

    wqkv, proj = run(
        make_prep(heads, size),
        [shape((heads * 3 * LANES, width)), shape((heads * LANES, width))],
        [qkv_weight.transpose(1, 2, 0), proj_weight],
        "prep",
    )
    group = (lax.axis_index("dp") * experts).astype(jnp.int32).reshape(1)
    normed, cot, tok, perm, pick0, pick1, link, grad_out = run(
        prologue_body,
        [
            shape((rows, width)),
            shape((rows, width)),
            shape((rows, width)),
            shape((rows, rows)),
            shape((rows, places)),
            shape((rows, places)),
            shape((places, places)),
            shape((places, width)),
        ],
        [tokens, cotangent, group, gate_weights.T, routes.T, slot_index.T],
        "prologue",
        extra=4,
        smem=(2,),
        loose=2,
        scratch=[
            pltpu.VMEM((rows, width), bf16),
            pltpu.VMEM((rows, width), bf16),
            pltpu.SemaphoreType.DMA((4,)),
        ],
    )
    half = count // 2
    cot_cold = cot[places:]
    cots = {0: cot_cold}
    mask = 2
    while mask < half:
        cots.update({k ^ mask: hop(y, "tensor", mask) for k, y in list(cots.items())})
        mask *= 2
    near_cots = list(cots.values())

    def first_half(have):
        near = [
            hop(have[k - 1], "tensor", 1) if k % 2 else have[k] for k in range(half)
        ]
        return run(
            make_half(half, heads, size, scale),
            [shape((half * rows, heads * 3 * LANES)), shape((width, half * rows))],
            after(near, near_cots) + [wqkv],
            "half",
        extra=6,
            loose=half,
            scratch=[
                pltpu.VMEM((half * rows, width), bf16),
                pltpu.SemaphoreType.DMA((half,)),
            ],
        )

    box = []

    def hold(have):
        box.append((have, first_half(have)))
        return box[0][1]

    normed_all = gather_rel(normed, hold)
    have, (qkv_a, fn_a) = box[0]

    far = count // 2
    qkv, ctx_hot, ask_hot, even, odd = run(
        make_front(count, places, heads, size, scale),
        [
            shape((total, heads * 3 * LANES)),
            shape((hot_all, heads * LANES)),
            shape((hot_all, heads * LANES)),
            shape((hot_all // 2, width)),
            shape((hot_all // 2, width)),
        ],
        normed_all[half:] + [qkv_a, wqkv, proj],
        "front",
        extra=8,
        loose=half,
        scratch=[
            pltpu.VMEM((half * rows, width), bf16),
            pltpu.SemaphoreType.DMA((half,)),
        ],
    )
    cots[far] = hop(after(cot_cold, have[far]), "tensor", far)
    odd = after(odd, cots[far])
    hot_sums = fold_scatter(even, odd, places, "fold_hot")

    outs = run(
        make_mid(count // 2, groups),
        [shape((places, width)), shape((places, width), f32), shape((places, 1), f32)]
        + [shape((each, 2 * width))] * groups,
        hot_sums + [tok[:places], link, grad_out],
        "mid_hot",
    )
    mid_hot, normal_hot, factor_hot = outs[:3]
    pieces = outs[3:]

    ctx_cold, ask_cold, even_cold, odd_cold = run(
        make_cold(count, places, heads, size),
        [
            shape((count * cold, heads * LANES)),
            shape((count * cold, heads * LANES)),
            shape((count * cold // 2, width)),
            shape((count * cold // 2, width)),
        ],
        [after(qkv, mid_hot), proj],
        "cold",
        extra=14,
        flops=4 * total * total * heads * LANES,
    )
    start = after(cots[far], mid_hot)
    rest = {far: start}
    mask = 2
    while mask < far:
        rest.update({k ^ mask: hop(y, "tensor", mask) for k, y in list(rest.items())})
        mask *= 2
    cots.update(rest)
    landed = jnp.concatenate(
        [pieces[0]] + [hop(pieces[g], "dp", g) for g in range(1, groups)], axis=0
    )
    cold_theirs = hop(after(odd_cold, ctx_cold), "tensor", 1)
    landed = after(landed, ctx_cold, list(cots.values()))
    arrived_all = gather_rel(landed)
    arrived, slot_grads, hidden, grad_pre, even, odd = run(
        make_expert(count, experts),
        [
            shape((slots, width)),
            shape((slots, width)),
            shape((experts, slots, hidden_dev)),
            shape((experts, slots, hidden_dev)),
            shape((slots // 2, 2 * width)),
            shape((slots // 2, 2 * width)),
        ],
        arrived_all + [up_weight, down_weight],
        "experts",
        extra=8,
        flops=6 * slots * width * hidden_dev * experts,
    )
    sums = fold_scatter(even, odd, places, "fold_slots")

    pieces = run(
        make_split(count // 2, groups),
        [shape((each, 2 * width))] * groups,
        sums,
        "split_slots",
    )
    cot_all = [hop(cots[k - 1], "tensor", 1) if k % 2 else cots[k] for k in range(count)]
    cold_mine, cold_send = halve(after(even_cold, hidden), cold_theirs, "fold_cold_1")
    pieces = after(pieces, cold_mine)
    back = [pieces[0]] + [hop(pieces[g], "dp", g) for g in range(1, groups)]
    cold_theirs = hop(after(cold_send, pieces[0]), "tensor", 2)
    gq, gk, gv, gp = run(
        make_cold_back(count, places, heads, size, scale),
        [
            shape((count * cold, heads * LANES)),
            shape((heads * LANES, total), f32),
            shape((heads * LANES, total), f32),
            shape((heads * LANES, width), f32),
        ],
        cot_all + [after(qkv, pieces[0]), proj, ctx_cold, ask_cold],
        "cold_back",
        extra=16,
        flops=10 * total * total * heads * LANES,
        loose=count,
        scratch=[
            pltpu.VMEM((count * cold, width), bf16),
            pltpu.SemaphoreType.DMA((count,)),
        ],
    )
    back = after(back, gp, cold_theirs)
    grad_hot, expert_out = run(
        make_mid_back(groups),
        [shape((places, width)), shape((places, width))],
        back + [link, cot[:places], normal_hot, factor_hot],
        "mid_back",
    )
    box.clear()

    def turn(_):
        box.append(
            run(
                make_turn(half),
                [shape((width, half * rows))],
                after(normed_all[half:], grad_hot),
                "turn",
        extra=3,
            )[0]
        )
        return box[0]

    grad_hot_all = gather_rel(grad_hot, turn)
    fn_b = box[0]
    mask = 4
    cold_mine = after(cold_mine, grad_hot)
    while mask < count:
        cold_mine, cold_send = halve(cold_mine, cold_theirs, f"fold_cold_{mask // 2}")
        cold_theirs = hop(cold_send, "tensor", mask)
        mask *= 2
    cold_sums = [cold_mine, cold_theirs]

    me = lax.axis_index("dp").astype(jnp.int32).reshape(1)
    each_w = width // groups
    first_w = near_rows(each_w)
    halves = [(groups // 2 * n, heads * 4 * size) for n in (first_w, each_w - first_w)]
    keep_a, send_a, keep_b, send_b = run(
        make_hot_back(count, heads, size, groups, scale),
        [shape(halves[0]), shape(halves[0]), shape(halves[1]), shape(halves[1])],
        after(grad_hot_all, cold_mine)
        + [me, qkv, proj, ctx_hot, ask_hot, gq, gk, gv, gp, fn_a, fn_b],
        "hot_back",
        extra=10,
        smem=(count,),
        scratch=[
            pltpu.VMEM((heads * 3 * size, total), bf16),
            pltpu.VMEM((total, LANES), bf16),
            pltpu.VMEM((width, heads * 4 * size), bf16),
        ],
    )
    grad_up, grad_down = run(
        make_weight_grads(experts),
        [shape(up_weight.shape), shape(down_weight.shape)],
        [after(arrived, keep_a), slot_grads, hidden, grad_pre],
        "weight_grads",
        extra=10,
    )
    mask = 1
    while True:
        got_a = hop(send_a, "dp", mask)
        got_b = hop(send_b, "dp", groups // 2 // mask)
        if mask == groups // 2:
            break
        keep_a, send_a = halve(keep_a, got_a, f"fold_a_{mask}")
        keep_b, send_b = halve(keep_b, got_b, f"fold_b_{mask}")
        mask *= 2
    parts = [keep_a, got_a, keep_b, got_b]
    layer_out, gate_grad = run(
        make_epilogue(2),
        [shape((rows, width)), shape((2, rows), f32)],
        cold_sums
        + [tok[places:], mid_hot, perm, pick0, pick1, expert_out, gate_weights.T, cotangent],
        "epilogue",
        extra=4,
    )
    grad_qkv, grad_proj = run(
        make_last(heads, size),
        [shape((width // groups, heads, 3 * size), f32), shape((heads, size, width // groups), f32)],
        after(parts, layer_out, grad_up),
        "last",
        extra=6,
    )
    return (layer_out, gate_grad.T, grad_qkv, grad_proj, grad_up, grad_down)


def solution(mesh):
    return jax.shard_map(
        shards,
        mesh=mesh,
        in_specs=(
            P(("dp", "tensor"), None),
            P(("dp", "tensor"), None),
            P(("dp", "tensor"), None),
            P(("dp", "tensor"), None),
            P(("dp", "tensor"), None),
            P(None, "tensor", None),
            P("tensor", None, None),
            P("dp", None, "tensor"),
            P("dp", "tensor", None),
        ),
        out_specs=(
            P(("dp", "tensor"), None),
            P(("dp", "tensor"), None),
            P("dp", "tensor", None),
            P("tensor", None, "dp"),
            P("dp", None, "tensor"),
            P("dp", "tensor", None),
        ),
        check_vma=False,
    )
```

```python
import math

import jax
import jax.numpy as jnp
from jax import lax
from jax.experimental import pallas as pl
from jax.experimental.pallas import tpu as pltpu
from jax.sharding import PartitionSpec as P

CAP = 2
LANES = 128
epsilon = 1e-06
half_root = 1.0 / math.sqrt(2.0)
bell_scale = 1.0 / math.sqrt(2.0 * math.pi)
LOG2E = math.log2(math.e)
f32 = jnp.float32
bf16 = jnp.bfloat16


def norm_parts(row_block):
    widened = row_block.astype(f32)
    center = widened - jnp.mean(widened, axis=-1, keepdims=True)
    factor = lax.rsqrt(jnp.mean(center * center, axis=-1, keepdims=True) + epsilon)
    return (center * factor, factor)


def norm_back(normal_rows, factor, upstream):
    mean_up = jnp.mean(upstream, axis=-1, keepdims=True)
    mean_mix = jnp.mean(upstream * normal_rows, axis=-1, keepdims=True)
    return factor * (upstream - mean_up - normal_rows * mean_mix)


def dot(a, b):
    return lax.dot_general(a, b, (((1,), (0,)), ((), ())), preferred_element_type=f32)


def dot_nt(a, b):
    return lax.dot_general(a, b, (((1,), (1,)), ((), ())), preferred_element_type=f32)


def dot_tn(a, b):
    return lax.dot_general(a, b, (((0,), (0,)), ((), ())), preferred_element_type=f32)


def run(body, outs, ins, name, flops=0, extra=1, moved=None, smem=(), loose=0, scratch=()):
    specs = [
        pl.BlockSpec(
            memory_space=pl.ANY if i < loose else pltpu.SMEM if i in smem else pltpu.VMEM
        )
        for i in range(len(ins))
    ]
    sizes = [math.prod(x.shape) * x.dtype.itemsize for x in list(ins)[loose:] + list(outs)]
    sizes += [math.prod(x.shape) * x.dtype.itemsize for x in scratch if x.dtype in (f32, bf16)]
    limit = int(sum(sizes) * 1.2) + extra * 2**20
    return pl.pallas_call(
        body,
        out_shape=list(outs),
        in_specs=specs,
        out_specs=[pl.BlockSpec(memory_space=pltpu.VMEM)] * len(outs),
        scratch_shapes=list(scratch),
        compiler_params=pltpu.CompilerParams(vmem_limit_bytes=limit),
        cost_estimate=pl.CostEstimate(
            flops=int(flops), bytes_accessed=int(sum(sizes) if moved is None else moved), transcendentals=0
        ),
        name=name,
    )(*ins)


def after(x, *others):
    return lax.optimization_barrier((x, others))[0]


def pull(pairs, sems):
    copies = [pltpu.make_async_copy(a, b, sems.at[i]) for i, (a, b) in enumerate(pairs)]
    for c in copies:
        c.start()
    for c in copies:
        c.wait()


def shape(dims, dtype=bf16):
    return jax.ShapeDtypeStruct(tuple(dims), dtype)


def block_of(rows, most=256):
    return max(b for b in range(16, most + 1, 16) if rows % b == 0)


def hop(x, axis, mask):
    size = lax.axis_size(axis)
    return lax.ppermute(x, axis, [(i, i ^ mask) for i in range(size)])


def gather_rel(x, hold=None, firm=()):
    size = lax.axis_size("tensor")
    have = {0: x}
    odd = {}
    mask = size // 2
    while mask > 1:
        have.update({k ^ mask: hop(y, "tensor", mask) for k, y in list(have.items())})
        mask //= 2
    if hold is not None:
        held = hold(have)
        last = size - 2
        have[last] = after(have[last], held)
    return [hop(have[k - 1], "tensor", 1) if k % 2 else have[k] for k in range(size)]


def fold_order(keys, flip=False):
    bits = range(7, -1, -1) if flip else range(8)
    return sorted(keys, key=lambda k: tuple((k >> b) & 1 for b in bits))


def prologue_body(tok_in, cot_in, group, gate_t, routes_t, slots_t, *outs):
    normed_o, cot_hot_o, cot_cold_o, tok_hot_o, tok_cold_o, perm_o, pick0_o, pick1_o, link_o, gout_o, tok, cot, sems = outs
    half = tok.shape[0] // 2
    pairs = [(tok_in, tok), (cot_in, cot)]
    copies = [
        pltpu.make_async_copy(
            a.at[i * half : (i + 1) * half], b.at[i * half : (i + 1) * half], sems.at[2 * n + i]
        )
        for n, (a, b) in enumerate(pairs)
        for i in range(2)
    ]
    for c in copies:
        c.start()
    rows = tok.shape[0]
    places = pick0_o.shape[1]
    code_t = jnp.where(slots_t[...] >= 0, (routes_t[...] ^ group[0]) * CAP + slots_t[...], -1)
    packed = jnp.concatenate(
        [code_t.astype(f32), gate_t[...], jnp.zeros((4, rows), f32)], axis=0
    ).T
    code = packed[:, 0:2].astype(jnp.int32)
    gate = packed[:, 2:4]
    lane = lax.broadcasted_iota(jnp.int32, (rows, LANES), 1)
    wide0 = (code[:, 0:1] == lane).astype(f32)
    wide1 = (code[:, 1:2] == lane).astype(f32)
    kept0 = (code[:, 0:1] >= 0).astype(f32)
    prim = wide0 + wide1 * (1.0 - kept0)
    plain = 1.0 - jnp.sum(prim, axis=1, keepdims=True)
    open_at = 1.0 - jnp.sum(prim, axis=0, keepdims=True)
    ri = lax.broadcasted_iota(jnp.int32, (rows, rows), 0)
    ci = lax.broadcasted_iota(jnp.int32, (rows, rows), 1)
    row_rank = dot(
        (ci < ri).astype(bf16), jnp.broadcast_to(plain, (rows, rows)).astype(bf16)
    )
    place_rank = dot(
        jnp.broadcast_to(open_at, (rows, rows)).astype(bf16), (ri < ci).astype(bf16)
    )
    filler = plain * open_at * (row_rank == place_rank).astype(f32)
    perm = (prim + filler).astype(bf16)
    perm_o[...] = perm
    for c in copies:
        c.wait()
    normal, _ = norm_parts(tok[...])
    normed_o[...] = dot_tn(perm, normal.astype(bf16)).astype(bf16)
    for source, hot_o, cold_o in ((cot, cot_hot_o, cot_cold_o), (tok, tok_hot_o, tok_cold_o)):
        moved = dot_tn(perm, source[...]).astype(bf16)
        hot_o[...] = moved[:places]
        cold_o[...] = moved[places:]
    pick0 = wide0.astype(bf16)
    pick1 = wide1.astype(bf16)
    pick0_o[...] = pick0[:, :places]
    pick1_o[...] = pick1[:, :places]
    link_o[...] = dot_tn((pick0 + pick1), prim.astype(bf16))[:places, :places].astype(bf16)
    upstream = cot[...].astype(f32)
    g0 = (gate[:, 0:1] * upstream).astype(bf16)
    g1 = (gate[:, 1:2] * upstream).astype(bf16)
    gout_o[...] = (dot_tn(pick0, g0) + dot_tn(pick1, g1))[:places].astype(bf16)


def make_prep(heads, size):
    def body(w, p, wo, po):
        wo[...] = jnp.zeros_like(wo)
        po[...] = jnp.zeros_like(po)
        for h in range(heads):
            for i in range(3):
                at = (3 * h + i) * LANES
                wo[at : at + size] = w[h, i * size : (i + 1) * size]
            po[h * LANES : h * LANES + size] = p[h]

    return body


def spare_lanes(dims, size):
    lane = lax.broadcasted_iota(jnp.int32, dims, 1) % LANES
    return (lane >= size) & (lane < size + 3)


def with_term(rows, term, size):
    lane = lax.broadcasted_iota(jnp.int32, rows.shape, 1)
    first = term.astype(bf16).astype(f32)
    second = (term - first).astype(bf16).astype(f32)
    third = term - first - second
    term = jnp.where(lane == size, first, jnp.where(lane == size + 1, second, third))
    return jnp.where(spare_lanes(rows.shape, size), term, rows.astype(f32)).astype(bf16)


def project(rows, weights, heads, size, scale):
    raw = dot_nt(rows, weights)
    part = lax.broadcasted_iota(jnp.int32, raw.shape, 1) // LANES % 3
    factor = jnp.where(part == 0, scale * LOG2E, 1.0)
    ones = ((part != 0) & spare_lanes(raw.shape, size)).astype(f32)
    return (raw * factor + ones).astype(bf16)


def attend(queries, keys, values, size):
    raised = jnp.exp2(dot_nt(queries, keys))
    total = jnp.sum(raised, axis=-1, keepdims=True)
    shares = raised * (1.0 / total)
    return dot(shares.astype(bf16), values).astype(bf16), with_term(queries, -jnp.log2(total), size)


def part_of(ref, rows, which, head):
    at = (3 * head + which) * LANES
    return ref[rows, at : at + LANES]


def pieces_of(ref, first, count, every, lo, hi, at):
    return jnp.concatenate(
        [ref[(first + k) * every + lo : (first + k) * every + hi, at] for k in range(count)], axis=0
    )


def make_half(count, heads, size, scale):
    def body(*refs):
        shards, (weights, qkv, fn_t, fn, sems) = refs[:count], refs[count:]
        rows = shards[0].shape[0]
        pull([(shards[k], fn.at[k * rows : (k + 1) * rows]) for k in range(count)], sems)
        for k in range(count):
            at = slice(k * rows, (k + 1) * rows)
            fn_t[:, at] = fn[at, :].T
        step = block_of(fn.shape[0])

        def chunk(i, _):
            at = pl.ds(pl.multiple_of(i * step, 16), step)
            qkv[at, :] = project(fn[at, :], weights[...], heads, size, scale)
            return 0

        lax.fori_loop(0, fn.shape[0] // step, chunk, 0)

    return body


def make_turn(count):
    def body(*refs):
        shards, fn_t = refs[:count], refs[count]
        rows = shards[0].shape[0]
        for k in range(count):
            fn_t[:, k * rows : (k + 1) * rows] = shards[k][...].T

    return body


def make_front(count, places, heads, size, scale):
    def body(*refs):
        half = count // 2
        shards, (first, weights, proj) = refs[:half], refs[half : half + 3]
        qkv, ctx, ask, even, odd, fn, sems = refs[half + 3 :]
        rows = shards[0].shape[0]
        pull([(shards[k], fn.at[k * rows : (k + 1) * rows]) for k in range(half)], sems)
        done = first.shape[0]
        qkv[:done] = first[...]
        step = block_of(fn.shape[0])

        def chunk(i, _):
            at = pl.ds(pl.multiple_of(i * step, 16), step)
            to = pl.ds(pl.multiple_of(done + i * step, 16), step)
            qkv[to, :] = project(fn[at, :], weights[...], heads, size, scale)
            return 0

        lax.fori_loop(0, fn.shape[0] // step, chunk, 0)
        every = slice(None)
        for h in range(heads):
            cut = slice(h * LANES, (h + 1) * LANES)
            queries = pieces_of(
                qkv, 0, count, rows, 0, places, slice(3 * h * LANES, (3 * h + 1) * LANES)
            )
            ctx[:, cut], ask[:, cut] = attend(
                queries, part_of(qkv, every, 1, h), part_of(qkv, every, 2, h), size
            )
        part = dot(ctx[...], proj[...]).astype(bf16)
        for i, k in enumerate(range(0, count, 2)):
            even[i * places : (i + 1) * places] = part[k * places : (k + 1) * places]
            odd[i * places : (i + 1) * places] = part[(k + 1) * places : (k + 2) * places]

    return body


def make_cold(count, places, heads, size):
    def body(qkv, proj, ctx, ask, even_a, odd_a, even_b, odd_b):
        rows = qkv.shape[0] // count
        cold = rows - places
        upper = upper_rows(cold)
        every = slice(None)
        group = min(4, count)
        order = fold_order(range(0, count, 2))
        for first in range(0, count, group):
            at = slice(first * cold, (first + group) * cold)
            for h in range(heads):
                cut = slice(h * LANES, (h + 1) * LANES)
                queries = pieces_of(
                    qkv, first, group, rows, places, rows, slice(3 * h * LANES, (3 * h + 1) * LANES)
                )
                ctx[at, cut], ask[at, cut] = attend(
                    queries, part_of(qkv, every, 1, h), part_of(qkv, every, 2, h), size
                )
            part = dot(ctx[at, :], proj[...]).astype(bf16)
            for k in range(first, first + group):
                one = part[(k - first) * cold : (k - first + 1) * cold]
                i = order.index(k // 2 * 2)
                to = odd_a if k % 2 else even_a
                to[i * upper : (i + 1) * upper] = one[:upper]
                to = odd_b if k % 2 else even_b
                to[i * (cold - upper) : (i + 1) * (cold - upper)] = one[upper:]

    return body


def back_block(ask, keys, values, ctx, grad_ctx, size):
    shares = jnp.exp2(dot_nt(ask, keys))
    mix = jnp.sum(grad_ctx.astype(f32) * ctx.astype(f32), axis=-1, keepdims=True)
    grad_ctx = with_term(grad_ctx, -mix, size)
    grad_scores = (shares * dot_nt(grad_ctx, values)).astype(bf16)
    return (
        dot(grad_scores, keys),
        dot_tn(ask, grad_scores),
        dot_tn(grad_ctx, shares.astype(bf16)),
    )


def make_cold_back(count, places, heads, size, scale):
    def body(*refs):
        shards, (qkv, proj, ctx, ask) = refs[:count], refs[count : count + 4]
        gq, gk, gv, gp, cots, sems = refs[count + 4 :]
        cold = shards[0].shape[0]
        pull([(shards[k], cots.at[k * cold : (k + 1) * cold]) for k in range(count)], sems)
        every = slice(None)
        group = min(4, count)
        for first in range(0, count, group):
            at = slice(first * cold, (first + group) * cold)
            grad_ctx = dot_nt(cots[at, :], proj[...]).astype(bf16)
            proj_grad = dot_tn(ctx[at, :], cots[at, :])
            for h in range(heads):
                cut = slice(h * LANES, (h + 1) * LANES)
                a, b, c = back_block(
                    ask[at, cut],
                    part_of(qkv, every, 1, h),
                    part_of(qkv, every, 2, h),
                    ctx[at, cut],
                    grad_ctx[:, cut],
                    size,
                )
                gq[at, cut] = (a * scale).astype(bf16)
                if first:
                    gk[cut, :] += b
                    gv[cut, :] += c
                else:
                    gk[cut, :] = b
                    gv[cut, :] = c
            if first:
                gp[...] += proj_grad
            else:
                gp[...] = proj_grad

    return body


def make_hot_back(count, heads, size, groups, scale):
    def body(*refs):
        shards = refs[:count]
        place, qkv, proj, ctx, ask, gq, gk, gv, gp, fn_a, fn_b = refs[count : count + 11]
        outs = refs[count + 11 : count + 15]
        rows_t, grad_q, whole = refs[count + 15 :]
        grads = jnp.concatenate([s[...] for s in shards], axis=0)
        places = shards[0].shape[0]
        rows = qkv.shape[0] // count
        cold = rows - places
        grad_ctx = dot_nt(grads, proj[...]).astype(bf16)
        proj_grad = gp[...] + dot_tn(ctx[...], grads)
        base = heads * 3 * size
        every = slice(None)
        proj_rows = []
        for h in range(heads):
            cut = slice(h * LANES, (h + 1) * LANES)
            a, b, c = back_block(
                ask[:, cut],
                part_of(qkv, every, 1, h),
                part_of(qkv, every, 2, h),
                ctx[:, cut],
                grad_ctx[:, cut],
                size,
            )
            a = (a * scale).astype(bf16)
            for k in range(count):
                grad_q[k * rows : k * rows + places] = a[k * places : (k + 1) * places]
                grad_q[k * rows + places : (k + 1) * rows] = gq[k * cold : (k + 1) * cold, cut]
            at = h * 3 * size
            rows_t[at : at + size, :] = grad_q[...].T[:size]
            rows_t[at + size : at + 2 * size, :] = ((gk[cut, :] + b) * (1.0 / LOG2E))[
                :size
            ].astype(bf16)
            rows_t[at + 2 * size : at + 3 * size, :] = (gv[cut, :] + c)[:size].astype(bf16)
            proj_rows.append(proj_grad[h * LANES : h * LANES + size].astype(bf16))
        done = fn_a.shape[1]
        turned = rows_t[...].T
        whole[:, :base] = (dot(fn_a[...], turned[:done]) + dot(fn_b[...], turned[done:])).astype(
            bf16
        )
        whole[:, base:] = jnp.concatenate(proj_rows, axis=0).T
        each = whole.shape[0] // groups
        cuts = (0, near_rows(each), each)
        for n in range(2):
            size_n = cuts[n + 1] - cuts[n]
            for i, g in enumerate(fold_order(range(groups), n == 1)):
                at = pl.multiple_of((place[0] ^ g) * each + cuts[n], 16)
                to = outs[2 * n + i // (groups // 2)]
                i = i % (groups // 2)
                to[i * size_n : (i + 1) * size_n] = whole[pl.ds(at, size_n), :]

    return body


def upper_rows(rows):
    return (rows * 5 // 7 + 15) // 16 * 16


def near_rows(rows):
    return (rows // 2 + 15) // 16 * 16


def make_last(heads, size):
    def body(a, b, c, d, qkv_o, proj_o):
        total = jnp.concatenate([total_of([a, b]), total_of([c, d])], axis=0)
        base = heads * 3 * size
        turned = total[:, base:].T
        for h in range(heads):
            qkv_o[:, h, :] = total[:, h * 3 * size : (h + 1) * 3 * size]
            proj_o[h] = turned[h * size : (h + 1) * size]

    return body


def make_fold(count):
    def body(mine, theirs, *outs):
        rows = outs[0].shape[0]
        for i in range(count):
            at = slice(i * rows, (i + 1) * rows)
            outs[i][...] = (mine[at].astype(f32) + theirs[at].astype(f32)).astype(bf16)

    return body


def total_of(refs):
    total = refs[0][...].astype(f32)
    for r in refs[1:]:
        total = total + r[...].astype(f32)
    return total


def make_mid(count, groups):
    def body(*refs):
        parts, (tok, link, grads) = refs[:count], refs[count : count + 3]
        mid_o, normal_o, factor_o = refs[count + 3 : count + 6]
        outs = refs[count + 6 :]
        mid = (tok[...].astype(f32) + total_of(parts)).astype(bf16)
        normal, factor = norm_parts(mid)
        mid_o[...] = mid
        normal_o[...] = normal
        factor_o[...] = factor
        slot_in = dot(link[...], normal.astype(bf16))
        each = slot_in.shape[0] // groups
        for g in range(groups):
            at = slice(g * each, (g + 1) * each)
            both = jnp.concatenate([slot_in[at], grads[at].astype(f32)], axis=1)
            outs[g][...] = both.astype(bf16)

    return body


def slot_mask(rows, experts, e):
    row = lax.broadcasted_iota(jnp.int32, (rows, 1), 0)
    return (row // CAP) % experts == e


def make_expert(count, experts):
    def body(*refs):
        shards = refs[:count]
        up, down, arrived, grads, hid_o, pre_o, even, odd = refs[count:]
        width = arrived.shape[1]
        arrived[...] = jnp.concatenate([s[:, :width] for s in shards], axis=0)
        grads[...] = jnp.concatenate([s[:, width:] for s in shards], axis=0)
        rows = arrived.shape[0]
        forth = None
        back = None
        for e in range(experts):
            keep = slot_mask(rows, experts, e)
            pre = dot(arrived[...], up[e])
            cdf = 0.5 * (1.0 + lax.erf(pre * half_root))
            hidden = jnp.where(keep, pre * cdf, 0.0).astype(bf16)
            slope = cdf + pre * jnp.exp(-0.5 * pre * pre) * bell_scale
            grad_pre = jnp.where(keep, dot_nt(grads[...], down[e]) * slope, 0.0).astype(bf16)
            hid_o[e] = hidden
            pre_o[e] = grad_pre
            a = dot(hidden, down[e])
            b = dot_nt(grad_pre, up[e])
            forth = a if forth is None else forth + a
            back = b if back is None else back + b
        both = jnp.concatenate([back, forth], axis=1).astype(bf16)
        each = rows // count
        for k in range(count):
            to = odd if k % 2 else even
            to[(k // 2) * each : (k // 2 + 1) * each] = both[k * each : (k + 1) * each]

    return body


def make_weight_grads(experts):
    def body(arrived, grads, hidden, grad_pre, up_o, down_o):
        for e in range(experts):
            up_o[e] = dot_tn(arrived[...], grad_pre[e]).astype(bf16)
            down_o[e] = dot_tn(hidden[e], grads[...]).astype(bf16)

    return body


def make_split(count, groups):
    def body(*refs):
        parts, outs = refs[:count], refs[count:]
        total = total_of(parts)
        each = total.shape[0] // groups
        for g in range(groups):
            outs[g][...] = total[g * each : (g + 1) * each].astype(bf16)

    return body


def make_mid_back(groups):
    def body(*refs):
        parts = refs[:groups]
        link, cot, normal, factor, grad_o, expert_o = refs[groups:]
        both = jnp.concatenate([p[...].astype(f32) for p in parts], axis=0).astype(bf16)
        width = cot.shape[1]
        expert_o[...] = both[:, width:]
        grad_norm = dot_tn(link[...], both[:, :width])
        grad_o[...] = (
            cot[...].astype(f32) + norm_back(normal[...], factor[...], grad_norm)
        ).astype(bf16)

    return body


def make_epilogue():
    def body(*refs):
        parts = refs[:4]
        tok, mid_hot, perm, pick0, pick1, experts, gate_t, cot, out, gate_o = refs[4:]
        sums = jnp.concatenate([total_of(parts[:2]), total_of(parts[2:])], axis=0)
        cold = (tok[...].astype(f32) + sums).astype(bf16)
        ordered = jnp.concatenate([mid_hot[...], cold], axis=0)
        mid = dot(perm[...], ordered)
        gate = jnp.concatenate([gate_t[...], jnp.zeros((6, gate_t.shape[1]), f32)], axis=0).T
        first = dot(pick0[...], experts[...])
        second = dot(pick1[...], experts[...])
        out[...] = (mid + gate[:, 0:1] * first + gate[:, 1:2] * second).astype(bf16)
        upstream = cot[...].astype(f32)
        lane = lax.broadcasted_iota(jnp.int32, (upstream.shape[0], LANES), 1)
        one = jnp.sum(upstream * first, axis=-1, keepdims=True)
        two = jnp.sum(upstream * second, axis=-1, keepdims=True)
        gate_o[...] = jnp.where(lane == 0, one, two).T[:2]

    return body


def fold_scatter(even, odd, rows, name):
    count = lax.axis_size("tensor") // 2
    theirs = hop(odd, "tensor", 1)
    sums = run(
        make_fold(count), [shape((rows, even.shape[1]))] * count, [even, theirs], name
    )
    return [sums[0]] + [hop(sums[i], "tensor", 2 * i) for i in range(1, count)]


def halve(mine, theirs, name):
    half = (mine.shape[0] // 2, mine.shape[1])
    return run(make_fold(2), [shape(half), shape(half)], [mine, theirs], name)


def shards(
    tokens,
    cotangent,
    gate_weights,
    routes,
    slot_index,
    qkv_weight,
    proj_weight,
    up_weight,
    down_weight,
):
    rows, width = tokens.shape
    heads, size = qkv_weight.shape[1], qkv_weight.shape[2] // 3
    scale = size ** (-0.5)
    groups = lax.axis_size("dp")
    count = lax.axis_size("tensor")
    experts, _, hidden_dev = up_weight.shape
    each = experts * CAP
    places = groups * each
    cold = rows - places
    hot_all = count * places
    total = count * rows
    slots = count * places

    wqkv, proj = run(
        make_prep(heads, size),
        [shape((heads * 3 * LANES, width)), shape((heads * LANES, width))],
        [qkv_weight.transpose(1, 2, 0), proj_weight],
        "prep",
    )
    group = (lax.axis_index("dp") * experts).astype(jnp.int32).reshape(1)
    normed, cot_hot, cot_cold, tok_hot, tok_cold, perm, pick0, pick1, link, grad_out = run(
        prologue_body,
        [
            shape((rows, width)),
            shape((places, width)),
            shape((cold, width)),
            shape((places, width)),
            shape((cold, width)),
            shape((rows, rows)),
            shape((rows, places)),
            shape((rows, places)),
            shape((places, places)),
            shape((places, width)),
        ],
        [tokens, cotangent, group, gate_weights.T, routes.T, slot_index.T],
        "prologue",
        extra=57,
        smem=(2,),
        loose=2,
        scratch=[
            pltpu.VMEM((rows, width), bf16),
            pltpu.VMEM((rows, width), bf16),
            pltpu.SemaphoreType.DMA((4,)),
        ],
    )
    half = count // 2
    cots = {0: cot_cold, 1: hop(cot_cold, "tensor", 1)}
    def first_half(have):
        near = [
            hop(have[k - 1], "tensor", 1) if k % 2 else have[k] for k in range(half)
        ]
        return run(
            make_half(half, heads, size, scale),
            [shape((half * rows, heads * 3 * LANES)), shape((width, half * rows))],
            after(near, cots[1]) + [wqkv],
            "half",
        extra=6,
        moved=1024,
            loose=half,
            scratch=[
                pltpu.VMEM((half * rows, width), bf16),
                pltpu.SemaphoreType.DMA((half,)),
            ],
        )

    box = []

    def hold(have):
        box.append((have, first_half(have)))
        return box[0][1]

    normed_all = gather_rel(normed, hold)
    have, (qkv_a, fn_a) = box[0]

    far = count // 2
    qkv, ctx_hot, ask_hot, even, odd = run(
        make_front(count, places, heads, size, scale),
        [
            shape((total, heads * 3 * LANES)),
            shape((hot_all, heads * LANES)),
            shape((hot_all, heads * LANES)),
            shape((hot_all // 2, width)),
            shape((hot_all // 2, width)),
        ],
        normed_all[half:] + [qkv_a, wqkv, proj],
        "front",
        extra=8,
        moved=1024,
        loose=half,
        scratch=[
            pltpu.VMEM((half * rows, width), bf16),
            pltpu.SemaphoreType.DMA((half,)),
        ],
    )
    hot_sums = fold_scatter(even, odd, places, "fold_hot")

    outs = run(
        make_mid(count // 2, groups),
        [shape((places, width)), shape((places, width), f32), shape((places, 1), f32)]
        + [shape((each, 2 * width))] * groups,
        hot_sums + [tok_hot, link, grad_out],
        "mid_hot",
    )
    mid_hot, normal_hot, factor_hot = outs[:3]
    pieces = outs[3:]

    upper = upper_rows(cold)
    parts_cold = [(half * n, width) for n in (upper, upper, cold - upper, cold - upper)]
    ctx_cold, ask_cold, even_a, odd_a, even_b, odd_b = run(
        make_cold(count, places, heads, size),
        [
            shape((count * cold, heads * LANES)),
            shape((count * cold, heads * LANES)),
        ]
        + [shape(p) for p in parts_cold],
        [after(qkv, mid_hot), proj],
        "cold",
        extra=14,
        flops=4 * total * total * heads * LANES,
    )
    mask = far
    starts = {0: after(cot_cold, mid_hot)}
    while mask > 1:
        cots[mask] = hop(starts[0], "tensor", mask)
        mask //= 2
    landed = jnp.concatenate(
        [pieces[0]] + [hop(pieces[g], "dp", g) for g in range(1, groups)], axis=0
    )
    landed = after(landed, ctx_cold, list(cots.values()))
    arrived_all = gather_rel(landed)
    start, mask = {k: after(y, arrived_all[count - 2], arrived_all[2]) for k, y in cots.items()}, far // 2
    early = [k for k in cots if k and k % 2 == 0]
    for k in early:
        cots[k + 1] = hop(after(cots[k], arrived_all), "tensor", 1)
    while mask > 1:
        for k in list(cots):
            if k % 2 == 0 and k > mask and k ^ mask not in cots:
                start[k ^ mask] = cots[k ^ mask] = hop(start[k], "tensor", mask)
        mask //= 2
    theirs_a = hop(after(odd_a, arrived_all), "tensor", 1)
    theirs_b = hop(after(odd_b, arrived_all), "tensor", 1)
    arrived, slot_grads, hidden, grad_pre, even, odd = run(
        make_expert(count, experts),
        [
            shape((slots, width)),
            shape((slots, width)),
            shape((experts, slots, hidden_dev)),
            shape((experts, slots, hidden_dev)),
            shape((slots // 2, 2 * width)),
            shape((slots // 2, 2 * width)),
        ],
        arrived_all + [up_weight, down_weight],
        "experts",
        extra=8,
        flops=6 * slots * width * hidden_dev * experts,
    )
    keep_a, send_a = halve(even_a, theirs_a, "fold_cold_1a")
    keep_b, send_b = halve(even_b, theirs_b, "fold_cold_1b")
    sums = fold_scatter(even, after(odd, list(cots.values()), keep_a, keep_b), places, "fold_slots")
    for k in range(1, count, 2):
        if k not in cots:
            cots[k] = hop(after(cots[k - 1], arrived_all), "tensor", 1)
    cot_all = [cots[k] for k in range(count)]
    gq, gk, gv, gp = run(
        make_cold_back(count, places, heads, size, scale),
        [
            shape((count * cold, heads * LANES)),
            shape((heads * LANES, total), f32),
            shape((heads * LANES, total), f32),
            shape((heads * LANES, width), f32),
        ],
        cot_all + [after(qkv, sums[0]), proj, ctx_cold, ask_cold],
        "cold_back",
        extra=16,
        flops=10 * total * total * heads * LANES,
        loose=count,
        scratch=[
            pltpu.VMEM((count * cold, width), bf16),
            pltpu.SemaphoreType.DMA((count,)),
        ],
    )
    sums = after(sums, gp)

    pieces = run(
        make_split(count // 2, groups),
        [shape((each, 2 * width))] * groups,
        sums,
        "split_slots",
    )
    back = [pieces[0]] + [hop(pieces[g], "dp", g) for g in range(1, groups)]
    theirs_a = hop(after(send_a, pieces[0]), "tensor", 2)
    back = after(back, theirs_a)
    grad_hot, expert_out = run(
        make_mid_back(groups),
        [shape((places, width)), shape((places, width))],
        back + [link, cot_hot, normal_hot, factor_hot],
        "mid_back",
    )
    box.clear()

    def turn(_):
        box.append(
            run(
                make_turn(half),
                [shape((width, half * rows))],
                after(normed_all[half:], grad_hot),
                "turn",
        extra=3,
            )[0]
        )
        return box[0]

    grad_hot_all = gather_rel(grad_hot, turn)
    fn_b = box[0]
    keep_a = after(keep_a, grad_hot)
    theirs_b = hop(after(send_b, grad_hot_all), "tensor", 2)
    mask = 4
    while mask < count:
        keep_a, send_a = halve(keep_a, theirs_a, f"fold_cold_{mask // 2}a")
        theirs_a = hop(send_a, "tensor", mask)
        keep_b, send_b = halve(keep_b, theirs_b, f"fold_cold_{mask // 2}b")
        theirs_b = hop(send_b, "tensor", mask)
        mask *= 2
    cold_sums = [keep_a, theirs_a, keep_b, theirs_b]

    me = lax.axis_index("dp").astype(jnp.int32).reshape(1)
    each_w = width // groups
    first_w = near_rows(each_w)
    halves = [(groups // 2 * n, heads * 4 * size) for n in (first_w, each_w - first_w)]
    keep_a, send_a, keep_b, send_b = run(
        make_hot_back(count, heads, size, groups, scale),
        [shape(halves[0]), shape(halves[0]), shape(halves[1]), shape(halves[1])],
        after(grad_hot_all, keep_a)
        + [me, qkv, proj, ctx_hot, ask_hot, gq, gk, gv, gp, fn_a, fn_b],
        "hot_back",
        extra=10,
        moved=1024,
        smem=(count,),
        scratch=[
            pltpu.VMEM((heads * 3 * size, total), bf16),
            pltpu.VMEM((total, LANES), bf16),
            pltpu.VMEM((width, heads * 4 * size), bf16),
        ],
    )
    grad_up, grad_down = run(
        make_weight_grads(experts),
        [shape(up_weight.shape), shape(down_weight.shape)],
        [after(arrived, keep_a), slot_grads, hidden, grad_pre],
        "weight_grads",
        extra=10,
        moved=1024,
    )
    mask = 1
    while True:
        got_a = hop(send_a, "dp", mask)
        got_b = hop(send_b, "dp", groups // 2 // mask)
        if mask == 1:
            got_a, got_b = after((got_a, got_b), grad_up, cold_sums[2])
        if mask == groups // 2:
            break
        keep_a, send_a = halve(keep_a, got_a, f"fold_a_{mask}")
        keep_b, send_b = halve(keep_b, got_b, f"fold_b_{mask}")
        mask *= 2
    parts = [keep_a, got_a, keep_b, got_b]
    layer_out, gate_grad = run(
        make_epilogue(),
        [shape((rows, width)), shape((2, rows), f32)],
        cold_sums
        + [tok_cold, mid_hot, perm, pick0, pick1, expert_out, gate_weights.T, cotangent],
        "epilogue",
        extra=4,
    )
    grad_qkv, grad_proj = run(
        make_last(heads, size),
        [shape((width // groups, heads, 3 * size), f32), shape((heads, size, width // groups), f32)],
        after(parts, layer_out, grad_up),
        "last",
        extra=6,
    )
    return (layer_out, gate_grad.T, grad_qkv, grad_proj, grad_up, grad_down)


def solution(mesh):
    return jax.shard_map(
        shards,
        mesh=mesh,
        in_specs=(
            P(("dp", "tensor"), None),
            P(("dp", "tensor"), None),
            P(("dp", "tensor"), None),
            P(("dp", "tensor"), None),
            P(("dp", "tensor"), None),
            P(None, "tensor", None),
            P("tensor", None, None),
            P("dp", None, "tensor"),
            P("dp", "tensor", None),
        ),
        out_specs=(
            P(("dp", "tensor"), None),
            P(("dp", "tensor"), None),
            P("dp", "tensor", None),
            P("tensor", None, "dp"),
            P("dp", None, "tensor"),
            P("dp", "tensor", None),
        ),
        check_vma=False,
    )
```

```python
import math

import jax
import jax.numpy as jnp
from jax import lax
from jax.experimental import pallas as pl
from jax.experimental.pallas import tpu as pltpu
from jax.sharding import PartitionSpec as P

CAP = 2
LANES = 128
epsilon = 1e-06
half_root = 1.0 / math.sqrt(2.0)
bell_scale = 1.0 / math.sqrt(2.0 * math.pi)
LOG2E = math.log2(math.e)
f32 = jnp.float32
bf16 = jnp.bfloat16


def norm_parts(row_block):
    widened = row_block.astype(f32)
    center = widened - jnp.mean(widened, axis=-1, keepdims=True)
    factor = lax.rsqrt(jnp.mean(center * center, axis=-1, keepdims=True) + epsilon)
    return (center * factor, factor)


def norm_back(normal_rows, factor, upstream):
    mean_up = jnp.mean(upstream, axis=-1, keepdims=True)
    mean_mix = jnp.mean(upstream * normal_rows, axis=-1, keepdims=True)
    return factor * (upstream - mean_up - normal_rows * mean_mix)


def dot(a, b):
    return lax.dot_general(a, b, (((1,), (0,)), ((), ())), preferred_element_type=f32)


def dot_nt(a, b):
    return lax.dot_general(a, b, (((1,), (1,)), ((), ())), preferred_element_type=f32)


def dot_tn(a, b):
    return lax.dot_general(a, b, (((0,), (0,)), ((), ())), preferred_element_type=f32)


def run(body, outs, ins, name, flops=0, extra=1, moved=None, smem=(), loose=0, scratch=()):
    specs = [
        pl.BlockSpec(
            memory_space=pl.ANY if i < loose else pltpu.SMEM if i in smem else pltpu.VMEM
        )
        for i in range(len(ins))
    ]
    sizes = [math.prod(x.shape) * x.dtype.itemsize for x in list(ins)[loose:] + list(outs)]
    sizes += [math.prod(x.shape) * x.dtype.itemsize for x in scratch if x.dtype in (f32, bf16)]
    limit = int(sum(sizes) * 1.2) + extra * 2**20
    return pl.pallas_call(
        body,
        out_shape=list(outs),
        in_specs=specs,
        out_specs=[pl.BlockSpec(memory_space=pltpu.VMEM)] * len(outs),
        scratch_shapes=list(scratch),
        compiler_params=pltpu.CompilerParams(vmem_limit_bytes=limit),
        cost_estimate=pl.CostEstimate(
            flops=int(flops), bytes_accessed=int(sum(sizes) if moved is None else moved), transcendentals=0
        ),
        name=name,
    )(*ins)


def after(x, *others):
    return lax.optimization_barrier((x, others))[0]


def pull(pairs, sems):
    copies = [pltpu.make_async_copy(a, b, sems.at[i]) for i, (a, b) in enumerate(pairs)]
    for c in copies:
        c.start()
    for c in copies:
        c.wait()


def shape(dims, dtype=bf16):
    return jax.ShapeDtypeStruct(tuple(dims), dtype)


def block_of(rows, most=256):
    return max(b for b in range(16, most + 1, 16) if rows % b == 0)


def hop(x, axis, mask):
    size = lax.axis_size(axis)
    return lax.ppermute(x, axis, [(i, i ^ mask) for i in range(size)])


def gather_rel(x, hold=None, firm=()):
    size = lax.axis_size("tensor")
    have = {0: x}
    odd = {}
    mask = size // 2
    while mask > 1:
        have.update({k ^ mask: hop(y, "tensor", mask) for k, y in list(have.items())})
        mask //= 2
    if hold is not None:
        held = hold(have)
        last = size - 2
        have[last] = after(have[last], held)
    return [hop(have[k - 1], "tensor", 1) if k % 2 else have[k] for k in range(size)]


def fold_order(keys, flip=False):
    bits = range(7, -1, -1) if flip else range(8)
    return sorted(keys, key=lambda k: tuple((k >> b) & 1 for b in bits))


def prologue_body(tok_in, cot_in, group, gate_t, routes_t, slots_t, *outs):
    normed_o, cot_hot_o, cot_cold_o, tok_hot_o, tok_cold_o, perm_o, pick0_o, pick1_o, link_o, gout_o, tok, cot, sems = outs
    half = tok.shape[0] // 2
    pairs = [(tok_in, tok), (cot_in, cot)]
    copies = [
        pltpu.make_async_copy(
            a.at[i * half : (i + 1) * half], b.at[i * half : (i + 1) * half], sems.at[2 * n + i]
        )
        for n, (a, b) in enumerate(pairs)
        for i in range(2)
    ]
    for c in copies:
        c.start()
    rows = tok.shape[0]
    places = pick0_o.shape[1]
    code_t = jnp.where(slots_t[...] >= 0, (routes_t[...] ^ group[0]) * CAP + slots_t[...], -1)
    packed = jnp.concatenate(
        [code_t.astype(f32), gate_t[...], jnp.zeros((4, rows), f32)], axis=0
    ).T
    code = packed[:, 0:2].astype(jnp.int32)
    gate = packed[:, 2:4]
    lane = lax.broadcasted_iota(jnp.int32, (rows, LANES), 1)
    wide0 = (code[:, 0:1] == lane).astype(f32)
    wide1 = (code[:, 1:2] == lane).astype(f32)
    kept0 = (code[:, 0:1] >= 0).astype(f32)
    prim = wide0 + wide1 * (1.0 - kept0)
    plain = 1.0 - jnp.sum(prim, axis=1, keepdims=True)
    open_at = 1.0 - jnp.sum(prim, axis=0, keepdims=True)
    ri = lax.broadcasted_iota(jnp.int32, (rows, rows), 0)
    ci = lax.broadcasted_iota(jnp.int32, (rows, rows), 1)
    row_rank = dot(
        (ci < ri).astype(bf16), jnp.broadcast_to(plain, (rows, rows)).astype(bf16)
    )
    place_rank = dot(
        jnp.broadcast_to(open_at, (rows, rows)).astype(bf16), (ri < ci).astype(bf16)
    )
    filler = plain * open_at * (row_rank == place_rank).astype(f32)
    perm = (prim + filler).astype(bf16)
    perm_o[...] = perm
    for c in copies:
        c.wait()
    normal, _ = norm_parts(tok[...])
    normed_o[...] = dot_tn(perm, normal.astype(bf16)).astype(bf16)
    for source, hot_o, cold_o in ((cot, cot_hot_o, cot_cold_o), (tok, tok_hot_o, tok_cold_o)):
        moved = dot_tn(perm, source[...]).astype(bf16)
        hot_o[...] = moved[:places]
        cold_o[...] = moved[places:]
    pick0 = wide0.astype(bf16)
    pick1 = wide1.astype(bf16)
    pick0_o[...] = pick0[:, :places]
    pick1_o[...] = pick1[:, :places]
    link_o[...] = dot_tn((pick0 + pick1), prim.astype(bf16))[:places, :places].astype(bf16)
    upstream = cot[...].astype(f32)
    g0 = (gate[:, 0:1] * upstream).astype(bf16)
    g1 = (gate[:, 1:2] * upstream).astype(bf16)
    gout_o[...] = (dot_tn(pick0, g0) + dot_tn(pick1, g1))[:places].astype(bf16)


def make_prep(heads, size):
    def body(w, p, wo, po):
        wo[...] = jnp.zeros_like(wo)
        po[...] = jnp.zeros_like(po)
        for h in range(heads):
            for i in range(3):
                at = (3 * h + i) * LANES
                wo[at : at + size] = w[h, i * size : (i + 1) * size]
            po[h * LANES : h * LANES + size] = p[h]

    return body


def spare_lanes(dims, size):
    lane = lax.broadcasted_iota(jnp.int32, dims, 1) % LANES
    return (lane >= size) & (lane < size + 3)


def with_term(rows, term, size):
    lane = lax.broadcasted_iota(jnp.int32, rows.shape, 1)
    first = term.astype(bf16).astype(f32)
    second = (term - first).astype(bf16).astype(f32)
    third = term - first - second
    term = jnp.where(lane == size, first, jnp.where(lane == size + 1, second, third))
    return jnp.where(spare_lanes(rows.shape, size), term, rows.astype(f32)).astype(bf16)


def project(rows, weights, heads, size, scale):
    raw = dot_nt(rows, weights)
    part = lax.broadcasted_iota(jnp.int32, raw.shape, 1) // LANES % 3
    factor = jnp.where(part == 0, scale * LOG2E, 1.0)
    ones = ((part != 0) & spare_lanes(raw.shape, size)).astype(f32)
    return (raw * factor + ones).astype(bf16)


def attend(queries, keys, values, size):
    raised = jnp.exp2(dot_nt(queries, keys))
    total = jnp.sum(raised, axis=-1, keepdims=True)
    shares = raised * (1.0 / total)
    return dot(shares.astype(bf16), values).astype(bf16), with_term(queries, -jnp.log2(total), size)


def part_of(ref, rows, which, head):
    at = (3 * head + which) * LANES
    return ref[rows, at : at + LANES]


def pieces_of(ref, first, count, every, lo, hi, at):
    return jnp.concatenate(
        [ref[(first + k) * every + lo : (first + k) * every + hi, at] for k in range(count)], axis=0
    )


def make_half(count, heads, size, scale):
    def body(*refs):
        shards, (weights, qkv, fn_t, fn, sems) = refs[:count], refs[count:]
        rows = shards[0].shape[0]
        pull([(shards[k], fn.at[k * rows : (k + 1) * rows]) for k in range(count)], sems)
        for k in range(count):
            at = slice(k * rows, (k + 1) * rows)
            fn_t[:, at] = fn[at, :].T
        step = block_of(fn.shape[0])

        def chunk(i, _):
            at = pl.ds(pl.multiple_of(i * step, 16), step)
            qkv[at, :] = project(fn[at, :], weights[...], heads, size, scale)
            return 0

        lax.fori_loop(0, fn.shape[0] // step, chunk, 0)

    return body


def make_turn(count):
    def body(*refs):
        shards, fn_t = refs[:count], refs[count]
        rows = shards[0].shape[0]
        for k in range(count):
            fn_t[:, k * rows : (k + 1) * rows] = shards[k][...].T

    return body


def make_front(count, places, heads, size, scale):
    def body(*refs):
        half = count // 2
        shards, (first, weights, proj) = refs[:half], refs[half : half + 3]
        qkv, ctx, ask, even, odd, fn, sems = refs[half + 3 :]
        rows = shards[0].shape[0]
        pull([(shards[k], fn.at[k * rows : (k + 1) * rows]) for k in range(half)], sems)
        done = first.shape[0]
        qkv[:done] = first[...]
        step = block_of(fn.shape[0])

        def chunk(i, _):
            at = pl.ds(pl.multiple_of(i * step, 16), step)
            to = pl.ds(pl.multiple_of(done + i * step, 16), step)
            qkv[to, :] = project(fn[at, :], weights[...], heads, size, scale)
            return 0

        lax.fori_loop(0, fn.shape[0] // step, chunk, 0)
        every = slice(None)
        for h in range(heads):
            cut = slice(h * LANES, (h + 1) * LANES)
            queries = pieces_of(
                qkv, 0, count, rows, 0, places, slice(3 * h * LANES, (3 * h + 1) * LANES)
            )
            ctx[:, cut], ask[:, cut] = attend(
                queries, part_of(qkv, every, 1, h), part_of(qkv, every, 2, h), size
            )
        part = dot(ctx[...], proj[...]).astype(bf16)
        for i, k in enumerate(range(0, count, 2)):
            even[i * places : (i + 1) * places] = part[k * places : (k + 1) * places]
            odd[i * places : (i + 1) * places] = part[(k + 1) * places : (k + 2) * places]

    return body


def make_cold(count, places, heads, size):
    def body(qkv, proj, ctx, ask, even_a, odd_a, even_b, odd_b):
        rows = qkv.shape[0] // count
        cold = rows - places
        upper = upper_rows(cold)
        every = slice(None)
        group = min(4, count)
        order = fold_order(range(0, count, 2))
        for first in range(0, count, group):
            at = slice(first * cold, (first + group) * cold)
            for h in range(heads):
                cut = slice(h * LANES, (h + 1) * LANES)
                queries = pieces_of(
                    qkv, first, group, rows, places, rows, slice(3 * h * LANES, (3 * h + 1) * LANES)
                )
                ctx[at, cut], ask[at, cut] = attend(
                    queries, part_of(qkv, every, 1, h), part_of(qkv, every, 2, h), size
                )
            part = dot(ctx[at, :], proj[...]).astype(bf16)
            for k in range(first, first + group):
                one = part[(k - first) * cold : (k - first + 1) * cold]
                i = order.index(k // 2 * 2)
                to = odd_a if k % 2 else even_a
                to[i * upper : (i + 1) * upper] = one[:upper]
                to = odd_b if k % 2 else even_b
                to[i * (cold - upper) : (i + 1) * (cold - upper)] = one[upper:]

    return body


def back_block(ask, keys, values, ctx, grad_ctx, size):
    shares = jnp.exp2(dot_nt(ask, keys))
    mix = jnp.sum(grad_ctx.astype(f32) * ctx.astype(f32), axis=-1, keepdims=True)
    grad_ctx = with_term(grad_ctx, -mix, size)
    grad_scores = (shares * dot_nt(grad_ctx, values)).astype(bf16)
    return (
        dot(grad_scores, keys),
        dot_tn(ask, grad_scores),
        dot_tn(grad_ctx, shares.astype(bf16)),
    )


def make_cold_back(count, places, heads, size, scale):
    def body(*refs):
        shards, (qkv, proj, ctx, ask) = refs[:count], refs[count : count + 4]
        gq, gk, gv, gp, cots, sems = refs[count + 4 :]
        cold = shards[0].shape[0]
        pull([(shards[k], cots.at[k * cold : (k + 1) * cold]) for k in range(count)], sems)
        every = slice(None)
        group = min(4, count)
        for first in range(0, count, group):
            at = slice(first * cold, (first + group) * cold)
            grad_ctx = dot_nt(cots[at, :], proj[...]).astype(bf16)
            proj_grad = dot_tn(ctx[at, :], cots[at, :])
            for h in range(heads):
                cut = slice(h * LANES, (h + 1) * LANES)
                a, b, c = back_block(
                    ask[at, cut],
                    part_of(qkv, every, 1, h),
                    part_of(qkv, every, 2, h),
                    ctx[at, cut],
                    grad_ctx[:, cut],
                    size,
                )
                gq[at, cut] = (a * scale).astype(bf16)
                if first:
                    gk[cut, :] += b
                    gv[cut, :] += c
                else:
                    gk[cut, :] = b
                    gv[cut, :] = c
            if first:
                gp[...] += proj_grad
            else:
                gp[...] = proj_grad

    return body


def make_hot_back(count, heads, size, groups, scale):
    def body(*refs):
        shards = refs[:count]
        place, qkv, proj, ctx, ask, gq, gk, gv, gp, fn_a, fn_b = refs[count : count + 11]
        outs = refs[count + 11 : count + 15]
        rows_t, grad_q, whole = refs[count + 15 :]
        grads = jnp.concatenate([s[...] for s in shards], axis=0)
        places = shards[0].shape[0]
        rows = qkv.shape[0] // count
        cold = rows - places
        grad_ctx = dot_nt(grads, proj[...]).astype(bf16)
        proj_grad = gp[...] + dot_tn(ctx[...], grads)
        base = heads * 3 * size
        every = slice(None)
        proj_rows = []
        for h in range(heads):
            cut = slice(h * LANES, (h + 1) * LANES)
            a, b, c = back_block(
                ask[:, cut],
                part_of(qkv, every, 1, h),
                part_of(qkv, every, 2, h),
                ctx[:, cut],
                grad_ctx[:, cut],
                size,
            )
            a = (a * scale).astype(bf16)
            for k in range(count):
                grad_q[k * rows : k * rows + places] = a[k * places : (k + 1) * places]
                grad_q[k * rows + places : (k + 1) * rows] = gq[k * cold : (k + 1) * cold, cut]
            at = h * 3 * size
            rows_t[at : at + size, :] = grad_q[...].T[:size]
            rows_t[at + size : at + 2 * size, :] = ((gk[cut, :] + b) * (1.0 / LOG2E))[
                :size
            ].astype(bf16)
            rows_t[at + 2 * size : at + 3 * size, :] = (gv[cut, :] + c)[:size].astype(bf16)
            proj_rows.append(proj_grad[h * LANES : h * LANES + size].astype(bf16))
        done = fn_a.shape[1]
        turned = rows_t[...].T
        whole[:, :base] = (dot(fn_a[...], turned[:done]) + dot(fn_b[...], turned[done:])).astype(
            bf16
        )
        whole[:, base:] = jnp.concatenate(proj_rows, axis=0).T
        each = whole.shape[0] // groups
        cuts = (0, near_rows(each), each)
        for n in range(2):
            size_n = cuts[n + 1] - cuts[n]
            for i, g in enumerate(fold_order(range(groups), n == 1)):
                at = pl.multiple_of((place[0] ^ g) * each + cuts[n], 16)
                to = outs[2 * n + i // (groups // 2)]
                i = i % (groups // 2)
                to[i * size_n : (i + 1) * size_n] = whole[pl.ds(at, size_n), :]

    return body


def upper_rows(rows):
    return (rows * 5 // 7 + 15) // 16 * 16


def near_rows(rows):
    return (rows // 2 + 15) // 16 * 16


def make_last(heads, size):
    def body(a, b, c, d, qkv_o, proj_o):
        total = jnp.concatenate([total_of([a, b]), total_of([c, d])], axis=0)
        base = heads * 3 * size
        turned = total[:, base:].T
        for h in range(heads):
            qkv_o[:, h, :] = total[:, h * 3 * size : (h + 1) * 3 * size]
            proj_o[h] = turned[h * size : (h + 1) * size]

    return body


def make_fold(count):
    def body(mine, theirs, *outs):
        rows = outs[0].shape[0]
        for i in range(count):
            at = slice(i * rows, (i + 1) * rows)
            outs[i][...] = (mine[at].astype(f32) + theirs[at].astype(f32)).astype(bf16)

    return body


def total_of(refs):
    total = refs[0][...].astype(f32)
    for r in refs[1:]:
        total = total + r[...].astype(f32)
    return total


def make_mid(count, groups):
    def body(*refs):
        parts, (tok, link, grads) = refs[:count], refs[count : count + 3]
        mid_o, normal_o, factor_o = refs[count + 3 : count + 6]
        outs = refs[count + 6 :]
        mid = (tok[...].astype(f32) + total_of(parts)).astype(bf16)
        normal, factor = norm_parts(mid)
        mid_o[...] = mid
        normal_o[...] = normal
        factor_o[...] = factor
        slot_in = dot(link[...], normal.astype(bf16))
        each = slot_in.shape[0] // groups
        for g in range(groups):
            at = slice(g * each, (g + 1) * each)
            both = jnp.concatenate([slot_in[at], grads[at].astype(f32)], axis=1)
            outs[g][...] = both.astype(bf16)

    return body


def slot_mask(rows, experts, e):
    row = lax.broadcasted_iota(jnp.int32, (rows, 1), 0)
    return (row // CAP) % experts == e


def make_expert(count, experts):
    def body(*refs):
        shards = refs[:count]
        up, down, arrived, grads, hid_o, pre_o, even, odd = refs[count:]
        width = arrived.shape[1]
        arrived[...] = jnp.concatenate([s[:, :width] for s in shards], axis=0)
        grads[...] = jnp.concatenate([s[:, width:] for s in shards], axis=0)
        rows = arrived.shape[0]
        forth = None
        back = None
        for e in range(experts):
            keep = slot_mask(rows, experts, e)
            pre = dot(arrived[...], up[e])
            cdf = 0.5 * (1.0 + lax.erf(pre * half_root))
            hidden = jnp.where(keep, pre * cdf, 0.0).astype(bf16)
            slope = cdf + pre * jnp.exp(-0.5 * pre * pre) * bell_scale
            grad_pre = jnp.where(keep, dot_nt(grads[...], down[e]) * slope, 0.0).astype(bf16)
            hid_o[e] = hidden
            pre_o[e] = grad_pre
            a = dot(hidden, down[e])
            b = dot_nt(grad_pre, up[e])
            forth = a if forth is None else forth + a
            back = b if back is None else back + b
        both = jnp.concatenate([back, forth], axis=1).astype(bf16)
        each = rows // count
        for k in range(count):
            to = odd if k % 2 else even
            to[(k // 2) * each : (k // 2 + 1) * each] = both[k * each : (k + 1) * each]

    return body


def make_weight_grads(experts):
    def body(arrived, grads, hidden, grad_pre, up_o, down_o):
        for e in range(experts):
            up_o[e] = dot_tn(arrived[...], grad_pre[e]).astype(bf16)
            down_o[e] = dot_tn(hidden[e], grads[...]).astype(bf16)

    return body


def make_split(count, groups):
    def body(*refs):
        parts, outs = refs[:count], refs[count:]
        total = total_of(parts)
        each = total.shape[0] // groups
        for g in range(groups):
            outs[g][...] = total[g * each : (g + 1) * each].astype(bf16)

    return body


def make_mid_back(groups):
    def body(*refs):
        parts = refs[:groups]
        link, cot, normal, factor, grad_o, expert_o = refs[groups:]
        both = jnp.concatenate([p[...].astype(f32) for p in parts], axis=0).astype(bf16)
        width = cot.shape[1]
        expert_o[...] = both[:, width:]
        grad_norm = dot_tn(link[...], both[:, :width])
        grad_o[...] = (
            cot[...].astype(f32) + norm_back(normal[...], factor[...], grad_norm)
        ).astype(bf16)

    return body


def make_epilogue():
    def body(*refs):
        parts = refs[:4]
        tok, mid_hot, perm, pick0, pick1, experts, gate_t, cot, out, gate_o = refs[4:]
        sums = jnp.concatenate([total_of(parts[:2]), total_of(parts[2:])], axis=0)
        cold = (tok[...].astype(f32) + sums).astype(bf16)
        ordered = jnp.concatenate([mid_hot[...], cold], axis=0)
        mid = dot(perm[...], ordered)
        gate = jnp.concatenate([gate_t[...], jnp.zeros((6, gate_t.shape[1]), f32)], axis=0).T
        first = dot(pick0[...], experts[...])
        second = dot(pick1[...], experts[...])
        out[...] = (mid + gate[:, 0:1] * first + gate[:, 1:2] * second).astype(bf16)
        upstream = cot[...].astype(f32)
        lane = lax.broadcasted_iota(jnp.int32, (upstream.shape[0], LANES), 1)
        one = jnp.sum(upstream * first, axis=-1, keepdims=True)
        two = jnp.sum(upstream * second, axis=-1, keepdims=True)
        gate_o[...] = jnp.where(lane == 0, one, two).T[:2]

    return body


def fold_scatter(even, odd, rows, name):
    count = lax.axis_size("tensor") // 2
    theirs = hop(odd, "tensor", 1)
    sums = run(
        make_fold(count), [shape((rows, even.shape[1]))] * count, [even, theirs], name
    )
    return [sums[0]] + [hop(sums[i], "tensor", 2 * i) for i in range(1, count)]


def halve(mine, theirs, name):
    half = (mine.shape[0] // 2, mine.shape[1])
    return run(make_fold(2), [shape(half), shape(half)], [mine, theirs], name)


def shards(
    tokens,
    cotangent,
    gate_weights,
    routes,
    slot_index,
    qkv_weight,
    proj_weight,
    up_weight,
    down_weight,
):
    rows, width = tokens.shape
    heads, size = qkv_weight.shape[1], qkv_weight.shape[2] // 3
    scale = size ** (-0.5)
    groups = lax.axis_size("dp")
    count = lax.axis_size("tensor")
    experts, _, hidden_dev = up_weight.shape
    each = experts * CAP
    places = groups * each
    cold = rows - places
    hot_all = count * places
    total = count * rows
    slots = count * places

    wqkv, proj = run(
        make_prep(heads, size),
        [shape((heads * 3 * LANES, width)), shape((heads * LANES, width))],
        [qkv_weight.transpose(1, 2, 0), proj_weight],
        "prep",
    )
    group = (lax.axis_index("dp") * experts).astype(jnp.int32).reshape(1)
    normed, cot_hot, cot_cold, tok_hot, tok_cold, perm, pick0, pick1, link, grad_out = run(
        prologue_body,
        [
            shape((rows, width)),
            shape((places, width)),
            shape((cold, width)),
            shape((places, width)),
            shape((cold, width)),
            shape((rows, rows)),
            shape((rows, places)),
            shape((rows, places)),
            shape((places, places)),
            shape((places, width)),
        ],
        [tokens, cotangent, group, gate_weights.T, routes.T, slot_index.T],
        "prologue",
        extra=57,
        smem=(2,),
        loose=2,
        scratch=[
            pltpu.VMEM((rows, width), bf16),
            pltpu.VMEM((rows, width), bf16),
            pltpu.SemaphoreType.DMA((4,)),
        ],
    )
    half = count // 2
    cots = {0: cot_cold, 1: hop(cot_cold, "tensor", 1)}
    def first_half(have):
        near = [
            hop(have[k - 1], "tensor", 1) if k % 2 else have[k] for k in range(half)
        ]
        return run(
            make_half(half, heads, size, scale),
            [shape((half * rows, heads * 3 * LANES)), shape((width, half * rows))],
            after(near, cots[1]) + [wqkv],
            "half",
        extra=6,
        moved=1024,
            loose=half,
            scratch=[
                pltpu.VMEM((half * rows, width), bf16),
                pltpu.SemaphoreType.DMA((half,)),
            ],
        )

    box = []

    def hold(have):
        box.append((have, first_half(have)))
        return box[0][1]

    normed_all = gather_rel(normed, hold)
    have, (qkv_a, fn_a) = box[0]

    far = count // 2
    qkv, ctx_hot, ask_hot, even, odd = run(
        make_front(count, places, heads, size, scale),
        [
            shape((total, heads * 3 * LANES)),
            shape((hot_all, heads * LANES)),
            shape((hot_all, heads * LANES)),
            shape((hot_all // 2, width)),
            shape((hot_all // 2, width)),
        ],
        normed_all[half:] + [qkv_a, wqkv, proj],
        "front",
        extra=8,
        moved=1024,
        loose=half,
        scratch=[
            pltpu.VMEM((half * rows, width), bf16),
            pltpu.SemaphoreType.DMA((half,)),
        ],
    )
    hot_sums = fold_scatter(even, odd, places, "fold_hot")
    start, mask = after(cot_cold, have[count - 2]), far
    while mask > 1:
        cots[mask] = hop(start, "tensor", mask)
        mask //= 2
    hot_sums = after(hot_sums, list(cots.values()))

    outs = run(
        make_mid(count // 2, groups),
        [shape((places, width)), shape((places, width), f32), shape((places, 1), f32)]
        + [shape((each, 2 * width))] * groups,
        hot_sums + [tok_hot, link, grad_out],
        "mid_hot",
    )
    mid_hot, normal_hot, factor_hot = outs[:3]
    pieces = outs[3:]

    upper = upper_rows(cold)
    parts_cold = [(half * n, width) for n in (upper, upper, cold - upper, cold - upper)]
    ctx_cold, ask_cold, even_a, odd_a, even_b, odd_b = run(
        make_cold(count, places, heads, size),
        [
            shape((count * cold, heads * LANES)),
            shape((count * cold, heads * LANES)),
        ]
        + [shape(p) for p in parts_cold],
        [after(qkv, mid_hot), proj],
        "cold",
        extra=14,
        flops=4 * total * total * heads * LANES,
    )
    start, mask = {k: after(y, mid_hot) for k, y in cots.items()}, far // 2
    early = [k for k in cots if k and k % 2 == 0]
    while mask > 1:
        for k in list(cots):
            if k % 2 == 0 and k > mask and k ^ mask not in cots:
                start[k ^ mask] = cots[k ^ mask] = hop(start[k], "tensor", mask)
        mask //= 2
    landed = jnp.concatenate(
        [pieces[0]] + [hop(pieces[g], "dp", g) for g in range(1, groups)], axis=0
    )
    landed = after(landed, ctx_cold, list(cots.values()))
    arrived_all = gather_rel(landed)
    for k in early:
        cots[k + 1] = hop(after(cots[k], arrived_all), "tensor", 1)
    theirs_a = hop(after(odd_a, arrived_all), "tensor", 1)
    theirs_b = hop(after(odd_b, arrived_all), "tensor", 1)
    arrived, slot_grads, hidden, grad_pre, even, odd = run(
        make_expert(count, experts),
        [
            shape((slots, width)),
            shape((slots, width)),
            shape((experts, slots, hidden_dev)),
            shape((experts, slots, hidden_dev)),
            shape((slots // 2, 2 * width)),
            shape((slots // 2, 2 * width)),
        ],
        arrived_all + [up_weight, down_weight],
        "experts",
        extra=8,
        flops=6 * slots * width * hidden_dev * experts,
    )
    keep_a, send_a = halve(even_a, theirs_a, "fold_cold_1a")
    keep_b, send_b = halve(even_b, theirs_b, "fold_cold_1b")
    sums = fold_scatter(even, after(odd, list(cots.values()), keep_a, keep_b), places, "fold_slots")
    theirs_a = hop(after(send_a, sums[0]), "tensor", 2)
    for k in range(1, count, 2):
        if k not in cots:
            cots[k] = hop(after(cots[k - 1], arrived_all), "tensor", 1)
    cot_all = [cots[k] for k in range(count)]
    gq, gk, gv, gp = run(
        make_cold_back(count, places, heads, size, scale),
        [
            shape((count * cold, heads * LANES)),
            shape((heads * LANES, total), f32),
            shape((heads * LANES, total), f32),
            shape((heads * LANES, width), f32),
        ],
        cot_all + [after(qkv, sums[0]), proj, ctx_cold, ask_cold],
        "cold_back",
        extra=16,
        flops=1e10,
        loose=count,
        scratch=[
            pltpu.VMEM((count * cold, width), bf16),
            pltpu.SemaphoreType.DMA((count,)),
        ],
    )
    sums = after(sums, gp)

    pieces = run(
        make_split(count // 2, groups),
        [shape((each, 2 * width))] * groups,
        sums,
        "split_slots",
    )
    back = [pieces[0]] + [hop(pieces[g], "dp", g) for g in range(1, groups)]
    back = after(back, theirs_a)
    grad_hot, expert_out = run(
        make_mid_back(groups),
        [shape((places, width)), shape((places, width))],
        back + [link, cot_hot, normal_hot, factor_hot],
        "mid_back",
    )
    box.clear()

    def turn(_):
        box.append(
            run(
                make_turn(half),
                [shape((width, half * rows))],
                after(normed_all[half:], grad_hot),
                "turn",
        extra=3,
            )[0]
        )
        return box[0]

    grad_hot_all = gather_rel(grad_hot, turn)
    fn_b = box[0]
    keep_a = after(keep_a, grad_hot)
    theirs_b = hop(after(send_b, grad_hot_all), "tensor", 2)
    mask = 4
    while mask < count:
        keep_a, send_a = halve(keep_a, theirs_a, f"fold_cold_{mask // 2}a")
        theirs_a = hop(send_a, "tensor", mask)
        keep_b, send_b = halve(keep_b, theirs_b, f"fold_cold_{mask // 2}b")
        theirs_b = hop(send_b, "tensor", mask)
        mask *= 2
    cold_sums = [keep_a, theirs_a, keep_b, theirs_b]

    me = lax.axis_index("dp").astype(jnp.int32).reshape(1)
    each_w = width // groups
    first_w = near_rows(each_w)
    halves = [(groups // 2 * n, heads * 4 * size) for n in (first_w, each_w - first_w)]
    keep_a, send_a, keep_b, send_b = run(
        make_hot_back(count, heads, size, groups, scale),
        [shape(halves[0]), shape(halves[0]), shape(halves[1]), shape(halves[1])],
        after(grad_hot_all, keep_a)
        + [me, qkv, proj, ctx_hot, ask_hot, gq, gk, gv, gp, fn_a, fn_b],
        "hot_back",
        extra=10,
        moved=1024,
        smem=(count,),
        scratch=[
            pltpu.VMEM((heads * 3 * size, total), bf16),
            pltpu.VMEM((total, LANES), bf16),
            pltpu.VMEM((width, heads * 4 * size), bf16),
        ],
    )
    grad_up, grad_down = run(
        make_weight_grads(experts),
        [shape(up_weight.shape), shape(down_weight.shape)],
        [after(arrived, keep_a), slot_grads, hidden, grad_pre],
        "weight_grads",
        extra=10,
        moved=1024,
    )
    mask = 1
    while True:
        got_a = hop(send_a, "dp", mask)
        got_b = hop(send_b, "dp", groups // 2 // mask)
        if mask == 1:
            got_a, got_b = after((got_a, got_b), grad_up, cold_sums[2])
        if mask == groups // 2:
            break
        keep_a, send_a = halve(keep_a, got_a, f"fold_a_{mask}")
        keep_b, send_b = halve(keep_b, got_b, f"fold_b_{mask}")
        mask *= 2
    parts = [keep_a, got_a, keep_b, got_b]
    layer_out, gate_grad = run(
        make_epilogue(),
        [shape((rows, width)), shape((2, rows), f32)],
        cold_sums
        + [tok_cold, mid_hot, perm, pick0, pick1, expert_out, gate_weights.T, cotangent],
        "epilogue",
        extra=4,
    )
    grad_qkv, grad_proj = run(
        make_last(heads, size),
        [shape((width // groups, heads, 3 * size), f32), shape((heads, size, width // groups), f32)],
        after(parts, layer_out, grad_up),
        "last",
        extra=6,
    )
    return (layer_out, gate_grad.T, grad_qkv, grad_proj, grad_up, grad_down)


def solution(mesh):
    return jax.shard_map(
        shards,
        mesh=mesh,
        in_specs=(
            P(("dp", "tensor"), None),
            P(("dp", "tensor"), None),
            P(("dp", "tensor"), None),
            P(("dp", "tensor"), None),
            P(("dp", "tensor"), None),
            P(None, "tensor", None),
            P("tensor", None, None),
            P("dp", None, "tensor"),
            P("dp", "tensor", None),
        ),
        out_specs=(
            P(("dp", "tensor"), None),
            P(("dp", "tensor"), None),
            P("dp", "tensor", None),
            P("tensor", None, "dp"),
            P("dp", None, "tensor"),
            P("dp", "tensor", None),
        ),
        check_vma=False,
    )
```

```python
import math

import jax
import jax.numpy as jnp
from jax import lax
from jax.experimental import pallas as pl
from jax.experimental.pallas import tpu as pltpu
from jax.sharding import PartitionSpec as P

CAP = 2
LANES = 128
epsilon = 1e-06
half_root = 1.0 / math.sqrt(2.0)
bell_scale = 1.0 / math.sqrt(2.0 * math.pi)
LOG2E = math.log2(math.e)
f32 = jnp.float32
bf16 = jnp.bfloat16


def norm_parts(row_block):
    widened = row_block.astype(f32)
    center = widened - jnp.mean(widened, axis=-1, keepdims=True)
    factor = lax.rsqrt(jnp.mean(center * center, axis=-1, keepdims=True) + epsilon)
    return (center * factor, factor)


def norm_back(normal_rows, factor, upstream):
    mean_up = jnp.mean(upstream, axis=-1, keepdims=True)
    mean_mix = jnp.mean(upstream * normal_rows, axis=-1, keepdims=True)
    return factor * (upstream - mean_up - normal_rows * mean_mix)


def dot(a, b):
    return lax.dot_general(a, b, (((1,), (0,)), ((), ())), preferred_element_type=f32)


def dot_nt(a, b):
    return lax.dot_general(a, b, (((1,), (1,)), ((), ())), preferred_element_type=f32)


def dot_tn(a, b):
    return lax.dot_general(a, b, (((0,), (0,)), ((), ())), preferred_element_type=f32)


def run(body, outs, ins, name, flops=0, extra=1, moved=None, smem=(), loose=0, scratch=()):
    specs = [
        pl.BlockSpec(
            memory_space=pl.ANY if i < loose else pltpu.SMEM if i in smem else pltpu.VMEM
        )
        for i in range(len(ins))
    ]
    sizes = [math.prod(x.shape) * x.dtype.itemsize for x in list(ins)[loose:] + list(outs)]
    sizes += [math.prod(x.shape) * x.dtype.itemsize for x in scratch if x.dtype in (f32, bf16)]
    limit = int(sum(sizes) * 1.2) + extra * 2**20
    return pl.pallas_call(
        body,
        out_shape=list(outs),
        in_specs=specs,
        out_specs=[pl.BlockSpec(memory_space=pltpu.VMEM)] * len(outs),
        scratch_shapes=list(scratch),
        compiler_params=pltpu.CompilerParams(vmem_limit_bytes=limit),
        cost_estimate=pl.CostEstimate(
            flops=int(flops), bytes_accessed=int(sum(sizes) if moved is None else moved), transcendentals=0
        ),
        name=name,
    )(*ins)


def after(x, *others):
    return lax.optimization_barrier((x, others))[0]


def pull(pairs, sems):
    copies = [pltpu.make_async_copy(a, b, sems.at[i]) for i, (a, b) in enumerate(pairs)]
    for c in copies:
        c.start()
    for c in copies:
        c.wait()


def shape(dims, dtype=bf16):
    return jax.ShapeDtypeStruct(tuple(dims), dtype)


def block_of(rows, most=256):
    return max(b for b in range(16, most + 1, 16) if rows % b == 0)


def hop(x, axis, mask):
    size = lax.axis_size(axis)
    return lax.ppermute(x, axis, [(i, i ^ mask) for i in range(size)])


def gather_rel(x, hold=None, firm=(), direct=False):
    size = lax.axis_size("tensor")
    have = {0: x}
    odd = {}
    mask = size // 2
    if direct:
        have.update({k: hop(x, "tensor", k) for k in range(2, size, 2)})
    while mask > 1 and not direct:
        have.update({k ^ mask: hop(y, "tensor", mask) for k, y in list(have.items())})
        mask //= 2
    if hold is not None:
        held = hold(have)
        last = size - 2
        have[last] = after(have[last], held)
    return [hop(have[k - 1], "tensor", 1) if k % 2 else have[k] for k in range(size)]


def fold_order(keys, flip=False):
    bits = range(7, -1, -1) if flip else range(8)
    return sorted(keys, key=lambda k: tuple((k >> b) & 1 for b in bits))


def prologue_body(tok_in, cot_in, group, gate_t, routes_t, slots_t, *outs):
    normed_o, cot_hot_o, cot_cold_o, tok_hot_o, tok_cold_o, perm_o, pick0_o, pick1_o, link_o, gout_o, tok, cot, sems = outs
    half = tok.shape[0] // 2
    pairs = [(tok_in, tok), (cot_in, cot)]
    copies = [
        pltpu.make_async_copy(
            a.at[i * half : (i + 1) * half], b.at[i * half : (i + 1) * half], sems.at[2 * n + i]
        )
        for n, (a, b) in enumerate(pairs)
        for i in range(2)
    ]
    for c in copies:
        c.start()
    rows = tok.shape[0]
    places = pick0_o.shape[1]
    code_t = jnp.where(slots_t[...] >= 0, (routes_t[...] ^ group[0]) * CAP + slots_t[...], -1)
    packed = jnp.concatenate(
        [code_t.astype(f32), gate_t[...], jnp.zeros((4, rows), f32)], axis=0
    ).T
    code = packed[:, 0:2].astype(jnp.int32)
    gate = packed[:, 2:4]
    lane = lax.broadcasted_iota(jnp.int32, (rows, LANES), 1)
    wide0 = (code[:, 0:1] == lane).astype(f32)
    wide1 = (code[:, 1:2] == lane).astype(f32)
    kept0 = (code[:, 0:1] >= 0).astype(f32)
    prim = wide0 + wide1 * (1.0 - kept0)
    plain = 1.0 - jnp.sum(prim, axis=1, keepdims=True)
    open_at = 1.0 - jnp.sum(prim, axis=0, keepdims=True)
    ri = lax.broadcasted_iota(jnp.int32, (rows, rows), 0)
    ci = lax.broadcasted_iota(jnp.int32, (rows, rows), 1)
    row_rank = dot(
        (ci < ri).astype(bf16), jnp.broadcast_to(plain, (rows, rows)).astype(bf16)
    )
    place_rank = dot(
        jnp.broadcast_to(open_at, (rows, rows)).astype(bf16), (ri < ci).astype(bf16)
    )
    filler = plain * open_at * (row_rank == place_rank).astype(f32)
    perm = (prim + filler).astype(bf16)
    perm_o[...] = perm
    for c in copies:
        c.wait()
    normal, _ = norm_parts(tok[...])
    normed_o[...] = dot_tn(perm, normal.astype(bf16)).astype(bf16)
    for source, hot_o, cold_o in ((cot, cot_hot_o, cot_cold_o), (tok, tok_hot_o, tok_cold_o)):
        moved = dot_tn(perm, source[...]).astype(bf16)
        hot_o[...] = moved[:places]
        cold_o[...] = moved[places:]
    pick0 = wide0.astype(bf16)
    pick1 = wide1.astype(bf16)
    pick0_o[...] = pick0[:, :places]
    pick1_o[...] = pick1[:, :places]
    link_o[...] = dot_tn((pick0 + pick1), prim.astype(bf16))[:places, :places].astype(bf16)
    upstream = cot[...].astype(f32)
    g0 = (gate[:, 0:1] * upstream).astype(bf16)
    g1 = (gate[:, 1:2] * upstream).astype(bf16)
    gout_o[...] = (dot_tn(pick0, g0) + dot_tn(pick1, g1))[:places].astype(bf16)


def make_prep(heads, size):
    def body(w, p, wo, po):
        wo[...] = jnp.zeros_like(wo)
        po[...] = jnp.zeros_like(po)
        for h in range(heads):
            for i in range(3):
                at = (3 * h + i) * LANES
                wo[at : at + size] = w[h, i * size : (i + 1) * size]
            po[h * LANES : h * LANES + size] = p[h]

    return body


def spare_lanes(dims, size):
    lane = lax.broadcasted_iota(jnp.int32, dims, 1) % LANES
    return (lane >= size) & (lane < size + 3)


def with_term(rows, term, size):
    lane = lax.broadcasted_iota(jnp.int32, rows.shape, 1)
    first = term.astype(bf16).astype(f32)
    second = (term - first).astype(bf16).astype(f32)
    third = term - first - second
    term = jnp.where(lane == size, first, jnp.where(lane == size + 1, second, third))
    return jnp.where(spare_lanes(rows.shape, size), term, rows.astype(f32)).astype(bf16)


def project(rows, weights, heads, size, scale):
    raw = dot_nt(rows, weights)
    part = lax.broadcasted_iota(jnp.int32, raw.shape, 1) // LANES % 3
    factor = jnp.where(part == 0, scale * LOG2E, 1.0)
    ones = ((part != 0) & spare_lanes(raw.shape, size)).astype(f32)
    return (raw * factor + ones).astype(bf16)


def attend(queries, keys, values, size):
    raised = jnp.exp2(dot_nt(queries, keys))
    total = jnp.sum(raised, axis=-1, keepdims=True)
    shares = raised * (1.0 / total)
    return dot(shares.astype(bf16), values).astype(bf16), with_term(queries, -jnp.log2(total), size)


def part_of(ref, rows, which, head):
    at = (3 * head + which) * LANES
    return ref[rows, at : at + LANES]


def pieces_of(ref, first, count, every, lo, hi, at):
    return jnp.concatenate(
        [ref[(first + k) * every + lo : (first + k) * every + hi, at] for k in range(count)], axis=0
    )


def make_half(count, heads, size, scale):
    def body(*refs):
        shards, (weights, qkv, fn_t, fn, sems) = refs[:count], refs[count:]
        rows = shards[0].shape[0]
        pull([(shards[k], fn.at[k * rows : (k + 1) * rows]) for k in range(count)], sems)
        for k in range(count):
            at = slice(k * rows, (k + 1) * rows)
            fn_t[:, at] = fn[at, :].T
        step = block_of(fn.shape[0])

        def chunk(i, _):
            at = pl.ds(pl.multiple_of(i * step, 16), step)
            qkv[at, :] = project(fn[at, :], weights[...], heads, size, scale)
            return 0

        lax.fori_loop(0, fn.shape[0] // step, chunk, 0)

    return body


def make_turn(count):
    def body(*refs):
        shards, fn_t = refs[:count], refs[count]
        rows = shards[0].shape[0]
        for k in range(count):
            fn_t[:, k * rows : (k + 1) * rows] = shards[k][...].T

    return body


def make_front(count, places, heads, size, scale):
    def body(*refs):
        half = count // 2
        shards, (first, weights, proj) = refs[:half], refs[half : half + 3]
        qkv, ctx, ask, even, odd, fn, sems = refs[half + 3 :]
        rows = shards[0].shape[0]
        pull([(shards[k], fn.at[k * rows : (k + 1) * rows]) for k in range(half)], sems)
        done = first.shape[0]
        qkv[:done] = first[...]
        step = block_of(fn.shape[0])

        def chunk(i, _):
            at = pl.ds(pl.multiple_of(i * step, 16), step)
            to = pl.ds(pl.multiple_of(done + i * step, 16), step)
            qkv[to, :] = project(fn[at, :], weights[...], heads, size, scale)
            return 0

        lax.fori_loop(0, fn.shape[0] // step, chunk, 0)
        every = slice(None)
        for h in range(heads):
            cut = slice(h * LANES, (h + 1) * LANES)
            queries = pieces_of(
                qkv, 0, count, rows, 0, places, slice(3 * h * LANES, (3 * h + 1) * LANES)
            )
            ctx[:, cut], ask[:, cut] = attend(
                queries, part_of(qkv, every, 1, h), part_of(qkv, every, 2, h), size
            )
        part = dot(ctx[...], proj[...]).astype(bf16)
        for i, k in enumerate(range(0, count, 2)):
            even[i * places : (i + 1) * places] = part[k * places : (k + 1) * places]
            odd[i * places : (i + 1) * places] = part[(k + 1) * places : (k + 2) * places]

    return body


def make_cold(count, places, heads, size):
    def body(qkv, proj, ctx, ask, even, odd):
        rows = qkv.shape[0] // count
        cold = rows - places
        every = slice(None)
        group = min(4, count)
        order = fold_order(range(0, count, 2))
        for first in range(0, count, group):
            at = slice(first * cold, (first + group) * cold)
            for h in range(heads):
                cut = slice(h * LANES, (h + 1) * LANES)
                queries = pieces_of(
                    qkv, first, group, rows, places, rows, slice(3 * h * LANES, (3 * h + 1) * LANES)
                )
                ctx[at, cut], ask[at, cut] = attend(
                    queries, part_of(qkv, every, 1, h), part_of(qkv, every, 2, h), size
                )
            part = dot(ctx[at, :], proj[...]).astype(bf16)
            for k in range(first, first + group):
                to = odd if k % 2 else even
                i = order.index(k // 2 * 2)
                to[i * cold : (i + 1) * cold] = part[(k - first) * cold : (k - first + 1) * cold]

    return body


def back_block(ask, keys, values, ctx, grad_ctx, size):
    shares = jnp.exp2(dot_nt(ask, keys))
    mix = jnp.sum(grad_ctx.astype(f32) * ctx.astype(f32), axis=-1, keepdims=True)
    grad_ctx = with_term(grad_ctx, -mix, size)
    grad_scores = (shares * dot_nt(grad_ctx, values)).astype(bf16)
    return (
        dot(grad_scores, keys),
        dot_tn(ask, grad_scores),
        dot_tn(grad_ctx, shares.astype(bf16)),
    )


def make_cold_back(count, places, heads, size, scale):
    def body(*refs):
        shards, (qkv, proj, ctx, ask) = refs[:count], refs[count : count + 4]
        gq, gk, gv, gp, cots, sems = refs[count + 4 :]
        cold = shards[0].shape[0]
        pull([(shards[k], cots.at[k * cold : (k + 1) * cold]) for k in range(count)], sems)
        every = slice(None)
        group = min(4, count)
        for first in range(0, count, group):
            at = slice(first * cold, (first + group) * cold)
            grad_ctx = dot_nt(cots[at, :], proj[...]).astype(bf16)
            proj_grad = dot_tn(ctx[at, :], cots[at, :])
            for h in range(heads):
                cut = slice(h * LANES, (h + 1) * LANES)
                a, b, c = back_block(
                    ask[at, cut],
                    part_of(qkv, every, 1, h),
                    part_of(qkv, every, 2, h),
                    ctx[at, cut],
                    grad_ctx[:, cut],
                    size,
                )
                gq[at, cut] = (a * scale).astype(bf16)
                if first:
                    gk[cut, :] += b
                    gv[cut, :] += c
                else:
                    gk[cut, :] = b
                    gv[cut, :] = c
            if first:
                gp[...] += proj_grad
            else:
                gp[...] = proj_grad

    return body


def make_hot_back(count, heads, size, groups, scale):
    def body(*refs):
        shards = refs[:count]
        place, qkv, proj, ctx, ask, gq, gk, gv, gp, fn_a, fn_b = refs[count : count + 11]
        outs = refs[count + 11 : count + 15]
        rows_t, grad_q, whole = refs[count + 15 :]
        grads = jnp.concatenate([s[...] for s in shards], axis=0)
        places = shards[0].shape[0]
        rows = qkv.shape[0] // count
        cold = rows - places
        grad_ctx = dot_nt(grads, proj[...]).astype(bf16)
        proj_grad = gp[...] + dot_tn(ctx[...], grads)
        base = heads * 3 * size
        every = slice(None)
        proj_rows = []
        for h in range(heads):
            cut = slice(h * LANES, (h + 1) * LANES)
            a, b, c = back_block(
                ask[:, cut],
                part_of(qkv, every, 1, h),
                part_of(qkv, every, 2, h),
                ctx[:, cut],
                grad_ctx[:, cut],
                size,
            )
            a = (a * scale).astype(bf16)
            for k in range(count):
                grad_q[k * rows : k * rows + places] = a[k * places : (k + 1) * places]
                grad_q[k * rows + places : (k + 1) * rows] = gq[k * cold : (k + 1) * cold, cut]
            at = h * 3 * size
            rows_t[at : at + size, :] = grad_q[...].T[:size]
            rows_t[at + size : at + 2 * size, :] = ((gk[cut, :] + b) * (1.0 / LOG2E))[
                :size
            ].astype(bf16)
            rows_t[at + 2 * size : at + 3 * size, :] = (gv[cut, :] + c)[:size].astype(bf16)
            proj_rows.append(proj_grad[h * LANES : h * LANES + size].astype(bf16))
        done = fn_a.shape[1]
        turned = rows_t[...].T
        whole[:, :base] = (dot(fn_a[...], turned[:done]) + dot(fn_b[...], turned[done:])).astype(
            bf16
        )
        whole[:, base:] = jnp.concatenate(proj_rows, axis=0).T
        each = whole.shape[0] // groups
        cuts = (0, near_rows(each), each)
        for n in range(2):
            size_n = cuts[n + 1] - cuts[n]
            for i, g in enumerate(fold_order(range(groups), n == 1)):
                at = pl.multiple_of((place[0] ^ g) * each + cuts[n], 16)
                to = outs[2 * n + i // (groups // 2)]
                i = i % (groups // 2)
                to[i * size_n : (i + 1) * size_n] = whole[pl.ds(at, size_n), :]

    return body


def near_rows(rows):
    return (rows // 2 + 15) // 16 * 16


def make_last(heads, size):
    def body(a, b, c, d, qkv_o, proj_o):
        total = jnp.concatenate([total_of([a, b]), total_of([c, d])], axis=0)
        base = heads * 3 * size
        turned = total[:, base:].T
        for h in range(heads):
            qkv_o[:, h, :] = total[:, h * 3 * size : (h + 1) * 3 * size]
            proj_o[h] = turned[h * size : (h + 1) * size]

    return body


def make_fold(count):
    def body(mine, theirs, *outs):
        rows = outs[0].shape[0]
        for i in range(count):
            at = slice(i * rows, (i + 1) * rows)
            outs[i][...] = (mine[at].astype(f32) + theirs[at].astype(f32)).astype(bf16)

    return body


def total_of(refs):
    total = refs[0][...].astype(f32)
    for r in refs[1:]:
        total = total + r[...].astype(f32)
    return total


def make_mid(count, groups):
    def body(*refs):
        parts, (tok, link, grads) = refs[:count], refs[count : count + 3]
        mid_o, normal_o, factor_o = refs[count + 3 : count + 6]
        outs = refs[count + 6 :]
        mid = (tok[...].astype(f32) + total_of(parts)).astype(bf16)
        normal, factor = norm_parts(mid)
        mid_o[...] = mid
        normal_o[...] = normal
        factor_o[...] = factor
        slot_in = dot(link[...], normal.astype(bf16))
        each = slot_in.shape[0] // groups
        for g in range(groups):
            at = slice(g * each, (g + 1) * each)
            both = jnp.concatenate([slot_in[at], grads[at].astype(f32)], axis=1)
            outs[g][...] = both.astype(bf16)

    return body


def slot_mask(rows, experts, e):
    row = lax.broadcasted_iota(jnp.int32, (rows, 1), 0)
    return (row // CAP) % experts == e


def make_expert(count, experts):
    def body(*refs):
        shards = refs[:count]
        up, down, arrived, grads, hid_o, pre_o, even, odd = refs[count:]
        width = arrived.shape[1]
        arrived[...] = jnp.concatenate([s[:, :width] for s in shards], axis=0)
        grads[...] = jnp.concatenate([s[:, width:] for s in shards], axis=0)
        rows = arrived.shape[0]
        forth = None
        back = None
        for e in range(experts):
            keep = slot_mask(rows, experts, e)
            pre = dot(arrived[...], up[e])
            cdf = 0.5 * (1.0 + lax.erf(pre * half_root))
            hidden = jnp.where(keep, pre * cdf, 0.0).astype(bf16)
            slope = cdf + pre * jnp.exp(-0.5 * pre * pre) * bell_scale
            grad_pre = jnp.where(keep, dot_nt(grads[...], down[e]) * slope, 0.0).astype(bf16)
            hid_o[e] = hidden
            pre_o[e] = grad_pre
            a = dot(hidden, down[e])
            b = dot_nt(grad_pre, up[e])
            forth = a if forth is None else forth + a
            back = b if back is None else back + b
        both = jnp.concatenate([back, forth], axis=1).astype(bf16)
        each = rows // count
        for k in range(count):
            to = odd if k % 2 else even
            to[(k // 2) * each : (k // 2 + 1) * each] = both[k * each : (k + 1) * each]

    return body


def make_weight_grads(experts):
    def body(arrived, grads, hidden, grad_pre, up_o, down_o):
        for e in range(experts):
            up_o[e] = dot_tn(arrived[...], grad_pre[e]).astype(bf16)
            down_o[e] = dot_tn(hidden[e], grads[...]).astype(bf16)

    return body


def make_split(count, groups):
    def body(*refs):
        parts, outs = refs[:count], refs[count:]
        total = total_of(parts)
        each = total.shape[0] // groups
        for g in range(groups):
            outs[g][...] = total[g * each : (g + 1) * each].astype(bf16)

    return body


def make_mid_back(groups):
    def body(*refs):
        parts = refs[:groups]
        link, cot, normal, factor, grad_o, expert_o = refs[groups:]
        both = jnp.concatenate([p[...].astype(f32) for p in parts], axis=0).astype(bf16)
        width = cot.shape[1]
        expert_o[...] = both[:, width:]
        grad_norm = dot_tn(link[...], both[:, :width])
        grad_o[...] = (
            cot[...].astype(f32) + norm_back(normal[...], factor[...], grad_norm)
        ).astype(bf16)

    return body


def make_epilogue(count):
    def body(*refs):
        parts = refs[:count]
        tok, mid_hot, perm, pick0, pick1, experts, gate_t, cot, out, gate_o = refs[count:]
        cold = (tok[...].astype(f32) + total_of(parts)).astype(bf16)
        ordered = jnp.concatenate([mid_hot[...], cold], axis=0)
        mid = dot(perm[...], ordered)
        gate = jnp.concatenate([gate_t[...], jnp.zeros((6, gate_t.shape[1]), f32)], axis=0).T
        first = dot(pick0[...], experts[...])
        second = dot(pick1[...], experts[...])
        out[...] = (mid + gate[:, 0:1] * first + gate[:, 1:2] * second).astype(bf16)
        upstream = cot[...].astype(f32)
        lane = lax.broadcasted_iota(jnp.int32, (upstream.shape[0], LANES), 1)
        one = jnp.sum(upstream * first, axis=-1, keepdims=True)
        two = jnp.sum(upstream * second, axis=-1, keepdims=True)
        gate_o[...] = jnp.where(lane == 0, one, two).T[:2]

    return body


def fold_scatter(even, odd, rows, name):
    count = lax.axis_size("tensor") // 2
    theirs = hop(odd, "tensor", 1)
    sums = run(
        make_fold(count), [shape((rows, even.shape[1]))] * count, [even, theirs], name
    )
    return [sums[0]] + [hop(sums[i], "tensor", 2 * i) for i in range(1, count)]


def halve(mine, theirs, name):
    half = (mine.shape[0] // 2, mine.shape[1])
    return run(make_fold(2), [shape(half), shape(half)], [mine, theirs], name)


def shards(
    tokens,
    cotangent,
    gate_weights,
    routes,
    slot_index,
    qkv_weight,
    proj_weight,
    up_weight,
    down_weight,
):
    rows, width = tokens.shape
    heads, size = qkv_weight.shape[1], qkv_weight.shape[2] // 3
    scale = size ** (-0.5)
    groups = lax.axis_size("dp")
    count = lax.axis_size("tensor")
    experts, _, hidden_dev = up_weight.shape
    each = experts * CAP
    places = groups * each
    cold = rows - places
    hot_all = count * places
    total = count * rows
    slots = count * places

    wqkv, proj = run(
        make_prep(heads, size),
        [shape((heads * 3 * LANES, width)), shape((heads * LANES, width))],
        [qkv_weight.transpose(1, 2, 0), proj_weight],
        "prep",
    )
    group = (lax.axis_index("dp") * experts).astype(jnp.int32).reshape(1)
    normed, cot_hot, cot_cold, tok_hot, tok_cold, perm, pick0, pick1, link, grad_out = run(
        prologue_body,
        [
            shape((rows, width)),
            shape((places, width)),
            shape((cold, width)),
            shape((places, width)),
            shape((cold, width)),
            shape((rows, rows)),
            shape((rows, places)),
            shape((rows, places)),
            shape((places, places)),
            shape((places, width)),
        ],
        [tokens, cotangent, group, gate_weights.T, routes.T, slot_index.T],
        "prologue",
        extra=57,
        smem=(2,),
        loose=2,
        scratch=[
            pltpu.VMEM((rows, width), bf16),
            pltpu.VMEM((rows, width), bf16),
            pltpu.SemaphoreType.DMA((4,)),
        ],
    )
    half = count // 2
    cots = {0: cot_cold, 1: hop(cot_cold, "tensor", 1)}
    def first_half(have):
        near = [
            hop(have[k - 1], "tensor", 1) if k % 2 else have[k] for k in range(half)
        ]
        return run(
            make_half(half, heads, size, scale),
            [shape((half * rows, heads * 3 * LANES)), shape((width, half * rows))],
            after(near, cots[1]) + [wqkv],
            "half",
        extra=6,
        moved=1024,
            loose=half,
            scratch=[
                pltpu.VMEM((half * rows, width), bf16),
                pltpu.SemaphoreType.DMA((half,)),
            ],
        )

    box = []

    def hold(have):
        box.append((have, first_half(have)))
        return box[0][1]

    normed_all = gather_rel(normed, hold)
    have, (qkv_a, fn_a) = box[0]

    far = count // 2
    qkv, ctx_hot, ask_hot, even, odd = run(
        make_front(count, places, heads, size, scale),
        [
            shape((total, heads * 3 * LANES)),
            shape((hot_all, heads * LANES)),
            shape((hot_all, heads * LANES)),
            shape((hot_all // 2, width)),
            shape((hot_all // 2, width)),
        ],
        normed_all[half:] + [qkv_a, wqkv, proj],
        "front",
        extra=8,
        moved=1024,
        loose=half,
        scratch=[
            pltpu.VMEM((half * rows, width), bf16),
            pltpu.SemaphoreType.DMA((half,)),
        ],
    )
    hot_sums = fold_scatter(even, odd, places, "fold_hot")
    start, mask = after(cot_cold, have[count - 2]), far
    while mask > 1:
        cots[mask] = hop(start, "tensor", mask)
        mask //= 2
    hot_sums = after(hot_sums, list(cots.values()))

    outs = run(
        make_mid(count // 2, groups),
        [shape((places, width)), shape((places, width), f32), shape((places, 1), f32)]
        + [shape((each, 2 * width))] * groups,
        hot_sums + [tok_hot, link, grad_out],
        "mid_hot",
    )
    mid_hot, normal_hot, factor_hot = outs[:3]
    pieces = outs[3:]

    ctx_cold, ask_cold, even_cold, odd_cold = run(
        make_cold(count, places, heads, size),
        [
            shape((count * cold, heads * LANES)),
            shape((count * cold, heads * LANES)),
        ]
        + [shape((half * cold, width))] * 2,
        [after(qkv, mid_hot), proj],
        "cold",
        extra=14,
        flops=4 * total * total * heads * LANES,
    )
    start, mask = {k: after(y, mid_hot) for k, y in cots.items()}, far // 2
    early = [k for k in cots if k and k % 2 == 0]
    while mask > 1:
        for k in list(cots):
            if k % 2 == 0 and k > mask and k ^ mask not in cots:
                start[k ^ mask] = cots[k ^ mask] = hop(start[k], "tensor", mask)
        mask //= 2
    landed = jnp.concatenate(
        [pieces[0]] + [hop(pieces[g], "dp", g) for g in range(1, groups)], axis=0
    )
    landed = after(landed, ctx_cold, list(cots.values()))
    arrived_all = gather_rel(landed, direct=True)
    for k in early:
        cots[k + 1] = hop(after(cots[k], arrived_all), "tensor", 1)
    cold_theirs = hop(after(odd_cold, arrived_all), "tensor", 1)
    arrived, slot_grads, hidden, grad_pre, even, odd = run(
        make_expert(count, experts),
        [
            shape((slots, width)),
            shape((slots, width)),
            shape((experts, slots, hidden_dev)),
            shape((experts, slots, hidden_dev)),
            shape((slots // 2, 2 * width)),
            shape((slots // 2, 2 * width)),
        ],
        arrived_all + [up_weight, down_weight],
        "experts",
        extra=8,
        flops=6 * slots * width * hidden_dev * experts,
    )
    cold_mine, cold_send = halve(even_cold, cold_theirs, "fold_cold_1")
    sums = fold_scatter(even, after(odd, list(cots.values()), cold_mine), places, "fold_slots")
    cold_theirs = hop(after(cold_send, sums[0]), "tensor", 2)
    for k in range(1, count, 2):
        if k not in cots:
            cots[k] = hop(after(cots[k - 1], arrived_all), "tensor", 1)
    cot_all = [cots[k] for k in range(count)]
    gq, gk, gv, gp = run(
        make_cold_back(count, places, heads, size, scale),
        [
            shape((count * cold, heads * LANES)),
            shape((heads * LANES, total), f32),
            shape((heads * LANES, total), f32),
            shape((heads * LANES, width), f32),
        ],
        cot_all + [after(qkv, sums[0]), proj, ctx_cold, ask_cold],
        "cold_back",
        extra=16,
        flops=1e10,
        loose=count,
        scratch=[
            pltpu.VMEM((count * cold, width), bf16),
            pltpu.SemaphoreType.DMA((count,)),
        ],
    )
    sums = after(sums, gp)

    pieces = run(
        make_split(count // 2, groups),
        [shape((each, 2 * width))] * groups,
        sums,
        "split_slots",
    )
    back = [pieces[0]] + [hop(pieces[g], "dp", g) for g in range(1, groups)]
    back = after(back, cold_theirs)
    grad_hot, expert_out = run(
        make_mid_back(groups),
        [shape((places, width)), shape((places, width))],
        back + [link, cot_hot, normal_hot, factor_hot],
        "mid_back",
    )
    box.clear()

    def turn(_):
        box.append(
            run(
                make_turn(half),
                [shape((width, half * rows))],
                after(normed_all[half:], grad_hot),
                "turn",
        extra=3,
            )[0]
        )
        return box[0]

    grad_hot_all = gather_rel(grad_hot, turn, direct=True)
    fn_b = box[0]
    cold_mine = after(cold_mine, grad_hot)
    mask = 4
    while mask < count:
        cold_mine, cold_send = halve(cold_mine, cold_theirs, f"fold_cold_{mask // 2}")
        cold_theirs = hop(cold_send, "tensor", mask)
        mask *= 2
    cold_sums = [cold_mine, cold_theirs]

    me = lax.axis_index("dp").astype(jnp.int32).reshape(1)
    each_w = width // groups
    first_w = near_rows(each_w)
    halves = [(groups // 2 * n, heads * 4 * size) for n in (first_w, each_w - first_w)]
    keep_a, send_a, keep_b, send_b = run(
        make_hot_back(count, heads, size, groups, scale),
        [shape(halves[0]), shape(halves[0]), shape(halves[1]), shape(halves[1])],
        after(grad_hot_all, cold_mine)
        + [me, qkv, proj, ctx_hot, ask_hot, gq, gk, gv, gp, fn_a, fn_b],
        "hot_back",
        extra=10,
        moved=1024,
        smem=(count,),
        scratch=[
            pltpu.VMEM((heads * 3 * size, total), bf16),
            pltpu.VMEM((total, LANES), bf16),
            pltpu.VMEM((width, heads * 4 * size), bf16),
        ],
    )
    grad_up, grad_down = run(
        make_weight_grads(experts),
        [shape(up_weight.shape), shape(down_weight.shape)],
        [after(arrived, keep_a), slot_grads, hidden, grad_pre],
        "weight_grads",
        extra=10,
        moved=1024,
    )
    mask = 1
    while True:
        got_a = hop(send_a, "dp", mask)
        got_b = hop(send_b, "dp", groups // 2 // mask)
        if mask == 1:
            got_a, got_b = after((got_a, got_b), grad_up)
        if mask == groups // 2:
            break
        keep_a, send_a = halve(keep_a, got_a, f"fold_a_{mask}")
        keep_b, send_b = halve(keep_b, got_b, f"fold_b_{mask}")
        mask *= 2
    parts = [keep_a, got_a, keep_b, got_b]
    layer_out, gate_grad = run(
        make_epilogue(2),
        [shape((rows, width)), shape((2, rows), f32)],
        cold_sums
        + [tok_cold, mid_hot, perm, pick0, pick1, expert_out, gate_weights.T, cotangent],
        "epilogue",
        extra=4,
    )
    grad_qkv, grad_proj = run(
        make_last(heads, size),
        [shape((width // groups, heads, 3 * size), f32), shape((heads, size, width // groups), f32)],
        after(parts, layer_out, grad_up),
        "last",
        extra=6,
    )
    return (layer_out, gate_grad.T, grad_qkv, grad_proj, grad_up, grad_down)


def solution(mesh):
    return jax.shard_map(
        shards,
        mesh=mesh,
        in_specs=(
            P(("dp", "tensor"), None),
            P(("dp", "tensor"), None),
            P(("dp", "tensor"), None),
            P(("dp", "tensor"), None),
            P(("dp", "tensor"), None),
            P(None, "tensor", None),
            P("tensor", None, None),
            P("dp", None, "tensor"),
            P("dp", "tensor", None),
        ),
        out_specs=(
            P(("dp", "tensor"), None),
            P(("dp", "tensor"), None),
            P("dp", "tensor", None),
            P("tensor", None, "dp"),
            P("dp", None, "tensor"),
            P("dp", "tensor", None),
        ),
        check_vma=False,
    )
```

```python
import math

import jax
import jax.numpy as jnp
from jax import lax
from jax.experimental import pallas as pl
from jax.experimental.pallas import tpu as pltpu
from jax.sharding import PartitionSpec as P

CAP = 2
LANES = 128
epsilon = 1e-06
half_root = 1.0 / math.sqrt(2.0)
bell_scale = 1.0 / math.sqrt(2.0 * math.pi)
LOG2E = math.log2(math.e)
f32 = jnp.float32
bf16 = jnp.bfloat16


def norm_parts(row_block):
    widened = row_block.astype(f32)
    center = widened - jnp.mean(widened, axis=-1, keepdims=True)
    factor = lax.rsqrt(jnp.mean(center * center, axis=-1, keepdims=True) + epsilon)
    return (center * factor, factor)


def norm_back(normal_rows, factor, upstream):
    mean_up = jnp.mean(upstream, axis=-1, keepdims=True)
    mean_mix = jnp.mean(upstream * normal_rows, axis=-1, keepdims=True)
    return factor * (upstream - mean_up - normal_rows * mean_mix)


def dot(a, b):
    return lax.dot_general(a, b, (((1,), (0,)), ((), ())), preferred_element_type=f32)


def dot_nt(a, b):
    return lax.dot_general(a, b, (((1,), (1,)), ((), ())), preferred_element_type=f32)


def dot_tn(a, b):
    return lax.dot_general(a, b, (((0,), (0,)), ((), ())), preferred_element_type=f32)


def run(body, outs, ins, name, flops=0, extra=1, moved=None, smem=(), loose=0, scratch=()):
    specs = [
        pl.BlockSpec(
            memory_space=pl.ANY if i < loose else pltpu.SMEM if i in smem else pltpu.VMEM
        )
        for i in range(len(ins))
    ]
    sizes = [math.prod(x.shape) * x.dtype.itemsize for x in list(ins)[loose:] + list(outs)]
    sizes += [math.prod(x.shape) * x.dtype.itemsize for x in scratch if x.dtype in (f32, bf16)]
    limit = int(sum(sizes) * 1.2) + extra * 2**20
    return pl.pallas_call(
        body,
        out_shape=list(outs),
        in_specs=specs,
        out_specs=[pl.BlockSpec(memory_space=pltpu.VMEM)] * len(outs),
        scratch_shapes=list(scratch),
        compiler_params=pltpu.CompilerParams(vmem_limit_bytes=limit),
        cost_estimate=pl.CostEstimate(
            flops=int(flops), bytes_accessed=int(sum(sizes) if moved is None else moved), transcendentals=0
        ),
        name=name,
    )(*ins)


def after(x, *others):
    return lax.optimization_barrier((x, others))[0]


def pull(pairs, sems):
    copies = [pltpu.make_async_copy(a, b, sems.at[i]) for i, (a, b) in enumerate(pairs)]
    for c in copies:
        c.start()
    for c in copies:
        c.wait()


def shape(dims, dtype=bf16):
    return jax.ShapeDtypeStruct(tuple(dims), dtype)


def block_of(rows, most=256):
    return max(b for b in range(16, most + 1, 16) if rows % b == 0)


def hop(x, axis, mask):
    size = lax.axis_size(axis)
    return lax.ppermute(x, axis, [(i, i ^ mask) for i in range(size)])


def gather_rel(x, hold=None, firm=(), direct=False):
    size = lax.axis_size("tensor")
    have = {0: x}
    odd = {}
    mask = size // 2
    if direct:
        have.update({k: hop(x, "tensor", k) for k in range(2, size, 2)})
    while mask > 1 and not direct:
        have.update({k ^ mask: hop(y, "tensor", mask) for k, y in list(have.items())})
        mask //= 2
    if hold is not None:
        held = hold(have)
        last = size - 2
        have[last] = after(have[last], held)
    return [hop(have[k - 1], "tensor", 1) if k % 2 else have[k] for k in range(size)]


def fold_order(keys, flip=False):
    bits = range(7, -1, -1) if flip else range(8)
    return sorted(keys, key=lambda k: tuple((k >> b) & 1 for b in bits))


def prologue_body(tok_in, cot_in, group, gate_t, routes_t, slots_t, *outs):
    normed_o, cot_hot_o, cot_cold_o, tok_hot_o, tok_cold_o, perm_o, pick0_o, pick1_o, link_o, gout_o, tok, cot, sems = outs
    half = tok.shape[0] // 2
    pairs = [(tok_in, tok), (cot_in, cot)]
    copies = [
        pltpu.make_async_copy(
            a.at[i * half : (i + 1) * half], b.at[i * half : (i + 1) * half], sems.at[2 * n + i]
        )
        for n, (a, b) in enumerate(pairs)
        for i in range(2)
    ]
    for c in copies:
        c.start()
    rows = tok.shape[0]
    places = pick0_o.shape[1]
    code_t = jnp.where(slots_t[...] >= 0, (routes_t[...] ^ group[0]) * CAP + slots_t[...], -1)
    packed = jnp.concatenate(
        [code_t.astype(f32), gate_t[...], jnp.zeros((4, rows), f32)], axis=0
    ).T
    code = packed[:, 0:2].astype(jnp.int32)
    gate = packed[:, 2:4]
    lane = lax.broadcasted_iota(jnp.int32, (rows, LANES), 1)
    wide0 = (code[:, 0:1] == lane).astype(f32)
    wide1 = (code[:, 1:2] == lane).astype(f32)
    kept0 = (code[:, 0:1] >= 0).astype(f32)
    prim = wide0 + wide1 * (1.0 - kept0)
    plain = 1.0 - jnp.sum(prim, axis=1, keepdims=True)
    open_at = 1.0 - jnp.sum(prim, axis=0, keepdims=True)
    ri = lax.broadcasted_iota(jnp.int32, (rows, rows), 0)
    ci = lax.broadcasted_iota(jnp.int32, (rows, rows), 1)
    row_rank = dot(
        (ci < ri).astype(bf16), jnp.broadcast_to(plain, (rows, rows)).astype(bf16)
    )
    place_rank = dot(
        jnp.broadcast_to(open_at, (rows, rows)).astype(bf16), (ri < ci).astype(bf16)
    )
    filler = plain * open_at * (row_rank == place_rank).astype(f32)
    perm = (prim + filler).astype(bf16)
    perm_o[...] = perm
    for c in copies:
        c.wait()
    normal, _ = norm_parts(tok[...])
    normed_o[...] = dot_tn(perm, normal.astype(bf16)).astype(bf16)
    for source, hot_o, cold_o in ((cot, cot_hot_o, cot_cold_o), (tok, tok_hot_o, tok_cold_o)):
        moved = dot_tn(perm, source[...]).astype(bf16)
        hot_o[...] = moved[:places]
        cold_o[...] = moved[places:]
    pick0 = wide0.astype(bf16)
    pick1 = wide1.astype(bf16)
    pick0_o[...] = pick0[:, :places]
    pick1_o[...] = pick1[:, :places]
    link_o[...] = dot_tn((pick0 + pick1), prim.astype(bf16))[:places, :places].astype(bf16)
    upstream = cot[...].astype(f32)
    g0 = (gate[:, 0:1] * upstream).astype(bf16)
    g1 = (gate[:, 1:2] * upstream).astype(bf16)
    gout_o[...] = (dot_tn(pick0, g0) + dot_tn(pick1, g1))[:places].astype(bf16)


def make_prep(heads, size):
    def body(w, p, wo, po):
        wo[...] = jnp.zeros_like(wo)
        po[...] = jnp.zeros_like(po)
        for h in range(heads):
            for i in range(3):
                at = (3 * h + i) * LANES
                wo[at : at + size] = w[h, i * size : (i + 1) * size]
            po[h * LANES : h * LANES + size] = p[h]

    return body


def spare_lanes(dims, size):
    lane = lax.broadcasted_iota(jnp.int32, dims, 1) % LANES
    return (lane >= size) & (lane < size + 3)


def with_term(rows, term, size):
    lane = lax.broadcasted_iota(jnp.int32, rows.shape, 1)
    first = term.astype(bf16).astype(f32)
    second = (term - first).astype(bf16).astype(f32)
    third = term - first - second
    term = jnp.where(lane == size, first, jnp.where(lane == size + 1, second, third))
    return jnp.where(spare_lanes(rows.shape, size), term, rows.astype(f32)).astype(bf16)


def project(rows, weights, heads, size, scale):
    raw = dot_nt(rows, weights)
    part = lax.broadcasted_iota(jnp.int32, raw.shape, 1) // LANES % 3
    factor = jnp.where(part == 0, scale * LOG2E, 1.0)
    ones = ((part != 0) & spare_lanes(raw.shape, size)).astype(f32)
    return (raw * factor + ones).astype(bf16)


def attend(queries, keys, values, size):
    raised = jnp.exp2(dot_nt(queries, keys))
    total = jnp.sum(raised, axis=-1, keepdims=True)
    shares = raised * (1.0 / total)
    return dot(shares.astype(bf16), values).astype(bf16), with_term(queries, -jnp.log2(total), size)


def part_of(ref, rows, which, head):
    at = (3 * head + which) * LANES
    return ref[rows, at : at + LANES]


def pieces_of(ref, first, count, every, lo, hi, at):
    return jnp.concatenate(
        [ref[(first + k) * every + lo : (first + k) * every + hi, at] for k in range(count)], axis=0
    )


def make_half(count, heads, size, scale):
    def body(*refs):
        shards, (weights, qkv, fn_t, fn, sems) = refs[:count], refs[count:]
        rows = shards[0].shape[0]
        pull([(shards[k], fn.at[k * rows : (k + 1) * rows]) for k in range(count)], sems)
        for k in range(count):
            at = slice(k * rows, (k + 1) * rows)
            fn_t[:, at] = fn[at, :].T
        step = block_of(fn.shape[0])

        def chunk(i, _):
            at = pl.ds(pl.multiple_of(i * step, 16), step)
            qkv[at, :] = project(fn[at, :], weights[...], heads, size, scale)
            return 0

        lax.fori_loop(0, fn.shape[0] // step, chunk, 0)

    return body


def make_turn(count):
    def body(*refs):
        shards, fn_t = refs[:count], refs[count]
        rows = shards[0].shape[0]
        for k in range(count):
            fn_t[:, k * rows : (k + 1) * rows] = shards[k][...].T

    return body


def make_front(count, places, heads, size, scale):
    def body(*refs):
        half = count // 2
        shards, (first, weights, proj) = refs[:half], refs[half : half + 3]
        qkv, ctx, ask, even, odd, fn, sems = refs[half + 3 :]
        rows = shards[0].shape[0]
        pull([(shards[k], fn.at[k * rows : (k + 1) * rows]) for k in range(half)], sems)
        done = first.shape[0]
        qkv[:done] = first[...]
        step = block_of(fn.shape[0])

        def chunk(i, _):
            at = pl.ds(pl.multiple_of(i * step, 16), step)
            to = pl.ds(pl.multiple_of(done + i * step, 16), step)
            qkv[to, :] = project(fn[at, :], weights[...], heads, size, scale)
            return 0

        lax.fori_loop(0, fn.shape[0] // step, chunk, 0)
        every = slice(None)
        for h in range(heads):
            cut = slice(h * LANES, (h + 1) * LANES)
            queries = pieces_of(
                qkv, 0, count, rows, 0, places, slice(3 * h * LANES, (3 * h + 1) * LANES)
            )
            ctx[:, cut], ask[:, cut] = attend(
                queries, part_of(qkv, every, 1, h), part_of(qkv, every, 2, h), size
            )
        part = dot(ctx[...], proj[...]).astype(bf16)
        for i, k in enumerate(range(0, count, 2)):
            even[i * places : (i + 1) * places] = part[k * places : (k + 1) * places]
            odd[i * places : (i + 1) * places] = part[(k + 1) * places : (k + 2) * places]

    return body


def make_cold(count, places, heads, size):
    def body(qkv, proj, ctx, ask, even, odd):
        rows = qkv.shape[0] // count
        cold = rows - places
        every = slice(None)
        group = min(4, count)
        order = fold_order(range(0, count, 2))
        for first in range(0, count, group):
            at = slice(first * cold, (first + group) * cold)
            for h in range(heads):
                cut = slice(h * LANES, (h + 1) * LANES)
                queries = pieces_of(
                    qkv, first, group, rows, places, rows, slice(3 * h * LANES, (3 * h + 1) * LANES)
                )
                ctx[at, cut], ask[at, cut] = attend(
                    queries, part_of(qkv, every, 1, h), part_of(qkv, every, 2, h), size
                )
            part = dot(ctx[at, :], proj[...]).astype(bf16)
            for k in range(first, first + group):
                to = odd if k % 2 else even
                i = order.index(k // 2 * 2)
                to[i * cold : (i + 1) * cold] = part[(k - first) * cold : (k - first + 1) * cold]

    return body


def back_block(ask, keys, values, ctx, grad_ctx, size):
    shares = jnp.exp2(dot_nt(ask, keys))
    mix = jnp.sum(grad_ctx.astype(f32) * ctx.astype(f32), axis=-1, keepdims=True)
    grad_ctx = with_term(grad_ctx, -mix, size)
    grad_scores = (shares * dot_nt(grad_ctx, values)).astype(bf16)
    return (
        dot(grad_scores, keys),
        dot_tn(ask, grad_scores),
        dot_tn(grad_ctx, shares.astype(bf16)),
    )


def make_cold_back(count, places, heads, size, scale):
    def body(*refs):
        shards, (qkv, proj, ctx, ask) = refs[:count], refs[count : count + 4]
        gq, gk, gv, gp, cots, sems = refs[count + 4 :]
        cold = shards[0].shape[0]
        pull([(shards[k], cots.at[k * cold : (k + 1) * cold]) for k in range(count)], sems)
        every = slice(None)
        group = min(4, count)
        for first in range(0, count, group):
            at = slice(first * cold, (first + group) * cold)
            grad_ctx = dot_nt(cots[at, :], proj[...]).astype(bf16)
            proj_grad = dot_tn(ctx[at, :], cots[at, :])
            for h in range(heads):
                cut = slice(h * LANES, (h + 1) * LANES)
                a, b, c = back_block(
                    ask[at, cut],
                    part_of(qkv, every, 1, h),
                    part_of(qkv, every, 2, h),
                    ctx[at, cut],
                    grad_ctx[:, cut],
                    size,
                )
                gq[at, cut] = (a * scale).astype(bf16)
                if first:
                    gk[cut, :] += b
                    gv[cut, :] += c
                else:
                    gk[cut, :] = b
                    gv[cut, :] = c
            if first:
                gp[...] += proj_grad
            else:
                gp[...] = proj_grad

    return body


def make_hot_back(count, heads, size, groups, scale):
    def body(*refs):
        shards = refs[:count]
        place, qkv, proj, ctx, ask, gq, gk, gv, gp, fn_a, fn_b = refs[count : count + 11]
        outs = refs[count + 11 : count + 15]
        rows_t, grad_q, whole = refs[count + 15 :]
        grads = jnp.concatenate([s[...] for s in shards], axis=0)
        places = shards[0].shape[0]
        rows = qkv.shape[0] // count
        cold = rows - places
        grad_ctx = dot_nt(grads, proj[...]).astype(bf16)
        proj_grad = gp[...] + dot_tn(ctx[...], grads)
        base = heads * 3 * size
        every = slice(None)
        proj_rows = []
        for h in range(heads):
            cut = slice(h * LANES, (h + 1) * LANES)
            a, b, c = back_block(
                ask[:, cut],
                part_of(qkv, every, 1, h),
                part_of(qkv, every, 2, h),
                ctx[:, cut],
                grad_ctx[:, cut],
                size,
            )
            a = (a * scale).astype(bf16)
            for k in range(count):
                grad_q[k * rows : k * rows + places] = a[k * places : (k + 1) * places]
                grad_q[k * rows + places : (k + 1) * rows] = gq[k * cold : (k + 1) * cold, cut]
            at = h * 3 * size
            rows_t[at : at + size, :] = grad_q[...].T[:size]
            rows_t[at + size : at + 2 * size, :] = ((gk[cut, :] + b) * (1.0 / LOG2E))[
                :size
            ].astype(bf16)
            rows_t[at + 2 * size : at + 3 * size, :] = (gv[cut, :] + c)[:size].astype(bf16)
            proj_rows.append(proj_grad[h * LANES : h * LANES + size].astype(bf16))
        done = fn_a.shape[1]
        turned = rows_t[...].T
        whole[:, :base] = (dot(fn_a[...], turned[:done]) + dot(fn_b[...], turned[done:])).astype(
            bf16
        )
        whole[:, base:] = jnp.concatenate(proj_rows, axis=0).T
        each = whole.shape[0] // groups
        cuts = (0, near_rows(each), each)
        for n in range(2):
            size_n = cuts[n + 1] - cuts[n]
            for i, g in enumerate(fold_order(range(groups), n == 1)):
                at = pl.multiple_of((place[0] ^ g) * each + cuts[n], 16)
                to = outs[2 * n + i // (groups // 2)]
                i = i % (groups // 2)
                to[i * size_n : (i + 1) * size_n] = whole[pl.ds(at, size_n), :]

    return body


def near_rows(rows):
    return (rows // 2 + 15) // 16 * 16


def make_last(heads, size):
    def body(a, b, c, d, qkv_o, proj_o):
        total = jnp.concatenate([total_of([a, b]), total_of([c, d])], axis=0)
        base = heads * 3 * size
        turned = total[:, base:].T
        for h in range(heads):
            qkv_o[:, h, :] = total[:, h * 3 * size : (h + 1) * 3 * size]
            proj_o[h] = turned[h * size : (h + 1) * size]

    return body


def make_fold(count):
    def body(mine, theirs, *outs):
        rows = outs[0].shape[0]
        for i in range(count):
            at = slice(i * rows, (i + 1) * rows)
            outs[i][...] = (mine[at].astype(f32) + theirs[at].astype(f32)).astype(bf16)

    return body


def total_of(refs):
    total = refs[0][...].astype(f32)
    for r in refs[1:]:
        total = total + r[...].astype(f32)
    return total


def make_mid(count, groups):
    def body(*refs):
        parts, (tok, link, grads) = refs[:count], refs[count : count + 3]
        mid_o, normal_o, factor_o = refs[count + 3 : count + 6]
        outs = refs[count + 6 :]
        mid = (tok[...].astype(f32) + total_of(parts)).astype(bf16)
        normal, factor = norm_parts(mid)
        mid_o[...] = mid
        normal_o[...] = normal
        factor_o[...] = factor
        slot_in = dot(link[...], normal.astype(bf16))
        each = slot_in.shape[0] // groups
        for g in range(groups):
            at = slice(g * each, (g + 1) * each)
            both = jnp.concatenate([slot_in[at], grads[at].astype(f32)], axis=1)
            outs[g][...] = both.astype(bf16)

    return body


def slot_mask(rows, experts, e):
    row = lax.broadcasted_iota(jnp.int32, (rows, 1), 0)
    return (row // CAP) % experts == e


def make_expert(count, experts):
    def body(*refs):
        shards = refs[:count]
        up, down, arrived, grads, hid_o, pre_o, even, odd = refs[count:]
        width = arrived.shape[1]
        arrived[...] = jnp.concatenate([s[:, :width] for s in shards], axis=0)
        grads[...] = jnp.concatenate([s[:, width:] for s in shards], axis=0)
        rows = arrived.shape[0]
        forth = None
        back = None
        for e in range(experts):
            keep = slot_mask(rows, experts, e)
            pre = dot(arrived[...], up[e])
            cdf = 0.5 * (1.0 + lax.erf(pre * half_root))
            hidden = jnp.where(keep, pre * cdf, 0.0).astype(bf16)
            slope = cdf + pre * jnp.exp(-0.5 * pre * pre) * bell_scale
            grad_pre = jnp.where(keep, dot_nt(grads[...], down[e]) * slope, 0.0).astype(bf16)
            hid_o[e] = hidden
            pre_o[e] = grad_pre
            a = dot(hidden, down[e])
            b = dot_nt(grad_pre, up[e])
            forth = a if forth is None else forth + a
            back = b if back is None else back + b
        both = jnp.concatenate([back, forth], axis=1).astype(bf16)
        each = rows // count
        for k in range(count):
            to = odd if k % 2 else even
            to[(k // 2) * each : (k // 2 + 1) * each] = both[k * each : (k + 1) * each]

    return body


def make_weight_grads(experts):
    def body(arrived, grads, hidden, grad_pre, up_o, down_o):
        for e in range(experts):
            up_o[e] = dot_tn(arrived[...], grad_pre[e]).astype(bf16)
            down_o[e] = dot_tn(hidden[e], grads[...]).astype(bf16)

    return body


def make_split(count, groups):
    def body(*refs):
        parts, outs = refs[:count], refs[count:]
        total = total_of(parts)
        each = total.shape[0] // groups
        for g in range(groups):
            outs[g][...] = total[g * each : (g + 1) * each].astype(bf16)

    return body


def make_mid_back(groups):
    def body(*refs):
        parts = refs[:groups]
        link, cot, normal, factor, grad_o, expert_o = refs[groups:]
        both = jnp.concatenate([p[...].astype(f32) for p in parts], axis=0).astype(bf16)
        width = cot.shape[1]
        expert_o[...] = both[:, width:]
        grad_norm = dot_tn(link[...], both[:, :width])
        grad_o[...] = (
            cot[...].astype(f32) + norm_back(normal[...], factor[...], grad_norm)
        ).astype(bf16)

    return body


def make_epilogue(count):
    def body(*refs):
        parts = refs[:count]
        tok, mid_hot, perm, pick0, pick1, experts, gate_t, cot, out, gate_o = refs[count:]
        cold = (tok[...].astype(f32) + total_of(parts)).astype(bf16)
        ordered = jnp.concatenate([mid_hot[...], cold], axis=0)
        mid = dot(perm[...], ordered)
        gate = jnp.concatenate([gate_t[...], jnp.zeros((6, gate_t.shape[1]), f32)], axis=0).T
        first = dot(pick0[...], experts[...])
        second = dot(pick1[...], experts[...])
        out[...] = (mid + gate[:, 0:1] * first + gate[:, 1:2] * second).astype(bf16)
        upstream = cot[...].astype(f32)
        lane = lax.broadcasted_iota(jnp.int32, (upstream.shape[0], LANES), 1)
        one = jnp.sum(upstream * first, axis=-1, keepdims=True)
        two = jnp.sum(upstream * second, axis=-1, keepdims=True)
        gate_o[...] = jnp.where(lane == 0, one, two).T[:2]

    return body


def fold_scatter(even, odd, rows, name):
    count = lax.axis_size("tensor") // 2
    theirs = hop(odd, "tensor", 1)
    sums = run(
        make_fold(count), [shape((rows, even.shape[1]))] * count, [even, theirs], name
    )
    return [sums[0]] + [hop(sums[i], "tensor", 2 * i) for i in range(1, count)]


def halve(mine, theirs, name):
    half = (mine.shape[0] // 2, mine.shape[1])
    return run(make_fold(2), [shape(half), shape(half)], [mine, theirs], name)


def shards(
    tokens,
    cotangent,
    gate_weights,
    routes,
    slot_index,
    qkv_weight,
    proj_weight,
    up_weight,
    down_weight,
):
    rows, width = tokens.shape
    heads, size = qkv_weight.shape[1], qkv_weight.shape[2] // 3
    scale = size ** (-0.5)
    groups = lax.axis_size("dp")
    count = lax.axis_size("tensor")
    experts, _, hidden_dev = up_weight.shape
    each = experts * CAP
    places = groups * each
    cold = rows - places
    hot_all = count * places
    total = count * rows
    slots = count * places

    wqkv, proj = run(
        make_prep(heads, size),
        [shape((heads * 3 * LANES, width)), shape((heads * LANES, width))],
        [qkv_weight.transpose(1, 2, 0), proj_weight],
        "prep",
    )
    group = (lax.axis_index("dp") * experts).astype(jnp.int32).reshape(1)
    normed, cot_hot, cot_cold, tok_hot, tok_cold, perm, pick0, pick1, link, grad_out = run(
        prologue_body,
        [
            shape((rows, width)),
            shape((places, width)),
            shape((cold, width)),
            shape((places, width)),
            shape((cold, width)),
            shape((rows, rows)),
            shape((rows, places)),
            shape((rows, places)),
            shape((places, places)),
            shape((places, width)),
        ],
        [tokens, cotangent, group, gate_weights.T, routes.T, slot_index.T],
        "prologue",
        extra=57,
        smem=(2,),
        loose=2,
        scratch=[
            pltpu.VMEM((rows, width), bf16),
            pltpu.VMEM((rows, width), bf16),
            pltpu.SemaphoreType.DMA((4,)),
        ],
    )
    half = count // 2
    cots = {0: cot_cold, 1: hop(cot_cold, "tensor", 1)}
    def first_half(have):
        near = [
            hop(have[k - 1], "tensor", 1) if k % 2 else have[k] for k in range(half)
        ]
        return run(
            make_half(half, heads, size, scale),
            [shape((half * rows, heads * 3 * LANES)), shape((width, half * rows))],
            after(near, cots[1]) + [wqkv],
            "half",
        extra=6,
        moved=1024,
            loose=half,
            scratch=[
                pltpu.VMEM((half * rows, width), bf16),
                pltpu.SemaphoreType.DMA((half,)),
            ],
        )

    box = []

    def hold(have):
        box.append((have, first_half(have)))
        return box[0][1]

    normed_all = gather_rel(normed, hold)
    have, (qkv_a, fn_a) = box[0]

    far = count // 2
    qkv, ctx_hot, ask_hot, even, odd = run(
        make_front(count, places, heads, size, scale),
        [
            shape((total, heads * 3 * LANES)),
            shape((hot_all, heads * LANES)),
            shape((hot_all, heads * LANES)),
            shape((hot_all // 2, width)),
            shape((hot_all // 2, width)),
        ],
        normed_all[half:] + [qkv_a, wqkv, proj],
        "front",
        extra=8,
        moved=1024,
        loose=half,
        scratch=[
            pltpu.VMEM((half * rows, width), bf16),
            pltpu.SemaphoreType.DMA((half,)),
        ],
    )
    hot_sums = fold_scatter(even, odd, places, "fold_hot")
    start, mask = after(cot_cold, have[count - 2]), far
    while mask > 1:
        cots[mask] = hop(start, "tensor", mask)
        mask //= 2
    hot_sums = after(hot_sums, list(cots.values()))

    outs = run(
        make_mid(count // 2, groups),
        [shape((places, width)), shape((places, width), f32), shape((places, 1), f32)]
        + [shape((each, 2 * width))] * groups,
        hot_sums + [tok_hot, link, grad_out],
        "mid_hot",
    )
    mid_hot, normal_hot, factor_hot = outs[:3]
    pieces = outs[3:]

    ctx_cold, ask_cold, even_cold, odd_cold = run(
        make_cold(count, places, heads, size),
        [
            shape((count * cold, heads * LANES)),
            shape((count * cold, heads * LANES)),
        ]
        + [shape((half * cold, width))] * 2,
        [after(qkv, mid_hot), proj],
        "cold",
        extra=14,
        flops=4 * total * total * heads * LANES,
    )
    start, mask = {k: after(y, mid_hot) for k, y in cots.items()}, far // 2
    early = [k for k in cots if k and k % 2 == 0]
    while mask > 1:
        for k in list(cots):
            if k % 2 == 0 and k > mask and k ^ mask not in cots:
                start[k ^ mask] = cots[k ^ mask] = hop(start[k], "tensor", mask)
        mask //= 2
    landed = jnp.concatenate(
        [pieces[0]] + [hop(pieces[g], "dp", g) for g in range(1, groups)], axis=0
    )
    landed = after(landed, ctx_cold, list(cots.values()))
    arrived_all = gather_rel(landed, direct=True)
    for k in early:
        cots[k + 1] = hop(after(cots[k], arrived_all), "tensor", 1)
    cold_theirs = hop(after(odd_cold, arrived_all), "tensor", 1)
    arrived, slot_grads, hidden, grad_pre, even, odd = run(
        make_expert(count, experts),
        [
            shape((slots, width)),
            shape((slots, width)),
            shape((experts, slots, hidden_dev)),
            shape((experts, slots, hidden_dev)),
            shape((slots // 2, 2 * width)),
            shape((slots // 2, 2 * width)),
        ],
        arrived_all + [up_weight, down_weight],
        "experts",
        extra=8,
        flops=6 * slots * width * hidden_dev * experts,
    )
    cold_mine, cold_send = halve(even_cold, cold_theirs, "fold_cold_1")
    sums = fold_scatter(even, after(odd, list(cots.values()), cold_mine), places, "fold_slots")
    cold_theirs = hop(after(cold_send, sums[0]), "tensor", 2)
    for k in range(1, count, 2):
        if k not in cots:
            cots[k] = hop(after(cots[k - 1], arrived_all), "tensor", 1)
    cot_all = [cots[k] for k in range(count)]
    gq, gk, gv, gp = run(
        make_cold_back(count, places, heads, size, scale),
        [
            shape((count * cold, heads * LANES)),
            shape((heads * LANES, total), f32),
            shape((heads * LANES, total), f32),
            shape((heads * LANES, width), f32),
        ],
        cot_all + [after(qkv, sums[0]), proj, ctx_cold, ask_cold],
        "cold_back",
        extra=16,
        flops=1e10,
        loose=count,
        scratch=[
            pltpu.VMEM((count * cold, width), bf16),
            pltpu.SemaphoreType.DMA((count,)),
        ],
    )
    sums = after(sums, gp)

    pieces = run(
        make_split(count // 2, groups),
        [shape((each, 2 * width))] * groups,
        sums,
        "split_slots",
    )
    back = [pieces[0]] + [hop(pieces[g], "dp", g) for g in range(1, groups)]
    grad_hot, expert_out = run(
        make_mid_back(groups),
        [shape((places, width)), shape((places, width))],
        back + [link, cot_hot, normal_hot, factor_hot],
        "mid_back",
    )
    box.clear()

    def turn(_):
        box.append(
            run(
                make_turn(half),
                [shape((width, half * rows))],
                after(normed_all[half:], grad_hot),
                "turn",
        extra=3,
            )[0]
        )
        return box[0]

    grad_hot_all = gather_rel(grad_hot, turn, direct=True)
    fn_b = box[0]
    cold_mine = after(cold_mine, grad_hot)
    mask = 4
    while mask < count:
        cold_mine, cold_send = halve(cold_mine, cold_theirs, f"fold_cold_{mask // 2}")
        cold_theirs = hop(cold_send, "tensor", mask)
        mask *= 2
    cold_sums = [cold_mine, cold_theirs]

    me = lax.axis_index("dp").astype(jnp.int32).reshape(1)
    each_w = width // groups
    first_w = near_rows(each_w)
    halves = [(groups // 2 * n, heads * 4 * size) for n in (first_w, each_w - first_w)]
    keep_a, send_a, keep_b, send_b = run(
        make_hot_back(count, heads, size, groups, scale),
        [shape(halves[0]), shape(halves[0]), shape(halves[1]), shape(halves[1])],
        after(grad_hot_all, cold_mine)
        + [me, qkv, proj, ctx_hot, ask_hot, gq, gk, gv, gp, fn_a, fn_b],
        "hot_back",
        extra=10,
        moved=1024,
        smem=(count,),
        scratch=[
            pltpu.VMEM((heads * 3 * size, total), bf16),
            pltpu.VMEM((total, LANES), bf16),
            pltpu.VMEM((width, heads * 4 * size), bf16),
        ],
    )
    grad_up, grad_down = run(
        make_weight_grads(experts),
        [shape(up_weight.shape), shape(down_weight.shape)],
        [after(arrived, keep_a), slot_grads, hidden, grad_pre],
        "weight_grads",
        extra=10,
        moved=1024,
    )
    mask = 1
    while True:
        got_a = hop(send_a, "dp", mask)
        got_b = hop(send_b, "dp", groups // 2 // mask)
        if mask == 1:
            got_a, got_b = after((got_a, got_b), grad_up)
        if mask == groups // 2:
            break
        keep_a, send_a = halve(keep_a, got_a, f"fold_a_{mask}")
        keep_b, send_b = halve(keep_b, got_b, f"fold_b_{mask}")
        mask *= 2
    parts = [keep_a, got_a, keep_b, got_b]
    layer_out, gate_grad = run(
        make_epilogue(2),
        [shape((rows, width)), shape((2, rows), f32)],
        cold_sums
        + [tok_cold, mid_hot, perm, pick0, pick1, expert_out, gate_weights.T, cotangent],
        "epilogue",
        extra=4,
    )
    grad_qkv, grad_proj = run(
        make_last(heads, size),
        [shape((width // groups, heads, 3 * size), f32), shape((heads, size, width // groups), f32)],
        after(parts, layer_out, grad_up),
        "last",
        extra=6,
    )
    return (layer_out, gate_grad.T, grad_qkv, grad_proj, grad_up, grad_down)


def solution(mesh):
    return jax.shard_map(
        shards,
        mesh=mesh,
        in_specs=(
            P(("dp", "tensor"), None),
            P(("dp", "tensor"), None),
            P(("dp", "tensor"), None),
            P(("dp", "tensor"), None),
            P(("dp", "tensor"), None),
            P(None, "tensor", None),
            P("tensor", None, None),
            P("dp", None, "tensor"),
            P("dp", "tensor", None),
        ),
        out_specs=(
            P(("dp", "tensor"), None),
            P(("dp", "tensor"), None),
            P("dp", "tensor", None),
            P("tensor", None, "dp"),
            P("dp", None, "tensor"),
            P("dp", "tensor", None),
        ),
        check_vma=False,
    )
```
